256 devices in a mesh: gx: 32 (over x, z_lo, core), gy: 8 (over z_hi, y).
Axes of the slice: x: 4, y: 4, z: 8 (z_hi: 2, z_lo: 4; z = z_hi * 4 + z_lo), core: 2. Of those that a mesh axis runs over, the one named last changes fastest.
Arguments:
- positions: bfloat16 [3, 32768], P(None, ('gx', 'gy')), as said below
- species: int32 [32768], P(('gx', 'gy')), may hold values from 0 to 9
- neighbours: int32 [32768, 48], P(('gx', 'gy')), may hold values from 0 to 511
- counts: int32 [32768], P(('gx', 'gy')), may hold values from 1 to 48, as said below
- send_x: int32 [256, 2, 64], P(('gx', 'gy')), may hold values from 0 to 127
- send_y: int32 [256, 2, 128], P(('gx', 'gy')), may hold values from 0 to 255
- embed: bfloat16 [10, 128], replicated, may hold values from -6 to 6
- radial_w: float32 [2, 8, 128], replicated, may hold values from -2 to 2
- update_w: bfloat16 [2, 384, 128], replicated, may hold values from -0.3125 to 0.3125
- out_w: float32 [128], replicated, may hold values from -0.5 to 0.5
Outputs:
- atom_energy: float32 [32768], P(('gx', 'gy'))
- forces: float32 [3, 32768], P(None, ('gx', 'gy'))
The draws below stay inside these ranges and needn't reach their ends.
Inputs may be any that keep to these rules, and one draw needn't show every extreme that they name: `positions`: every coordinate is a multiple of 1/16 in [0, 8). `counts`: some atom has all 48 slots live.
All inputs are finite; a program needn't handle non-finite values.
Results may differ from the reference program's by a relative error of at most 0.012.
The reference program's roundings to bfloat16 on the way count: a program that leaves them out, or rounds other values in their place, can miss the bound.
Values may be sent and summed in bfloat16 or wider, within the bound.
A program may use at most 64 MiB of HBM per device.

```python
import math
import jax
import jax.numpy as jnp
from jax import lax

ATOMS_DEV = 128
K = 48
C = 128
NB = 8
SPECIES = 10
SX = 64
SY = 128
EXT = 512
DOMAINS = 256
NTOT = 32768
N_GX = 32
N_GY = 8


def draw_positions(key, part):
    key = jax.random.fold_in(key, 11)
    lattice = jax.random.randint(key, (3, NTOT), 0, 128)
    return (lattice.astype(jnp.float32) / 16.0).astype(jnp.bfloat16)


def draw_counts(key, part):
    key = jax.random.fold_in(key, 23)
    first, second = jax.random.split(key)
    domains = NTOT // ATOMS_DEV
    caps = jax.random.randint(first, (domains, 1), K // 4, K + 1)
    spread = jax.random.randint(second, (domains, ATOMS_DEV), 0, K)
    counts = caps - spread % (caps // 2 + 1)
    counts = counts.reshape(NTOT).at[0].set(K)
    return counts.astype(jnp.int32)


def set_ends(result, stream_key, smallest, high):
    place = [jax.random.randint(jax.random.fold_in(stream_key, axis), (), 0, length) for axis, length in enumerate(result.shape)]
    widest = result.shape.index(max(result.shape))
    next_to = place[:widest] + [(place[widest] + 1) % result.shape[widest]] + place[widest + 1:]
    return result.at[tuple(place)].set(smallest).at[tuple(next_to)].set(high)


def scatter_about(stream_key, extent, scale, reach, kind=jnp.bfloat16):
    values = jax.random.normal(stream_key, extent, jnp.float32) * scale
    return jnp.minimum(jnp.maximum(values, -reach), reach).astype(kind)


def setup_inputs(seed: int = 0) -> dict:
    seeds = jax.random.split(jax.random.key(seed), 11)
    return {
        "positions": draw_positions(jax.random.fold_in(seeds[10], 71), 0),
        "species": set_ends(jax.random.randint(seeds[1], (NTOT,), 0, SPECIES), jax.random.fold_in(seeds[1], 1), 0, SPECIES - 1).astype(jnp.int32),
        "neighbours": set_ends(jax.random.randint(seeds[2], (NTOT, K), 0, EXT), jax.random.fold_in(seeds[2], 1), 0, EXT - 1).astype(jnp.int32),
        "counts": draw_counts(jax.random.fold_in(seeds[10], 71), 0),
        "send_x": set_ends(jax.random.randint(seeds[4], (DOMAINS, 2, SX), 0, ATOMS_DEV), jax.random.fold_in(seeds[4], 1), 0, ATOMS_DEV - 1).astype(jnp.int32),
        "send_y": set_ends(jax.random.randint(seeds[5], (DOMAINS, 2, SY), 0, ATOMS_DEV + 2 * SX), jax.random.fold_in(seeds[5], 1), 0, (ATOMS_DEV + 2 * SX) - 1).astype(jnp.int32),
        "embed": scatter_about(seeds[6], (SPECIES, C), 1.0, 6.0),
        "radial_w": scatter_about(seeds[7], (2, NB, C), NB ** -0.5, 2.0, jnp.float32),
        "update_w": scatter_about(seeds[8], (2, 3 * C, C), (3 * C) ** -0.5, 0.3125),
        "out_w": scatter_about(seeds[9], (C,), C ** -0.5, 0.5, jnp.float32),
    }


BOX = 8.0
SCALE = 0.25
HIGH = lax.Precision.HIGHEST

def geometry(rel):
    dist = jnp.sqrt(lax.optimization_barrier(jnp.sum(rel * rel, axis=0)) + 1.0)
    unit_x = rel[0] / dist
    unit_y = rel[1] / dist
    unit_z = rel[2] / dist
    root3 = math.sqrt(3.0)
    root5 = math.sqrt(5.0)
    root15 = math.sqrt(15.0)
    harm = jnp.stack([jnp.ones_like(dist), root3 * unit_x, root3 * unit_y, root3 * unit_z, root15 * unit_x * unit_y, root15 * unit_y * unit_z, 0.5 * root5 * (3.0 * unit_z * unit_z - 1.0), root15 * unit_x * unit_z, 0.5 * root15 * (unit_x * unit_x - unit_y * unit_y)], 0)
    centers = 1.0 + 2.0 * jnp.arange(NB).astype(dist.dtype)[:, None]
    basis = jnp.exp(-0.125 * (dist[None, :] - centers) ** 2)
    return (harm, basis)

def invariants(amps):
    return jnp.concatenate([amps[:, 0:1], lax.optimization_barrier(jnp.sum(amps[:, 1:4] ** 2, axis=1, keepdims=True)), lax.optimization_barrier(jnp.sum(amps[:, 4:9] ** 2, axis=1, keepdims=True))], 1)

def invariant_grads(amps, grad_inv):
    return jnp.concatenate([grad_inv[:, 0:1], 2.0 * amps[:, 1:4] * grad_inv[:, 1:2], 2.0 * amps[:, 4:9] * grad_inv[:, 2:3]], 1)

def silu_slope(z):
    sig = jax.nn.sigmoid(z)
    return sig * (1.0 + z * (1.0 - sig))

def edge_sums(rel, nbr, live, h_ext, weights, rows):
    harm, basis = geometry(rel)
    radial = jnp.einsum('be,bc->ec', basis, weights, precision=HIGH)
    gathered = jnp.take(h_ext, nbr, axis=0).astype(jnp.float32)
    message = radial * gathered * live[:, None]
    width = message.shape[1]
    return SCALE * jnp.einsum('lnk,nkc->nlc', harm.reshape(9, rows, -1), message.reshape(rows, -1, width), precision=HIGH)

def edge_grads(rel, nbr, live, grad_amps, h_ext, weights, rows, features):
    (harm, basis), back = jax.vjp(geometry, rel)
    radial = jnp.einsum('be,bc->ec', basis, weights, precision=HIGH)
    gathered = jnp.take(h_ext, nbr, axis=0).astype(jnp.float32)
    message = radial * gathered * live[:, None]
    width = message.shape[1]
    harm3 = harm.reshape(9, rows, -1)
    grad_msg = SCALE * jnp.einsum('lnk,nlc->nkc', harm3, grad_amps, precision=HIGH).reshape(-1, width)
    grad_harm = SCALE * jnp.einsum('nlc,nkc->lnk', grad_amps, message.reshape(rows, -1, width), precision=HIGH).reshape(9, -1)
    grad_radial = grad_msg * gathered * live[:, None]
    grad_basis = jnp.einsum('ec,bc->be', grad_radial, weights, precision=HIGH)
    grad_rel = back((grad_harm, grad_basis))[0]
    rows_grad = grad_msg * radial * live[:, None] if features else None
    return (rows_grad, grad_rel)

def update(amps, h_own, weights):
    flat = invariants(amps).reshape(amps.shape[0], -1).astype(jnp.bfloat16)
    z = jnp.dot(flat, weights, preferred_element_type=jnp.float32)
    return (z, (h_own.astype(jnp.float32) + jax.nn.silu(z)).astype(jnp.bfloat16))

def back_update(z, grad_h, weights):
    grad_z = grad_h * silu_slope(z)
    grad_inv = jnp.dot(grad_z, weights.astype(jnp.float32).T, precision=HIGH)
    return grad_inv.reshape(z.shape[0], 3, -1)

def embed_rows(spc, embed):
    onehot = (spc[:, None] == jnp.arange(SPECIES).astype(jnp.bfloat16)[None, :]).astype(jnp.bfloat16)
    return jnp.dot(onehot, embed, preferred_element_type=jnp.float32).astype(jnp.bfloat16)

def take_rows(arr, idx):
    return jax.vmap(jax.vmap(lambda a, i: jnp.take(a, i, axis=0)))(arr, idx)

def add_rows(arr, idx, vals):
    return jax.vmap(jax.vmap(lambda a, i, v: a.at[i].add(v)))(arr, idx, vals)

def move_geo(piece, column, sign):
    return piece.at[..., column].add(jnp.asarray(sign * BOX, piece.dtype))

def keep_rows(piece, column, sign):
    return piece

def extend_rows(arr, send_x, send_y, moved):
    low = moved(jnp.roll(take_rows(arr, send_x[:, :, 0]), 1, axis=0), 0, -1.0)
    high = moved(jnp.roll(take_rows(arr, send_x[:, :, 1]), -1, axis=0), 0, 1.0)
    section = jnp.concatenate([arr, low, high], 2)
    low = moved(jnp.roll(take_rows(section, send_y[:, :, 0]), 1, axis=1), 1, -1.0)
    high = moved(jnp.roll(take_rows(section, send_y[:, :, 1]), -1, axis=1), 1, 1.0)
    return jnp.concatenate([section, low, high], 2)

def return_rows(arr, send_x, send_y):
    first = ATOMS_DEV + 2 * SX
    base = arr[:, :, :first]
    base = add_rows(base, send_y[:, :, 0], jnp.roll(arr[:, :, first:first + SY], -1, axis=1))
    base = add_rows(base, send_y[:, :, 1], jnp.roll(arr[:, :, first + SY:], 1, axis=1))
    own = base[:, :, :ATOMS_DEV]
    own = add_rows(own, send_x[:, :, 0], jnp.roll(base[:, :, ATOMS_DEV:ATOMS_DEV + SX], -1, axis=0))
    own = add_rows(own, send_x[:, :, 1], jnp.roll(base[:, :, ATOMS_DEV + SX:], 1, axis=0))
    return own

def scatter_grads(nbr, grad_rel):
    own_idx = jnp.arange(ATOMS_DEV * K) // K
    grad_pos = jnp.zeros((3, EXT), jnp.float32).at[:, nbr].add(grad_rel)
    return grad_pos.at[:, own_idx].add(-grad_rel)

def relative(geo_d, nbr_d):
    pos_ext = geo_d[:, :3].astype(jnp.float32).T
    return jnp.take(pos_ext, nbr_d, axis=1) - jnp.repeat(pos_ext[:, :ATOMS_DEV], K, axis=1)

def reference(positions, species, neighbours, counts, send_x, send_y, embed, radial_w, update_w, out_w):
    grid_x, grid_y = (N_GX, N_GY)
    domains = grid_x * grid_y
    pos = positions.reshape(3, grid_x, grid_y, ATOMS_DEV).transpose(1, 2, 3, 0)
    spc = species.reshape(grid_x, grid_y, ATOMS_DEV, 1).astype(jnp.bfloat16)
    geo = jnp.concatenate([pos, spc], -1)
    sends_x = send_x.reshape(grid_x, grid_y, 2, SX)
    sends_y = send_y.reshape(grid_x, grid_y, 2, SY)
    geo_ext = extend_rows(geo, sends_x, sends_y, move_geo).reshape(domains, EXT, 4)
    nbr = neighbours.reshape(domains, ATOMS_DEV * K)
    live = (jnp.arange(K)[None, None, :] < counts.reshape(domains, ATOMS_DEV, 1)).astype(jnp.float32)
    live = live.reshape(domains, ATOMS_DEV * K)

    def first_layer(inputs):
        geo_d, nbr_d, live_d = inputs
        h0_ext = embed_rows(geo_d[:, 3], embed)
        amps = edge_sums(relative(geo_d, nbr_d), nbr_d, live_d, h0_ext, radial_w[0], ATOMS_DEV)
        return update(amps, h0_ext[:ATOMS_DEV], update_w[0])[1]
    h1 = lax.map(first_layer, (geo_ext, nbr, live))
    h1_ext = extend_rows(h1.reshape(grid_x, grid_y, ATOMS_DEV, C), sends_x, sends_y, keep_rows)
    h1_ext = h1_ext.reshape(domains, EXT, C)

    def second_layer(inputs):
        geo_d, nbr_d, live_d, h_ext = inputs
        rel = relative(geo_d, nbr_d)
        amps = edge_sums(rel, nbr_d, live_d, h_ext, radial_w[1], ATOMS_DEV)
        z, h2 = update(amps, h_ext[:ATOMS_DEV], update_w[1])
        energy = jnp.dot(h2.astype(jnp.float32), out_w, precision=HIGH)
        grad_h = jnp.broadcast_to(out_w, (ATOMS_DEV, C))
        grad_amps = invariant_grads(amps, back_update(z, grad_h, update_w[1]))
        rows_grad, grad_rel = edge_grads(rel, nbr_d, live_d, grad_amps, h_ext, radial_w[1], ATOMS_DEV, True)
        grad_feat = jnp.zeros((EXT, C), jnp.float32).at[nbr_d].add(rows_grad)
        grad_feat = grad_feat.at[:ATOMS_DEV].add(grad_h)
        return (energy, grad_feat, scatter_grads(nbr_d, grad_rel))
    energy, grad_feat, grad_two = lax.map(second_layer, (geo_ext, nbr, live, h1_ext))
    grad_h1 = return_rows(grad_feat.reshape(grid_x, grid_y, EXT, C), sends_x, sends_y)
    grad_h1 = grad_h1.reshape(domains, ATOMS_DEV, C)

    def first_back(inputs):
        geo_d, nbr_d, live_d, grad_h = inputs
        rel = relative(geo_d, nbr_d)
        h0_ext = embed_rows(geo_d[:, 3], embed)
        amps = edge_sums(rel, nbr_d, live_d, h0_ext, radial_w[0], ATOMS_DEV)
        z = update(amps, h0_ext[:ATOMS_DEV], update_w[0])[0]
        grad_amps = invariant_grads(amps, back_update(z, grad_h, update_w[0]))
        grad_rel = edge_grads(rel, nbr_d, live_d, grad_amps, h0_ext, radial_w[0], ATOMS_DEV, False)[1]
        return scatter_grads(nbr_d, grad_rel)
    grad_one = lax.map(first_back, (geo_ext, nbr, live, grad_h1))
    grad_pos = (grad_one + grad_two).transpose(0, 2, 1).reshape(grid_x, grid_y, EXT, 3)
    own = return_rows(grad_pos, sends_x, sends_y)
    forces = -own.transpose(3, 0, 1, 2).reshape(3, NTOT)
    return (energy.reshape(NTOT), forces)
```

```python
import functools
import math

import jax
import jax.numpy as jnp
from jax import lax
from jax.experimental import pallas as pl
from jax.experimental.pallas import tpu as pltpu
from jax.sharding import PartitionSpec as P

F32 = jnp.float32
BF16 = jnp.bfloat16
I32 = jnp.int32
MESH = pl.DeviceIdType.MESH

ATOMS = 128
SLOTS = 48
GROUP = 8
CHUNKS = ATOMS // GROUP
EDGES = GROUP * SLOTS
WIDTH = 128
EXT = 512
NB = 8
BOX = 8.0
SCALE = 0.25
SIDES = ((1, 0), (-1, 0), (0, 1), (0, -1), (1, 1), (1, -1), (-1, 1), (-1, -1))
R3, R5, R15 = math.sqrt(3.0), math.sqrt(5.0), math.sqrt(15.0)


def mm(a, b):
    return lax.dot_general(a, b, (((1,), (0,)), ((), ())), preferred_element_type=F32)


def nt(a, b):
    return lax.dot_general(a, b, (((1,), (1,)), ((), ())), preferred_element_type=F32)


def iota(shape, axis):
    return lax.broadcasted_iota(I32, shape, axis)


def split(value):
    high = value.astype(BF16).astype(F32)
    return high, value - high


def onehot(index, total):
    shape = (total, index.shape[1])
    return jnp.where(iota(shape, 0) == index, 1.0, 0.0).astype(BF16)


def lanes_take(row, index):
    return jnp.take_along_axis(jnp.broadcast_to(row, index.shape), index, axis=1)


def kernel(
    remote,
    pos_ref, spc_ref, nbr_ref, cnt_ref, sx_ref, sy_ref, emb_ref, rw_ref, uw_ref, ow_ref,
    en_ref, fo_ref,
    geo_out, geo_x, geo_in, geo_xin,
    h_sec, h_own, h_piece,
    g_sec, g_own, g_piece,
    p_out, p_piece, p_own, p_pin,
    nbr_d, spc_d, vec_d, harm_t, hot, hmat, hlow, basis, rad1, rad2, gat1, gat2, gms,
    amps1, amps2, gamps, z1_ref, gext, gharm, ohx, ohxt, ohy, ohyt, grel,
    send_sem, recv_sem,
):
    if remote:
        nx, ny = lax.axis_size("gx"), lax.axis_size("gy")
        me_x, me_y = lax.axis_index("gx"), lax.axis_index("gy")

        def place(side):
            return (lax.rem(me_x + side[0] + nx, nx), lax.rem(me_y + side[1] + ny, ny))

        barrier = pltpu.get_barrier_semaphore()
        for side in SIDES:
            pl.semaphore_signal(barrier, inc=1, device_id=place(side), device_id_type=MESH)

    def exchange(phase, parts):
        copies = []
        for number, side in enumerate(SIDES):
            src, dst = parts(side)
            if remote:
                copy = pltpu.make_async_remote_copy(
                    src_ref=src, dst_ref=dst,
                    send_sem=send_sem.at[phase, number], recv_sem=recv_sem.at[phase, number],
                    device_id=place(side), device_id_type=MESH,
                )
            else:
                copy = pltpu.make_async_copy(src, dst, recv_sem.at[phase, number])
            copy.start()
            copies.append(copy)
        return copies

    def finish(copies):
        for copy in copies:
            copy.wait()

    sx = jnp.concatenate([sx_ref[0:1, :], sx_ref[1:2, :]], axis=1)
    sel = jnp.where(iota((ATOMS, 128), 0) == sx, 1.0, 0.0)
    ohx[...] = sel.astype(BF16)
    ohxt[...] = sel.T.astype(BF16)

    spc = spc_ref[...].astype(F32)
    pos = pos_ref[...].astype(F32)
    zero = jnp.zeros((1, 128), F32)
    geo = jnp.concatenate([pos, spc, zero, zero, zero, zero], axis=0)
    sy = sy_ref[...].astype(F32)
    geo_out[0] = jnp.concatenate([pos, spc, sy[1:2], zero, zero, zero], axis=0)
    geo_out[1] = jnp.concatenate([pos, spc, sy[0:1], zero, zero, zero], axis=0)
    geo_x[...] = mm(geo.astype(BF16), ohx[...])

    if remote:
        pl.semaphore_wait(barrier, len(SIDES))

    def geo_parts(side):
        dx, dy = side
        if dx == 0:
            return geo_out.at[(1 + dy) // 2], geo_in.at[1 - dy]
        return geo_x, geo_xin.at[1 - dy, (1 - dx) // 2]

    copies = exchange(0, geo_parts)

    nbr_d[...] = jnp.concatenate(
        [nbr_ref[pl.ds(a, CHUNKS, stride=GROUP), :] for a in range(GROUP)], axis=1
    )

    def build(g, carry):
        hot[g] = onehot(nbr_d[pl.ds(g, 1), :], EXT)
        return carry

    lax.fori_loop(0, CHUNKS, build, 0)

    lane = iota((CHUNKS, EDGES), 1)
    of_lane = jnp.zeros((CHUNKS, EDGES), I32)
    for a in range(1, GROUP):
        of_lane += (lane >= a * SLOTS).astype(I32)
    slot = lane - of_lane * SLOTS
    atom = iota((CHUNKS, EDGES), 0) * GROUP + of_lane
    mask = of_lane[:GROUP] == iota((GROUP, EDGES), 0)

    embed_t = emb_ref[...].astype(F32).T.astype(BF16)
    w_t = []
    for t in range(2):
        high, low = split(rw_ref[t])
        w_t.append(
            jnp.concatenate([high, high, low, jnp.zeros_like(high)], axis=0).T.astype(BF16)
        )
    w_rows = []
    for t in range(2):
        w_rows.append(jnp.concatenate(split(rw_ref[t]), axis=0).astype(BF16))

    finish(copies)

    def section(j):
        own = geo if j == 0 else geo_in[1 + j]
        keep = iota((8, 128), 1) < 64
        row = iota((8, 128), 0)
        got = jnp.where(keep, geo_xin[1 + j, 0], geo_xin[1 + j, 1])
        got += jnp.where(row == 0, jnp.where(keep, -BOX, BOX), 0.0)
        return own, got

    row = iota((8, 128), 0)
    blocks = list(section(0))
    for number, j in enumerate((-1, 1)):
        own, got = section(j)
        index = own[4:5].astype(I32)
        chosen = jnp.where(iota((256, 128), 0) == index, 1.0, 0.0)
        ohy[number] = chosen.astype(BF16)
        ohyt[number] = chosen.T.astype(BF16)
        whole = jnp.concatenate([own, got], axis=1)
        whole = jnp.where(iota((8, 256), 0) < 4, whole, 0.0)
        picked = mm(whole.astype(BF16), ohy[number])
        blocks.append(picked + jnp.where(row == 1, BOX * j, 0.0))

    packed = []
    for block in blocks:
        x = ((block[0:1] + BOX) * 16.0).astype(I32)
        y = ((block[1:2] + BOX) * 16.0).astype(I32)
        zc = (block[2:3] * 16.0).astype(I32)
        packed.append(x + y * 512 + zc * 262144 + block[3:4].astype(I32) * 33554432)

    nbr = nbr_d[...]
    near = nbr & 127
    which = nbr >> 7
    far, mine, live = [], [], []
    for t in range(EDGES // 128):
        cut = slice(t * 128, (t + 1) * 128)
        value = lanes_take(packed[0], near[:, cut])
        for b in range(1, 4):
            value = jnp.where(which[:, cut] == b, lanes_take(packed[b], near[:, cut]), value)
        far.append(value)
        mine.append(lanes_take(packed[0], atom[:, cut]))
        live.append(lanes_take(cnt_ref[...], atom[:, cut]))
    far = jnp.concatenate(far, axis=1)
    mine = jnp.concatenate(mine, axis=1)
    live = jnp.where(slot < jnp.concatenate(live, axis=1), 1.0, 0.0)

    def coordinates(value):
        return value & 511, (value >> 9) & 511, (value >> 18) & 127

    rel = [
        (p - q).astype(F32) * (1.0 / 16.0)
        for p, q in zip(coordinates(far), coordinates(mine))
    ]
    square = rel[0] * rel[0] + rel[1] * rel[1] + rel[2] * rel[2] + 1.0
    dist = jnp.sqrt(square)
    inverse = 1.0 / dist
    ux, uy, uz = (r * inverse for r in rel)
    spc_d[...] = far >> 25
    for number, value in enumerate((dist, live, inverse, ux, uy, uz)):
        vec_d[number] = value
    harm = (
        R3 * ux, R3 * uy, R3 * uz, R15 * ux * uy, R15 * uy * uz,
        0.5 * R5 * (3.0 * uz * uz - 1.0), R15 * ux * uz, 0.5 * R15 * (ux * ux - uy * uy),
    )
    for number, value in enumerate(harm):
        harm_t[number] = SCALE * value

    def radial_basis(g):
        centers = 1.0 + 2.0 * iota((NB, EDGES), 0).astype(F32)
        away = vec_d[0, pl.ds(g, 1), :] - centers
        return away, jnp.exp(-0.125 * away * away) * vec_d[1, pl.ds(g, 1), :]

    def sums_of(g, message):
        high, low = split(message)
        high = high.astype(BF16)
        return nt(hmat[g], high) + nt(hlow[g], high) + nt(hmat[g], low.astype(BF16))

    def first(g, carry):
        unit = jnp.where(mask, SCALE, 0.0)
        rows = [unit]
        for m in range(8):
            rows.append(jnp.where(mask, harm_t[m, pl.ds(g, 1), :], 0.0))
        rows.append(jnp.zeros((GROUP, EDGES), F32))
        rows, fine = split(jnp.concatenate(rows, axis=0))
        hmat[g] = rows.astype(BF16)
        hlow[g] = fine.astype(BF16)
        high, low = split(radial_basis(g)[1])
        basis[g] = jnp.concatenate([high, low, high, jnp.zeros_like(high)], axis=0).astype(BF16)
        kinds = onehot(spc_d[pl.ds(g, 1), :], 16)
        gathered = mm(embed_t, kinds)
        radial = mm(w_t[0], basis[g])
        gat1[g] = gathered.astype(BF16)
        rad1[g] = radial.astype(BF16)
        sums = sums_of(g, gathered * radial)
        for m in range(9):
            amps1[m, pl.ds(pl.multiple_of(g * GROUP, GROUP), GROUP), :] = sums[
                m * GROUP : (m + 1) * GROUP
            ]
        return carry

    lax.fori_loop(0, CHUNKS, first, 0)

    def update(amps, old, t):
        one = amps[1] * amps[1] + amps[2] * amps[2] + amps[3] * amps[3]
        two = amps[4] * amps[4] + amps[5] * amps[5] + amps[6] * amps[6]
        two += amps[7] * amps[7] + amps[8] * amps[8]
        flat = jnp.concatenate([amps[0], one, two], axis=1).astype(BF16)
        z = mm(flat, uw_ref[t])
        return z, (old + z * jax.nn.sigmoid(z)).astype(BF16)

    def back(amps, z, grad, t):
        sig = jax.nn.sigmoid(z)
        grad_z = grad * (sig * (1.0 + z * (1.0 - sig)))
        grad_inv = nt(grad_z.astype(BF16), uw_ref[t])
        gamps[0] = grad_inv[:, :128]
        for m in range(1, 9):
            part = grad_inv[:, 128:256] if m < 4 else grad_inv[:, 256:]
            gamps[m] = 2.0 * amps[m] * part

    kinds_own = onehot(spc_ref[...], 16).astype(F32).T.astype(BF16)
    h0_own = mm(kinds_own, emb_ref[...])
    z1, h1 = update(amps1, h0_own, 0)
    z1_ref[...] = z1
    h_sec[1, 0:128] = h1
    h_own[...] = h1
    h_piece[...] = mm(ohxt[...], h1).astype(BF16)

    def h_parts(side):
        dx, dy = side
        if dx == 0:
            return h_own, h_sec.at[1 - dy, pl.ds(0, 128)]
        if dx == 1:
            return h_piece.at[pl.ds(0, 64)], h_sec.at[1 - dy, pl.ds(128, 64)]
        return h_piece.at[pl.ds(64, 64)], h_sec.at[1 - dy, pl.ds(192, 64)]

    copies = exchange(1, h_parts)

    def second_radial(g, carry):
        rad2[g] = mm(w_t[1], basis[g])
        return carry

    lax.fori_loop(0, CHUNKS, second_radial, 0)
    own_t = h1.astype(F32).T
    finish(copies)

    got_t = h_sec[1, 128:256].astype(F32).T
    low_t = mm(ohyt[0], h_sec[0]).T
    high_t = mm(ohyt[1], h_sec[2]).T
    h_t = jnp.concatenate([own_t, got_t, low_t, high_t], axis=1).astype(BF16)

    def second(g, carry):
        gathered = mm(h_t, hot[g])
        gat2[g] = gathered.astype(BF16)
        sums = sums_of(g, gathered * rad2[g])
        for m in range(9):
            amps2[m, pl.ds(pl.multiple_of(g * GROUP, GROUP), GROUP), :] = sums[
                m * GROUP : (m + 1) * GROUP
            ]
        return carry

    lax.fori_loop(0, CHUNKS, second, 0)
    z2, h2 = update(amps2, h1.astype(F32), 1)
    out_w = ow_ref[...]
    high, rest = split(out_w)
    mid, low = split(rest)
    readout = jnp.concatenate([high, mid, low, jnp.zeros((5, 128), F32)], axis=0).astype(BF16)
    parts = nt(readout, h2)
    en_ref[...] = parts[0:1] + parts[1:2] + parts[2:3]
    back(amps2, z2, out_w, 1)

    gext[...] = jnp.zeros_like(gext)

    def chunk_rows(g):
        at = pl.ds(pl.multiple_of(g * GROUP, GROUP), GROUP)
        rows = [gamps[m, at, :] for m in range(9)] + [jnp.zeros((GROUP, 128), F32)]
        return jnp.concatenate(rows, axis=0)

    def features(g, carry):
        grad = mm(chunk_rows(g).T.astype(BF16), hmat[g])
        gms[g] = grad.astype(BF16)
        rows = (grad * rad2[g]).astype(BF16)
        gext[...] += nt(hot[g], rows)
        return carry

    lax.fori_loop(0, CHUNKS, features, 0)

    for number, start in ((0, 256), (1, 384)):
        g_sec[2 * number] = mm(ohy[number], gext[start : start + 128].astype(BF16)).astype(BF16)
    g_sec[1, 128:256] = gext[128:256].astype(BF16)

    def g_parts(side):
        dx, dy = side
        if dx == 0:
            return g_sec.at[1 + dy, pl.ds(0, 128)], g_own.at[(1 - dy) // 2]
        if dx == -1:
            return g_sec.at[1 + dy, pl.ds(128, 64)], g_piece.at[1 - dy, pl.ds(0, 64)]
        return g_sec.at[1 + dy, pl.ds(192, 64)], g_piece.at[1 - dy, pl.ds(64, 64)]

    copies = exchange(2, g_parts)

    def adjoint(g, grad, gathered, radial, t):
        message = (gathered * radial).astype(BF16)
        wide = mm(chunk_rows(g).astype(BF16), message)
        rows = []
        for m in range(1, 9):
            part = jnp.where(mask, wide[m * GROUP : (m + 1) * GROUP], 0.0)
            rows.append(jnp.sum(part, axis=0, keepdims=True))
        two = mm(w_rows[t], (grad * gathered).astype(BF16))
        away, value = radial_basis(g)
        slope = (two[0:NB] + two[NB:]) * (-0.25 * away * value)
        rows.append(jnp.sum(slope, axis=0, keepdims=True))
        return rows

    def geometry_two(g, carry):
        rows = adjoint(
            g, gms[g].astype(F32), gat2[g].astype(F32), rad2[g], 1
        )
        for number, value in enumerate(rows):
            gharm[number, pl.ds(g, 1), :] = value
        return carry

    lax.fori_loop(0, CHUNKS, geometry_two, 0)
    finish(copies)

    grad_h1 = gext[0:128] + out_w + g_own[0].astype(F32) + g_own[1].astype(F32)
    piece = g_piece[0].astype(F32) + g_piece[1].astype(F32) + g_piece[2].astype(F32)
    grad_h1 += mm(ohx[...], piece.astype(BF16))
    back(amps1, z1_ref[...], grad_h1, 0)

    def geometry_one(g, carry):
        grad = mm(chunk_rows(g).T.astype(BF16), hmat[g])
        rows = adjoint(g, grad, gat1[g].astype(F32), rad1[g].astype(F32), 0)
        for number, value in enumerate(rows):
            gharm[number, pl.ds(g, 1), :] += value
        return carry

    lax.fori_loop(0, CHUNKS, geometry_one, 0)

    inv, vx, vy, vz = (vec_d[n] for n in range(2, 6))
    g1, g2, g3, g4, g5, g6, g7, g8 = (SCALE * gharm[n] for n in range(8))
    gx = R3 * g1 + R15 * (vy * g4 + vz * g7 + vx * g8)
    gy = R3 * g2 + R15 * (vx * g4 + vz * g5 - vy * g8)
    gz = R3 * g3 + R15 * (vy * g5 + vx * g7) + 3.0 * R5 * vz * g6
    along = gharm[8] - inv * (gx * vx + gy * vy + gz * vz)
    wide_rows = []
    for number, (grad, unit) in enumerate(((gx, vx), (gy, vy), (gz, vz))):
        high, low = split(grad * inv + unit * along)
        grel[number] = high
        grel[3 + number] = low
        wide_rows += [high, low]
    grel[6] = jnp.zeros((CHUNKS, EDGES), F32)
    grel[7] = jnp.zeros((CHUNKS, EDGES), F32)

    lane_atom = jnp.where(iota((ATOMS, EDGES), 0) % GROUP == of_lane[0:1], 1.0, 0.0).astype(BF16)
    sums = nt(jnp.concatenate(wide_rows, axis=0).astype(BF16), lane_atom)
    here = iota((CHUNKS, 128), 1) // GROUP == iota((CHUNKS, 128), 0)
    own_rows = []
    for number in range(3):
        both = sums[32 * number : 32 * number + 16] + sums[32 * number + 16 : 32 * number + 32]
        own_rows.append(jnp.sum(jnp.where(here, both, 0.0), axis=0, keepdims=True))

    def scatter(g, total):
        rows = jnp.concatenate([grel[n, pl.ds(g, 1), :] for n in range(8)], axis=0)
        return total + nt(rows.astype(BF16), hot[g])

    total = lax.fori_loop(0, CHUNKS, scatter, jnp.zeros((8, EXT), F32))
    total = total[0:3] + total[3:6]
    own_rows = jnp.concatenate(own_rows, axis=0)

    def six(value):
        high, low = split(value)
        return jnp.concatenate([high, low, jnp.zeros((2, value.shape[1]), F32)], axis=0).astype(BF16)

    def three(value):
        return value[0:3] + value[3:6]

    pad = jnp.zeros((5, 128), F32)
    for number, start in ((0, 256), (1, 384)):
        spread = three(nt(six(total[:, start : start + 128]), ohy[number]))
        p_out[number] = jnp.concatenate([spread[:, 0:128], pad], axis=0)
        p_piece[2 * number] = jnp.concatenate([spread[:, 128:256], pad], axis=0)
    p_piece[1] = jnp.concatenate([total[:, 128:256], pad], axis=0)

    def p_parts(side):
        dx, dy = side
        if dx == 0:
            return p_out.at[(1 + dy) // 2], p_own.at[(1 - dy) // 2]
        return p_piece.at[1 + dy], p_pin.at[1 - dy, (1 + dx) // 2]

    finish(exchange(3, p_parts))
    up = p_pin[0, 0] + p_pin[1, 0] + p_pin[2, 0]
    down = p_pin[0, 1] + p_pin[1, 1] + p_pin[2, 1]
    piece = jnp.where(iota((8, 128), 1) < 64, up, down)[0:3]
    result = total[:, 0:128] - own_rows + p_own[0][0:3] + p_own[1][0:3]
    result += three(nt(six(piece), ohx[...]))
    fo_ref[...] = -result


def body(remote, positions, species, neighbours, counts, send_x, send_y, embed, radial_w, update_w, out_w):
    embed = jnp.pad(embed, ((0, 16 - embed.shape[0]), (0, 0)))
    vmem = pl.BlockSpec(memory_space=pltpu.VMEM)
    chunked = (CHUNKS, 128, EDGES)
    scratch = [
        pltpu.VMEM((2, 8, 128), F32),
        pltpu.VMEM((8, 128), F32),
        pltpu.VMEM((3, 8, 128), F32),
        pltpu.VMEM((3, 2, 8, 128), F32),
        pltpu.VMEM((3, 256, 128), BF16),
        pltpu.VMEM((128, 128), BF16),
        pltpu.VMEM((128, 128), BF16),
        pltpu.VMEM((3, 256, 128), BF16),
        pltpu.VMEM((2, 128, 128), BF16),
        pltpu.VMEM((3, 128, 128), BF16),
        pltpu.VMEM((2, 8, 128), F32),
        pltpu.VMEM((3, 8, 128), F32),
        pltpu.VMEM((2, 8, 128), F32),
        pltpu.VMEM((3, 2, 8, 128), F32),
        pltpu.VMEM((CHUNKS, EDGES), I32),
        pltpu.VMEM((CHUNKS, EDGES), I32),
        pltpu.VMEM((6, CHUNKS, EDGES), F32),
        pltpu.VMEM((8, CHUNKS, EDGES), F32),
        pltpu.VMEM((CHUNKS, EXT, EDGES), BF16),
        pltpu.VMEM((CHUNKS, 80, EDGES), BF16),
        pltpu.VMEM((CHUNKS, 80, EDGES), BF16),
        pltpu.VMEM((CHUNKS, 32, EDGES), BF16),
        pltpu.VMEM(chunked, BF16),
        pltpu.VMEM(chunked, F32),
        pltpu.VMEM(chunked, BF16),
        pltpu.VMEM(chunked, BF16),
        pltpu.VMEM(chunked, BF16),
        pltpu.VMEM((9, 128, 128), F32),
        pltpu.VMEM((9, 128, 128), F32),
        pltpu.VMEM((9, 128, 128), F32),
        pltpu.VMEM((128, 128), F32),
        pltpu.VMEM((EXT, 128), F32),
        pltpu.VMEM((9, CHUNKS, EDGES), F32),
        pltpu.VMEM((128, 128), BF16),
        pltpu.VMEM((128, 128), BF16),
        pltpu.VMEM((2, 256, 128), BF16),
        pltpu.VMEM((2, 128, 256), BF16),
        pltpu.VMEM((8, CHUNKS, EDGES), F32),
        pltpu.SemaphoreType.DMA((4, 8)),
        pltpu.SemaphoreType.DMA((4, 8)),
    ]
    energy, forces = pl.pallas_call(
        functools.partial(kernel, remote),
        out_shape=(
            jax.ShapeDtypeStruct((1, ATOMS), F32),
            jax.ShapeDtypeStruct((3, ATOMS), F32),
        ),
        in_specs=[vmem] * 10,
        out_specs=(vmem, vmem),
        scratch_shapes=scratch,
        compiler_params=pltpu.CompilerParams(
            collective_id=0 if remote else None,
            has_side_effects=remote,
            vmem_limit_bytes=48 * 1024 * 1024,
        ),
    )(
        positions,
        species.reshape(1, ATOMS),
        neighbours,
        counts.reshape(1, ATOMS),
        send_x.reshape(2, 64),
        send_y.reshape(2, 128),
        embed,
        radial_w,
        update_w,
        out_w.reshape(1, WIDTH),
    )
    return energy.reshape(ATOMS), forces


def solution(mesh):
    return jax.shard_map(
        functools.partial(body, True),
        mesh=mesh,
        in_specs=(
            P(None, ("gx", "gy")),
            P(("gx", "gy")),
            P(("gx", "gy"), None),
            P(("gx", "gy")),
            P(("gx", "gy"), None, None),
            P(("gx", "gy"), None, None),
            P(),
            P(),
            P(),
            P(),
        ),
        out_specs=(P(("gx", "gy")), P(None, ("gx", "gy"))),
        check_vma=False,
    )
```

```python
import functools
import math

import jax
import jax.numpy as jnp
from jax import lax
from jax.experimental import pallas as pl
from jax.experimental.pallas import tpu as pltpu
from jax.sharding import PartitionSpec as P

F32 = jnp.float32
BF16 = jnp.bfloat16
I32 = jnp.int32
MESH = pl.DeviceIdType.MESH

ATOMS = 128
SLOTS = 48
GROUP = 8
CHUNKS = ATOMS // GROUP
PAIRS = CHUNKS // 2
EDGES = GROUP * SLOTS
WIDTH = 128
EXT = 512
NB = 8
BOX = 8.0
SCALE = 0.25
SIDES = ((1, 0), (-1, 0), (0, 1), (0, -1), (1, 1), (1, -1), (-1, 1), (-1, -1))
R3, R5, R15 = math.sqrt(3.0), math.sqrt(5.0), math.sqrt(15.0)


def mm(a, b):
    return lax.dot_general(a, b, (((1,), (0,)), ((), ())), preferred_element_type=F32)


def nt(a, b):
    return lax.dot_general(a, b, (((1,), (1,)), ((), ())), preferred_element_type=F32)


def iota(shape, axis):
    return lax.broadcasted_iota(I32, shape, axis)


def split(value):
    high = value.astype(BF16).astype(F32)
    return high, value - high


def onehot(index, total):
    shape = (total, index.shape[1])
    return jnp.where(iota(shape, 0) == index, 1.0, 0.0).astype(BF16)


def lanes_take(row, index):
    return jnp.take_along_axis(jnp.broadcast_to(row, index.shape), index, axis=1)


def kernel(
    remote,
    pos_ref, spc_ref, nbr_ref, cnt_ref, sx_ref, sy_ref, emb_ref, rw_ref, uw_hbm, ow_ref,
    en_ref, fo_ref,
    geo_out, geo_x, geo_in, geo_xin,
    h_sec, h_own, h_piece,
    g_sec, g_own, g_piece,
    p_out, p_piece, p_own, p_pin,
    nbr_t, nbr_d, spc_d, vec_d, harm_t, hot, hmat, hlow, basis, phi, rad2, gat2, gms, rows_t,
    kinds_amps, amps1, amps2, gamps, z1_ref, gext, gharm, ohx, ohxt, ohy, ohyt,
    uw_ref, uw_sem, send_sem, recv_sem,
):
    if remote:
        nx, ny = lax.axis_size("gx"), lax.axis_size("gy")
        me_x, me_y = lax.axis_index("gx"), lax.axis_index("gy")

        def place(side):
            return (lax.rem(me_x + side[0] + nx, nx), lax.rem(me_y + side[1] + ny, ny))

        barrier = pltpu.get_barrier_semaphore()
        for side in SIDES:
            pl.semaphore_signal(barrier, inc=1, device_id=place(side), device_id_type=MESH)

    def exchange(phase, parts):
        copies = []
        for number, side in enumerate(SIDES):
            src, dst = parts(side)
            if remote:
                copy = pltpu.make_async_remote_copy(
                    src_ref=src, dst_ref=dst,
                    send_sem=send_sem.at[phase, number], recv_sem=recv_sem.at[phase, number],
                    device_id=place(side), device_id_type=MESH,
                )
            else:
                copy = pltpu.make_async_copy(src, dst, recv_sem.at[phase, number])
            copy.start()
            copies.append(copy)
        return copies

    def finish(copies):
        for copy in copies:
            copy.wait()

    weights = pltpu.make_async_copy(uw_hbm, uw_ref, uw_sem)
    weights.start()

    sx = jnp.concatenate([sx_ref[0:1, :], sx_ref[1:2, :]], axis=1)
    sel = jnp.where(iota((ATOMS, 128), 0) == sx, 1.0, 0.0)
    ohx[...] = sel.astype(BF16)
    ohxt[...] = sel.T.astype(BF16)

    spc = spc_ref[...].astype(F32)
    pos = pos_ref[...].astype(F32)
    zero = jnp.zeros((1, 128), F32)
    geo = jnp.concatenate([pos, spc, zero, zero, zero, zero], axis=0)
    sy = sy_ref[...].astype(F32)
    geo_out[0] = jnp.concatenate([pos, spc, sy[1:2], zero, zero, zero], axis=0)
    geo_out[1] = jnp.concatenate([pos, spc, sy[0:1], zero, zero, zero], axis=0)
    geo_x[...] = mm(geo.astype(BF16), ohx[...])

    if remote:
        pl.semaphore_wait(barrier, len(SIDES))

    def geo_parts(side):
        dx, dy = side
        if dx == 0:
            return geo_out.at[(1 + dy) // 2], geo_in.at[1 - dy]
        return geo_x, geo_xin.at[1 - dy, (1 - dx) // 2]

    copies = exchange(0, geo_parts)

    nbr_t[...] = nbr_ref[...].T
    nbr_d[...] = jnp.concatenate(
        [nbr_t[pl.ds(a, CHUNKS, stride=GROUP), :] for a in range(GROUP)], axis=1
    )

    def lanes(g, count=1):
        return pl.ds(pl.multiple_of(g * (count * EDGES), 128), count * EDGES)

    def build(g, carry):
        index = jnp.broadcast_to(nbr_d[pl.ds(g, 1), :], (16, EDGES)).astype(jnp.int16)
        one, none = jnp.ones((16, EDGES), BF16), jnp.zeros((16, EDGES), BF16)
        first_rows = iota((16, EDGES), 0).astype(jnp.int16)
        for block in range(EXT // 16):
            hot[16 * block : 16 * block + 16, lanes(g)] = jnp.where(
                index - jnp.int16(16 * block) == first_rows, one, none
            )
        return carry

    lax.fori_loop(0, CHUNKS, build, 0, unroll=8)

    lane = iota((CHUNKS, EDGES), 1)
    of_lane = jnp.zeros((CHUNKS, EDGES), I32)
    for a in range(1, GROUP):
        of_lane += (lane >= a * SLOTS).astype(I32)
    slot = lane - of_lane * SLOTS
    atom = iota((CHUNKS, EDGES), 0) * GROUP + of_lane
    mask = of_lane[:GROUP] == iota((GROUP, EDGES), 0)

    high, low = split(rw_ref[1])
    w_t = jnp.concatenate([high, high, low, jnp.zeros_like(high)], axis=0).T.astype(BF16)
    w_rows = jnp.concatenate([high, low], axis=0).astype(BF16)
    embed = emb_ref[...].astype(F32)
    species = embed.shape[0]
    kind_w = jnp.concatenate([rw_ref[0] * embed[k : k + 1] for k in range(species)], axis=0)
    kind_high, kind_low = (v.astype(BF16) for v in split(kind_w))

    finish(copies)

    def section(j):
        own = geo if j == 0 else geo_in[1 + j]
        keep = iota((8, 128), 1) < 64
        row = iota((8, 128), 0)
        got = jnp.where(keep, geo_xin[1 + j, 0], geo_xin[1 + j, 1])
        got += jnp.where(row == 0, jnp.where(keep, -BOX, BOX), 0.0)
        return own, got

    row = iota((8, 128), 0)
    blocks = list(section(0))
    for number, j in enumerate((-1, 1)):
        own, got = section(j)
        index = own[4:5].astype(I32)
        chosen = jnp.where(iota((256, 128), 0) == index, 1.0, 0.0)
        ohy[number] = chosen.astype(BF16)
        ohyt[number] = chosen.T.astype(BF16)
        whole = jnp.concatenate([own, got], axis=1)
        whole = jnp.where(iota((8, 256), 0) < 4, whole, 0.0)
        picked = mm(whole.astype(BF16), ohy[number])
        blocks.append(picked + jnp.where(row == 1, BOX * j, 0.0))

    packed = []
    for block in blocks:
        x = ((block[0:1] + BOX) * 16.0).astype(I32)
        y = ((block[1:2] + BOX) * 16.0).astype(I32)
        zc = (block[2:3] * 16.0).astype(I32)
        packed.append(x + y * 512 + zc * 262144 + block[3:4].astype(I32) * 33554432)

    nbr = nbr_d[...]
    near = nbr & 127
    which = nbr >> 7
    far, mine, live = [], [], []
    for t in range(EDGES // 128):
        cut = slice(t * 128, (t + 1) * 128)
        value = lanes_take(packed[0], near[:, cut])
        for b in range(1, 4):
            value = jnp.where(which[:, cut] == b, lanes_take(packed[b], near[:, cut]), value)
        far.append(value)
        mine.append(lanes_take(packed[0], atom[:, cut]))
        live.append(lanes_take(cnt_ref[...], atom[:, cut]))
    far = jnp.concatenate(far, axis=1)
    mine = jnp.concatenate(mine, axis=1)
    live = jnp.where(slot < jnp.concatenate(live, axis=1), 1.0, 0.0)

    def coordinates(value):
        return value & 511, (value >> 9) & 511, (value >> 18) & 127

    rel = [
        (p - q).astype(F32) * (1.0 / 16.0)
        for p, q in zip(coordinates(far), coordinates(mine))
    ]
    square = rel[0] * rel[0] + rel[1] * rel[1] + rel[2] * rel[2] + 1.0
    dist = jnp.sqrt(square)
    inverse = 1.0 / dist
    ux, uy, uz = (r * inverse for r in rel)
    spc_d[...] = far >> 25
    for number, value in enumerate((dist, live, inverse, ux, uy, uz)):
        vec_d[number] = value
    harm = (
        R3 * ux, R3 * uy, R3 * uz, R15 * ux * uy, R15 * uy * uz,
        0.5 * R5 * (3.0 * uz * uz - 1.0), R15 * ux * uz, 0.5 * R15 * (ux * ux - uy * uy),
    )
    for number, value in enumerate(harm):
        harm_t[number] = SCALE * value

    def radial_basis(g):
        centers = 1.0 + 2.0 * iota((NB, EDGES), 0).astype(F32)
        away = vec_d[0, pl.ds(g, 1), :] - centers
        return away, jnp.exp(-0.125 * away * away) * vec_d[1, pl.ds(g, 1), :]

    def sums_of(g, high, low):
        left = jnp.concatenate([hmat[g], hlow[g], hmat[g]], axis=1)
        return nt(left, jnp.concatenate([high, high, low], axis=1))

    def store_sums(ref, g, sums):
        at = pl.ds(pl.multiple_of(g * GROUP, GROUP), GROUP)
        for m in range(9):
            ref[m, at, :] = sums[m * GROUP : (m + 1) * GROUP]

    def first(g, carry):
        unit = jnp.where(mask, SCALE, 0.0)
        rows = [unit]
        for m in range(8):
            rows.append(jnp.where(mask, harm_t[m, pl.ds(g, 1), :], 0.0))
        rows.append(jnp.zeros((GROUP, EDGES), F32))
        rows, fine = split(jnp.concatenate(rows, axis=0))
        hmat[g] = rows.astype(BF16)
        hlow[g] = fine.astype(BF16)
        high, low = split(radial_basis(g)[1])
        basis[g] = jnp.concatenate([high, low, high, jnp.zeros_like(high)], axis=0).astype(BF16)
        kind = spc_d[pl.ds(g, 1), :]
        phi_high, phi_low = (
            jnp.concatenate([jnp.where(kind == k, v, 0.0) for k in range(species)], axis=0)
            for v in (high, low)
        )
        phi[g] = phi_high.astype(BF16)
        store_sums(kinds_amps, g, sums_of(g, phi[g], phi_low.astype(BF16)))
        return carry

    lax.fori_loop(0, CHUNKS, first, 0, unroll=8)
    for m in range(9):
        high, low = (v.astype(BF16) for v in split(kinds_amps[m]))
        amps1[m] = mm(high, kind_high) + mm(low, kind_high) + mm(high, kind_low)
    weights.wait()

    def update(amps, old, t):
        one = amps[1] * amps[1] + amps[2] * amps[2] + amps[3] * amps[3]
        two = amps[4] * amps[4] + amps[5] * amps[5] + amps[6] * amps[6]
        two += amps[7] * amps[7] + amps[8] * amps[8]
        flat = jnp.concatenate([amps[0], one, two], axis=1).astype(BF16)
        z = mm(flat, uw_ref[t])
        return z, (old + z * jax.nn.sigmoid(z)).astype(BF16)

    def back(amps, z, grad, t):
        sig = jax.nn.sigmoid(z)
        grad_z = grad * (sig * (1.0 + z * (1.0 - sig)))
        grad_inv = nt(grad_z.astype(BF16), uw_ref[t])
        gamps[0] = grad_inv[:, :128]
        for m in range(1, 9):
            part = grad_inv[:, 128:256] if m < 4 else grad_inv[:, 256:]
            gamps[m] = 2.0 * amps[m] * part

    kinds_own = onehot(spc_ref[...], 16).astype(F32).T.astype(BF16)
    h0_own = mm(
        kinds_own, jnp.concatenate([embed, jnp.zeros((16 - species, 128), F32)], axis=0).astype(BF16)
    )
    z1, h1 = update(amps1, h0_own, 0)
    z1_ref[...] = z1
    h_sec[1, 0:128] = h1
    h_own[...] = h1
    h_piece[...] = mm(ohxt[...], h1).astype(BF16)

    def h_parts(side):
        dx, dy = side
        if dx == 0:
            return h_own, h_sec.at[1 - dy, pl.ds(0, 128)]
        if dx == 1:
            return h_piece.at[pl.ds(0, 64)], h_sec.at[1 - dy, pl.ds(128, 64)]
        return h_piece.at[pl.ds(64, 64)], h_sec.at[1 - dy, pl.ds(192, 64)]

    copies = exchange(1, h_parts)

    def second_radial(g, carry):
        rad2[:, lanes(g)] = mm(w_t, basis[g])
        return carry

    lax.fori_loop(0, CHUNKS, second_radial, 0, unroll=8)
    own_t = h1.astype(F32).T
    finish(copies)

    got_t = h_sec[1, 128:256].astype(F32).T
    low_t = mm(ohyt[0], h_sec[0]).T
    high_t = mm(ohyt[1], h_sec[2]).T
    h_t = jnp.concatenate([own_t, got_t, low_t, high_t], axis=1).astype(BF16)

    def second(p, carry):
        gathered = mm(h_t, hot[:, lanes(p, 2)])
        gat2[:, lanes(p, 2)] = gathered.astype(BF16)
        for half in range(2):
            g = 2 * p + half
            message = gathered[:, half * EDGES : (half + 1) * EDGES] * rad2[:, lanes(g)]
            high, low = (v.astype(BF16) for v in split(message))
            store_sums(amps2, g, sums_of(g, high, low))
        return carry

    lax.fori_loop(0, PAIRS, second, 0, unroll=4)
    z2, h2 = update(amps2, h1.astype(F32), 1)
    out_w = ow_ref[...]
    high, rest = split(out_w)
    mid, low = split(rest)
    readout = jnp.concatenate([high, mid, low, jnp.zeros((5, 128), F32)], axis=0).astype(BF16)
    parts = nt(readout, h2)
    en_ref[...] = parts[0:1] + parts[1:2] + parts[2:3]
    back(amps2, z2, out_w, 1)

    def chunk_rows(ref, g):
        at = pl.ds(pl.multiple_of(g * GROUP, GROUP), GROUP)
        rows = [ref[m, at, :] for m in range(9)]
        return jnp.concatenate(rows + [jnp.zeros_like(rows[0])], axis=0)

    def features(g, carry):
        grad = mm(chunk_rows(gamps, g).T.astype(BF16), hmat[g])
        gms[:, lanes(g)] = grad.astype(BF16)
        rows_t[:, lanes(g)] = (grad * rad2[:, lanes(g)]).astype(BF16)
        return carry

    lax.fori_loop(0, CHUNKS, features, 0, unroll=8)
    gext[...] = nt(hot[...], rows_t[...])

    for number, start in ((0, 256), (1, 384)):
        g_sec[2 * number] = mm(ohy[number], gext[start : start + 128].astype(BF16)).astype(BF16)
    g_sec[1, 128:256] = gext[128:256].astype(BF16)

    def g_parts(side):
        dx, dy = side
        if dx == 0:
            return g_sec.at[1 + dy, pl.ds(0, 128)], g_own.at[(1 - dy) // 2]
        if dx == -1:
            return g_sec.at[1 + dy, pl.ds(128, 64)], g_piece.at[1 - dy, pl.ds(0, 64)]
        return g_sec.at[1 + dy, pl.ds(192, 64)], g_piece.at[1 - dy, pl.ds(64, 64)]

    copies = exchange(2, g_parts)

    def harmonic_rows(wide):
        rows = []
        for m in range(1, 9):
            part = jnp.where(mask, wide[m * GROUP : (m + 1) * GROUP], 0.0)
            rows.append(jnp.sum(part, axis=0, keepdims=True))
        return rows

    def distance_row(g, by_basis):
        away, value = radial_basis(g)
        return jnp.sum(by_basis * (-0.25 * away * value), axis=0, keepdims=True)

    def geometry_two(g, carry):
        gathered = gat2[:, lanes(g)].astype(F32)
        message = (gathered * rad2[:, lanes(g)]).astype(BF16)
        rows = harmonic_rows(mm(chunk_rows(gamps, g).astype(BF16), message))
        two = mm(w_rows, (gms[:, lanes(g)].astype(F32) * gathered).astype(BF16))
        rows.append(distance_row(g, two[0:NB] + two[NB:]))
        for number, value in enumerate(rows):
            gharm[number, pl.ds(g, 1), :] = value
        return carry

    lax.fori_loop(0, CHUNKS, geometry_two, 0, unroll=8)
    finish(copies)

    grad_h1 = gext[0:128] + out_w + g_own[0].astype(F32) + g_own[1].astype(F32)
    piece = g_piece[0].astype(F32) + g_piece[1].astype(F32) + g_piece[2].astype(F32)
    grad_h1 += mm(ohx[...], piece.astype(BF16))
    back(amps1, z1_ref[...], grad_h1, 0)

    for m in range(9):
        kinds_amps[m] = nt(gamps[m].astype(BF16), kind_high)

    def geometry_one(g, carry):
        grads = chunk_rows(kinds_amps, g)
        rows = harmonic_rows(mm(grads.astype(BF16), phi[g]))
        by_kind = mm(grads.T.astype(BF16), hmat[g])
        kind = spc_d[pl.ds(g, 1), :]
        by_basis = jnp.where(kind == 0, by_kind[0:NB], 0.0)
        for k in range(1, species):
            by_basis += jnp.where(kind == k, by_kind[k * NB : (k + 1) * NB], 0.0)
        rows.append(distance_row(g, by_basis))
        for number, value in enumerate(rows):
            gharm[number, pl.ds(g, 1), :] += value
        return carry

    lax.fori_loop(0, CHUNKS, geometry_one, 0, unroll=8)

    inv, vx, vy, vz = (vec_d[n] for n in range(2, 6))
    g1, g2, g3, g4, g5, g6, g7, g8 = (SCALE * gharm[n] for n in range(8))
    gx = R3 * g1 + R15 * (vy * g4 + vz * g7 + vx * g8)
    gy = R3 * g2 + R15 * (vx * g4 + vz * g5 - vy * g8)
    gz = R3 * g3 + R15 * (vy * g5 + vx * g7) + 3.0 * R5 * vz * g6
    along = gharm[8] - inv * (gx * vx + gy * vy + gz * vz)
    wide_rows = []
    for grad, unit in ((gx, vx), (gy, vy), (gz, vz)):
        wide_rows += split(grad * inv + unit * along)

    lane_atom = jnp.where(iota((ATOMS, EDGES), 0) % GROUP == of_lane[0:1], 1.0, 0.0).astype(BF16)
    sums = nt(jnp.concatenate(wide_rows, axis=0).astype(BF16), lane_atom)
    here = iota((CHUNKS, 128), 1) // GROUP == iota((CHUNKS, 128), 0)
    own_rows = []
    for number in range(3):
        both = sums[32 * number : 32 * number + 16] + sums[32 * number + 16 : 32 * number + 32]
        own_rows.append(jnp.sum(jnp.where(here, both, 0.0), axis=0, keepdims=True))

    upper, lower = nbr >> 6, nbr & 63
    left, right = [], []
    for g in range(CHUNKS):
        here = iota((8, EDGES), 0) == upper[g : g + 1]
        left.append(
            jnp.concatenate([jnp.where(here, v[g : g + 1], 0.0) for v in wide_rows], axis=0).astype(BF16)
        )
        right.append(onehot(lower[g : g + 1], 64))
    both = nt(jnp.concatenate(left, axis=1), jnp.concatenate(right, axis=1))
    coords = []
    for number in range(3):
        value = both[16 * number : 16 * number + 8] + both[16 * number + 8 : 16 * number + 16]
        coords.append(jnp.concatenate([value[k : k + 1] for k in range(8)], axis=1))
    total = jnp.concatenate(coords, axis=0)
    own_rows = jnp.concatenate(own_rows, axis=0)

    def six(value):
        high, low = split(value)
        return jnp.concatenate([high, low, jnp.zeros((2, value.shape[1]), F32)], axis=0).astype(BF16)

    def three(value):
        return value[0:3] + value[3:6]

    pad = jnp.zeros((5, 128), F32)
    for number, start in ((0, 256), (1, 384)):
        spread = three(nt(six(total[:, start : start + 128]), ohy[number]))
        p_out[number] = jnp.concatenate([spread[:, 0:128], pad], axis=0)
        p_piece[2 * number] = jnp.concatenate([spread[:, 128:256], pad], axis=0)
    p_piece[1] = jnp.concatenate([total[:, 128:256], pad], axis=0)

    def p_parts(side):
        dx, dy = side
        if dx == 0:
            return p_out.at[(1 + dy) // 2], p_own.at[(1 - dy) // 2]
        return p_piece.at[1 + dy], p_pin.at[1 - dy, (1 + dx) // 2]

    finish(exchange(3, p_parts))
    up = p_pin[0, 0] + p_pin[1, 0] + p_pin[2, 0]
    down = p_pin[0, 1] + p_pin[1, 1] + p_pin[2, 1]
    piece = jnp.where(iota((8, 128), 1) < 64, up, down)[0:3]
    result = total[:, 0:128] - own_rows + p_own[0][0:3] + p_own[1][0:3]
    result += three(nt(six(piece), ohx[...]))
    fo_ref[...] = -result


def body(remote, positions, species, neighbours, counts, send_x, send_y, embed, radial_w, update_w, out_w):
    vmem = pl.BlockSpec(memory_space=pltpu.VMEM)
    kinds = embed.shape[0] * NB
    whole = (128, CHUNKS * EDGES)
    scratch = [
        pltpu.VMEM((2, 8, 128), F32),
        pltpu.VMEM((8, 128), F32),
        pltpu.VMEM((3, 8, 128), F32),
        pltpu.VMEM((3, 2, 8, 128), F32),
        pltpu.VMEM((3, 256, 128), BF16),
        pltpu.VMEM((128, 128), BF16),
        pltpu.VMEM((128, 128), BF16),
        pltpu.VMEM((3, 256, 128), BF16),
        pltpu.VMEM((2, 128, 128), BF16),
        pltpu.VMEM((3, 128, 128), BF16),
        pltpu.VMEM((2, 8, 128), F32),
        pltpu.VMEM((3, 8, 128), F32),
        pltpu.VMEM((2, 8, 128), F32),
        pltpu.VMEM((3, 2, 8, 128), F32),
        pltpu.VMEM((ATOMS, SLOTS), I32),
        pltpu.VMEM((CHUNKS, EDGES), I32),
        pltpu.VMEM((CHUNKS, EDGES), I32),
        pltpu.VMEM((6, CHUNKS, EDGES), F32),
        pltpu.VMEM((8, CHUNKS, EDGES), F32),
        pltpu.VMEM((EXT, CHUNKS * EDGES), BF16),
        pltpu.VMEM((CHUNKS, 80, EDGES), BF16),
        pltpu.VMEM((CHUNKS, 80, EDGES), BF16),
        pltpu.VMEM((CHUNKS, 32, EDGES), BF16),
        pltpu.VMEM((CHUNKS, kinds, EDGES), BF16),
        pltpu.VMEM(whole, F32),
        pltpu.VMEM(whole, BF16),
        pltpu.VMEM(whole, BF16),
        pltpu.VMEM(whole, BF16),
        pltpu.VMEM((9, 128, kinds), F32),
        pltpu.VMEM((9, 128, 128), F32),
        pltpu.VMEM((9, 128, 128), F32),
        pltpu.VMEM((9, 128, 128), F32),
        pltpu.VMEM((128, 128), F32),
        pltpu.VMEM((EXT, 128), F32),
        pltpu.VMEM((9, CHUNKS, EDGES), F32),
        pltpu.VMEM((128, 128), BF16),
        pltpu.VMEM((128, 128), BF16),
        pltpu.VMEM((2, 256, 128), BF16),
        pltpu.VMEM((2, 128, 256), BF16),
        pltpu.VMEM(update_w.shape, BF16),
        pltpu.SemaphoreType.DMA,
        pltpu.SemaphoreType.DMA((4, 8)),
        pltpu.SemaphoreType.DMA((4, 8)),
    ]
    energy, forces = pl.pallas_call(
        functools.partial(kernel, remote),
        out_shape=(
            jax.ShapeDtypeStruct((1, ATOMS), F32),
            jax.ShapeDtypeStruct((3, ATOMS), F32),
        ),
        in_specs=[vmem] * 8 + [pl.BlockSpec(memory_space=pl.ANY), vmem],
        out_specs=(vmem, vmem),
        scratch_shapes=scratch,
        compiler_params=pltpu.CompilerParams(
            collective_id=0 if remote else None,
            has_side_effects=remote,
            vmem_limit_bytes=48 * 1024 * 1024,
        ),
    )(
        positions,
        species.reshape(1, ATOMS),
        neighbours.T,
        counts.reshape(1, ATOMS),
        send_x.reshape(2, 64),
        send_y.reshape(2, 128),
        embed,
        radial_w,
        update_w,
        out_w.reshape(1, WIDTH),
    )
    return energy.reshape(ATOMS), forces


def solution(mesh):
    return jax.shard_map(
        functools.partial(body, True),
        mesh=mesh,
        in_specs=(
            P(None, ("gx", "gy")),
            P(("gx", "gy")),
            P(("gx", "gy"), None),
            P(("gx", "gy")),
            P(("gx", "gy"), None, None),
            P(("gx", "gy"), None, None),
            P(),
            P(),
            P(),
            P(),
        ),
        out_specs=(P(("gx", "gy")), P(None, ("gx", "gy"))),
        check_vma=False,
    )
```

```python
import functools
import math

import jax
import jax.numpy as jnp
from jax import lax
from jax.experimental import pallas as pl
from jax.experimental.pallas import tpu as pltpu
from jax.sharding import PartitionSpec as P

F32 = jnp.float32
BF16 = jnp.bfloat16
I32 = jnp.int32
MESH = pl.DeviceIdType.MESH

ATOMS = 128
SLOTS = 48
GROUP = 8
CHUNKS = ATOMS // GROUP
PAIRS = CHUNKS // 2
EDGES = GROUP * SLOTS
WIDTH = 128
EXT = 512
NB = 8
BOX = 8.0
SCALE = 0.25
SIDES = ((0, 1), (0, -1), (1, 1), (1, -1), (-1, 1), (-1, -1), (1, 0), (-1, 0))
R3, R5, R15 = math.sqrt(3.0), math.sqrt(5.0), math.sqrt(15.0)


def mm(a, b):
    return lax.dot_general(a, b, (((1,), (0,)), ((), ())), preferred_element_type=F32)


def nt(a, b):
    return lax.dot_general(a, b, (((1,), (1,)), ((), ())), preferred_element_type=F32)


def iota(shape, axis):
    return lax.broadcasted_iota(I32, shape, axis)


def split(value):
    high = value.astype(BF16).astype(F32)
    return high, value - high


def onehot(index, total):
    shape = (total, index.shape[1])
    return jnp.where(iota(shape, 0) == index, 1.0, 0.0).astype(BF16)


def lanes_take(row, index):
    return jnp.take_along_axis(jnp.broadcast_to(row, index.shape), index, axis=1)


def kernel(
    remote,
    *refs,
):
    inputs, out_ref, held, refs = refs[:10], refs[10], refs[11:21], refs[21:]
    pos_ref, spc_ref, nbr_ref, cnt_ref, sx_ref, sy_ref, emb_ref, rw_ref, uw_ref, ow_ref = held
    (geo_out, geo_x, geo_in, geo_xin,
    h_sec, h_own, h_piece,
    g_sec, g_own, g_piece,
    p_out, p_piece, p_own, p_pin,
    nbr_t, nbr_d, spc_d, vec_d, harm_t, hot, hmat, basis, phi, rad2, gat2, gms, rows_t,
    kinds_amps, amps1, amps2, gamps, z1_ref, gext, gharm, ohx, ohxt, ohy, ohyt,
    in_sem, send_sem, recv_sem) = refs
    loads = [
        pltpu.make_async_copy(src, dst, in_sem.at[number])
        for number, (src, dst) in enumerate(zip(inputs, held))
    ]
    if remote:
        nx, ny = lax.axis_size("gx"), lax.axis_size("gy")
        me_x, me_y = lax.axis_index("gx"), lax.axis_index("gy")

        def place(side):
            return (lax.rem(me_x + side[0] + nx, nx), lax.rem(me_y + side[1] + ny, ny))

        barrier = pltpu.get_barrier_semaphore()
        for side in SIDES:
            pl.semaphore_signal(barrier, inc=1, device_id=place(side), device_id_type=MESH)

    def exchange(phase, parts, only=None):
        copies = []
        for number, side in enumerate(SIDES):
            if only is not None and not only(side):
                continue
            src, dst = parts(side)
            if remote:
                copy = pltpu.make_async_remote_copy(
                    src_ref=src, dst_ref=dst,
                    send_sem=send_sem.at[phase, number], recv_sem=recv_sem.at[phase, number],
                    device_id=place(side), device_id_type=MESH,
                )
            else:
                copy = pltpu.make_async_copy(src, dst, recv_sem.at[phase, number])
            copy.start()
            copies.append(copy)
        return copies

    def finish(copies):
        for copy in copies:
            copy.wait()

    for number in (0, 1, 4, 5, 2, 3, 6, 7, 9, 8):
        loads[number].start()
    for number in (0, 1, 4, 5):
        loads[number].wait()

    sx = jnp.concatenate([sx_ref[0:1, :], sx_ref[1:2, :]], axis=1)
    sel = jnp.where(iota((ATOMS, 128), 0) == sx, 1.0, 0.0)
    ohx[...] = sel.astype(BF16)
    ohxt[...] = sel.T.astype(BF16)

    spc = spc_ref[...].astype(F32)
    pos = pos_ref[...].astype(F32)
    zero = jnp.zeros((1, 128), F32)
    geo = jnp.concatenate([pos, spc, zero, zero, zero, zero], axis=0)
    sy = sy_ref[...].astype(F32)
    geo_out[0] = jnp.concatenate([pos, spc, sy[1:2], zero, zero, zero], axis=0)
    geo_out[1] = jnp.concatenate([pos, spc, sy[0:1], zero, zero, zero], axis=0)
    geo_x[...] = mm(geo.astype(BF16), ohx[...])

    if remote:
        pl.semaphore_wait(barrier, len(SIDES))

    def geo_parts(side):
        dx, dy = side
        if dx == 0:
            return geo_out.at[(1 + dy) // 2], geo_in.at[1 - dy]
        return geo_x, geo_xin.at[1 - dy, (1 - dx) // 2]

    copies = exchange(0, geo_parts)

    loads[2].wait()
    nbr_t[...] = nbr_ref[...].T
    nbr_d[...] = jnp.concatenate(
        [nbr_t[pl.ds(a, CHUNKS, stride=GROUP), :] for a in range(GROUP)], axis=1
    )

    def lanes(g, count=1):
        return pl.ds(pl.multiple_of(g * (count * EDGES), 128), count * EDGES)

    def build(g, carry):
        index = jnp.broadcast_to(nbr_d[pl.ds(g, 1), :], (16, EDGES)).astype(jnp.int16)
        one, none = jnp.ones((16, EDGES), BF16), jnp.zeros((16, EDGES), BF16)
        first_rows = iota((16, EDGES), 0).astype(jnp.int16)
        for block in range(EXT // 16):
            hot[16 * block : 16 * block + 16, lanes(g)] = jnp.where(
                index - jnp.int16(16 * block) == first_rows, one, none
            )
        return carry

    lax.fori_loop(0, CHUNKS, build, 0, unroll=8)

    lane = iota((CHUNKS, EDGES), 1)
    of_lane = jnp.zeros((CHUNKS, EDGES), I32)
    for a in range(1, GROUP):
        of_lane += (lane >= a * SLOTS).astype(I32)
    slot = lane - of_lane * SLOTS
    atom = iota((CHUNKS, EDGES), 0) * GROUP + of_lane
    mask = of_lane[:GROUP] == iota((GROUP, EDGES), 0)

    for number in (3, 6, 7, 9):
        loads[number].wait()
    high, low = split(rw_ref[1])
    w_t = jnp.concatenate([high, high, low, jnp.zeros_like(high)], axis=0).T.astype(BF16)
    w_rows = jnp.concatenate([high, low], axis=0).astype(BF16)
    embed = emb_ref[...].astype(F32)
    species = embed.shape[0]
    kind_w = jnp.concatenate([rw_ref[0] * embed[k : k + 1] for k in range(species)], axis=0)
    kind_high, kind_low = (v.astype(BF16) for v in split(kind_w))

    finish(copies)

    def section(j):
        own = geo if j == 0 else geo_in[1 + j]
        keep = iota((8, 128), 1) < 64
        row = iota((8, 128), 0)
        got = jnp.where(keep, geo_xin[1 + j, 0], geo_xin[1 + j, 1])
        got += jnp.where(row == 0, jnp.where(keep, -BOX, BOX), 0.0)
        return own, got

    row = iota((8, 128), 0)
    blocks = list(section(0))
    for number, j in enumerate((-1, 1)):
        own, got = section(j)
        index = own[4:5].astype(I32)
        chosen = jnp.where(iota((256, 128), 0) == index, 1.0, 0.0)
        ohy[number] = chosen.astype(BF16)
        ohyt[number] = chosen.T.astype(BF16)
        whole = jnp.concatenate([own, got], axis=1)
        whole = jnp.where(iota((8, 256), 0) < 4, whole, 0.0)
        picked = mm(whole.astype(BF16), ohy[number])
        blocks.append(picked + jnp.where(row == 1, BOX * j, 0.0))

    packed = []
    for block in blocks:
        x = ((block[0:1] + BOX) * 16.0).astype(I32)
        y = ((block[1:2] + BOX) * 16.0).astype(I32)
        zc = (block[2:3] * 16.0).astype(I32)
        packed.append(x + y * 512 + zc * 262144 + block[3:4].astype(I32) * 33554432)

    nbr = nbr_d[...]
    near = nbr & 127
    which = nbr >> 7
    far, mine, live = [], [], []
    for t in range(EDGES // 128):
        cut = slice(t * 128, (t + 1) * 128)
        value = lanes_take(packed[0], near[:, cut])
        for b in range(1, 4):
            value = jnp.where(which[:, cut] == b, lanes_take(packed[b], near[:, cut]), value)
        far.append(value)
        mine.append(lanes_take(packed[0], atom[:, cut]))
        live.append(lanes_take(cnt_ref[...], atom[:, cut]))
    far = jnp.concatenate(far, axis=1)
    mine = jnp.concatenate(mine, axis=1)
    live = jnp.where(slot < jnp.concatenate(live, axis=1), 1.0, 0.0)

    def coordinates(value):
        return value & 511, (value >> 9) & 511, (value >> 18) & 127

    rel = [
        (p - q).astype(F32) * (1.0 / 16.0)
        for p, q in zip(coordinates(far), coordinates(mine))
    ]
    square = rel[0] * rel[0] + rel[1] * rel[1] + rel[2] * rel[2] + 1.0
    dist = jnp.sqrt(square)
    inverse = 1.0 / dist
    ux, uy, uz = (r * inverse for r in rel)
    spc_d[...] = far >> 25
    for number, value in enumerate((dist, live, inverse, ux, uy, uz)):
        vec_d[number] = value
    harm = (
        R3 * ux, R3 * uy, R3 * uz, R15 * ux * uy, R15 * uy * uz,
        0.5 * R5 * (3.0 * uz * uz - 1.0), R15 * ux * uz, 0.5 * R15 * (ux * ux - uy * uy),
    )
    for number, value in enumerate(harm):
        harm_t[number] = SCALE * value

    def radial_basis(g):
        centers = 1.0 + 2.0 * iota((NB, EDGES), 0).astype(F32)
        away = vec_d[0, pl.ds(g, 1), :] - centers
        return away, jnp.exp(-0.125 * away * away) * vec_d[1, pl.ds(g, 1), :]

    def sums_of(g, high, low):
        fill = jnp.zeros((128 - high.shape[0], EDGES), BF16)
        right = [high, low] if high.shape[0] == 128 else [high, fill, low]
        both = nt(hmat[g], jnp.concatenate(right, axis=0))
        n = high.shape[0]
        return both[:80, :n] + both[:80, 128 : 128 + n] + both[80:, :n]

    def store_sums(ref, g, sums):
        at = pl.ds(pl.multiple_of(g * GROUP, GROUP), GROUP)
        for m in range(9):
            ref[m, at, :] = sums[m * GROUP : (m + 1) * GROUP]

    def first(g, carry):
        unit = jnp.where(mask, SCALE, 0.0)
        rows = [unit]
        for m in range(8):
            rows.append(jnp.where(mask, harm_t[m, pl.ds(g, 1), :], 0.0))
        rows.append(jnp.zeros((GROUP, EDGES), F32))
        rows, fine = split(jnp.concatenate(rows, axis=0))
        hmat[g, 0:80] = rows.astype(BF16)
        hmat[g, 80:160] = fine.astype(BF16)
        high, low = split(radial_basis(g)[1])
        basis[g] = jnp.concatenate([high, low, high, jnp.zeros_like(high)], axis=0).astype(BF16)
        kind = spc_d[pl.ds(g, 1), :]
        phi_high, phi_low = (
            jnp.concatenate([jnp.where(kind == k, v, 0.0) for k in range(species)], axis=0)
            for v in (high, low)
        )
        phi[g] = phi_high.astype(BF16)
        store_sums(kinds_amps, g, sums_of(g, phi[g], phi_low.astype(BF16)))
        return carry

    lax.fori_loop(0, CHUNKS, first, 0, unroll=8)
    for m in range(9):
        high, low = (v.astype(BF16) for v in split(kinds_amps[m]))
        amps1[m] = mm(high, kind_high) + mm(low, kind_high) + mm(high, kind_low)
    loads[8].wait()

    def update(amps, old, t):
        one = amps[1] * amps[1] + amps[2] * amps[2] + amps[3] * amps[3]
        two = amps[4] * amps[4] + amps[5] * amps[5] + amps[6] * amps[6]
        two += amps[7] * amps[7] + amps[8] * amps[8]
        flat = jnp.concatenate([amps[0], one, two], axis=1).astype(BF16)
        z = mm(flat, uw_ref[t])
        return z, (old + z * jax.nn.sigmoid(z)).astype(BF16)

    def back(amps, z, grad, t):
        sig = jax.nn.sigmoid(z)
        grad_z = grad * (sig * (1.0 + z * (1.0 - sig)))
        grad_inv = nt(grad_z.astype(BF16), uw_ref[t])
        gamps[0] = grad_inv[:, :128]
        for m in range(1, 9):
            part = grad_inv[:, 128:256] if m < 4 else grad_inv[:, 256:]
            gamps[m] = 2.0 * amps[m] * part

    kinds_own = onehot(spc_ref[...], 16).astype(F32).T.astype(BF16)
    h0_own = mm(
        kinds_own, jnp.concatenate([embed, jnp.zeros((16 - species, 128), F32)], axis=0).astype(BF16)
    )
    z1, h1 = update(amps1, h0_own, 0)
    z1_ref[...] = z1
    h_sec[1, 0:128] = h1
    h_own[...] = h1

    def h_parts(side):
        dx, dy = side
        if dx == 0:
            return h_own, h_sec.at[1 - dy, pl.ds(0, 128)]
        if dx == 1:
            return h_piece.at[pl.ds(0, 64)], h_sec.at[1 - dy, pl.ds(128, 64)]
        return h_piece.at[pl.ds(64, 64)], h_sec.at[1 - dy, pl.ds(192, 64)]

    copies = exchange(1, h_parts, lambda side: side[0] == 0)
    h_piece[...] = mm(ohxt[...], h1).astype(BF16)
    copies += exchange(1, h_parts, lambda side: side[0] != 0)

    def second_radial(g, carry):
        rad2[:, lanes(g)] = mm(w_t, basis[g])
        return carry

    lax.fori_loop(0, CHUNKS, second_radial, 0, unroll=8)
    own_t = h1.astype(F32).T
    finish(copies)

    got_t = h_sec[1, 128:256].astype(F32).T
    low_t = mm(ohyt[0], h_sec[0]).T
    high_t = mm(ohyt[1], h_sec[2]).T
    h_t = jnp.concatenate([own_t, got_t, low_t, high_t], axis=1).astype(BF16)

    def second(p, carry):
        gathered = mm(h_t, hot[:, lanes(p, 2)])
        gat2[:, lanes(p, 2)] = gathered.astype(BF16)
        for half in range(2):
            g = 2 * p + half
            message = gathered[:, half * EDGES : (half + 1) * EDGES] * rad2[:, lanes(g)]
            high, low = (v.astype(BF16) for v in split(message))
            store_sums(amps2, g, sums_of(g, high, low))
        return carry

    lax.fori_loop(0, PAIRS, second, 0, unroll=8)
    z2, h2 = update(amps2, h1.astype(F32), 1)
    out_w = ow_ref[...]
    back(amps2, z2, out_w, 1)

    def chunk_rows(ref, g):
        at = pl.ds(pl.multiple_of(g * GROUP, GROUP), GROUP)
        rows = [ref[m, at, :] for m in range(9)]
        return jnp.concatenate(rows + [jnp.zeros_like(rows[0])], axis=0)

    def features(g, carry):
        grad = mm(chunk_rows(gamps, g).T.astype(BF16), hmat[g, 0:80])
        gms[:, lanes(g)] = grad.astype(BF16)
        rows_t[:, lanes(g)] = (grad * rad2[:, lanes(g)]).astype(BF16)
        return carry

    lax.fori_loop(0, CHUNKS, features, 0, unroll=8)
    far_rows = nt(hot[256:512], rows_t[...]).astype(BF16)
    for number in range(2):
        g_sec[2 * number] = mm(ohy[number], far_rows[128 * number : 128 * number + 128]).astype(BF16)

    def g_parts(side):
        dx, dy = side
        if dx == 0:
            return g_sec.at[1 + dy, pl.ds(0, 128)], g_own.at[(1 - dy) // 2]
        if dx == -1:
            return g_sec.at[1 + dy, pl.ds(128, 64)], g_piece.at[1 - dy, pl.ds(0, 64)]
        return g_sec.at[1 + dy, pl.ds(192, 64)], g_piece.at[1 - dy, pl.ds(64, 64)]

    copies = exchange(2, g_parts, lambda side: side[1] != 0)
    near_rows = nt(hot[0:256], rows_t[...])
    g_sec[1, 128:256] = near_rows[128:256].astype(BF16)
    copies += exchange(2, g_parts, lambda side: side[1] == 0)
    gext[...] = near_rows[0:128]

    high, rest = split(out_w)
    mid, low = split(rest)
    readout = jnp.concatenate([high, mid, low, jnp.zeros((5, 128), F32)], axis=0).astype(BF16)
    parts = nt(readout, h2)
    energy = parts[0:1] + parts[1:2] + parts[2:3]

    def harmonic_rows(wide):
        rows = []
        for m in range(1, 9):
            part = jnp.where(mask, wide[m * GROUP : (m + 1) * GROUP], 0.0)
            rows.append(jnp.sum(part, axis=0, keepdims=True))
        return rows

    def distance_row(g, by_basis):
        away, value = radial_basis(g)
        return jnp.sum(by_basis * (-0.25 * away * value), axis=0, keepdims=True)

    def geometry_two(g, carry):
        gathered = gat2[:, lanes(g)].astype(F32)
        message = (gathered * rad2[:, lanes(g)]).astype(BF16)
        rows = harmonic_rows(mm(chunk_rows(gamps, g).astype(BF16), message))
        two = mm(w_rows, (gms[:, lanes(g)].astype(F32) * gathered).astype(BF16))
        rows.append(distance_row(g, two[0:NB] + two[NB:]))
        for number, value in enumerate(rows):
            gharm[number, pl.ds(g, 1), :] = value
        return carry

    lax.fori_loop(0, CHUNKS, geometry_two, 0, unroll=8)
    finish(copies)

    grad_h1 = gext[...] + out_w + g_own[0].astype(F32) + g_own[1].astype(F32)
    piece = g_piece[0].astype(F32) + g_piece[1].astype(F32) + g_piece[2].astype(F32)
    grad_h1 += mm(ohx[...], piece.astype(BF16))
    back(amps1, z1_ref[...], grad_h1, 0)

    for m in range(9):
        kinds_amps[m] = nt(gamps[m].astype(BF16), kind_high)

    def geometry_one(g, carry):
        grads = chunk_rows(kinds_amps, g)
        rows = harmonic_rows(mm(grads.astype(BF16), phi[g]))
        by_kind = mm(grads.T.astype(BF16), hmat[g, 0:80])
        kind = spc_d[pl.ds(g, 1), :]
        by_basis = jnp.where(kind == 0, by_kind[0:NB], 0.0)
        for k in range(1, species):
            by_basis += jnp.where(kind == k, by_kind[k * NB : (k + 1) * NB], 0.0)
        rows.append(distance_row(g, by_basis))
        for number, value in enumerate(rows):
            gharm[number, pl.ds(g, 1), :] += value
        return carry

    lax.fori_loop(0, CHUNKS, geometry_one, 0, unroll=8)

    inv, vx, vy, vz = (vec_d[n] for n in range(2, 6))
    g1, g2, g3, g4, g5, g6, g7, g8 = (SCALE * gharm[n] for n in range(8))
    gx = R3 * g1 + R15 * (vy * g4 + vz * g7 + vx * g8)
    gy = R3 * g2 + R15 * (vx * g4 + vz * g5 - vy * g8)
    gz = R3 * g3 + R15 * (vy * g5 + vx * g7) + 3.0 * R5 * vz * g6
    along = gharm[8] - inv * (gx * vx + gy * vy + gz * vz)
    wide_rows = []
    for grad, unit in ((gx, vx), (gy, vy), (gz, vz)):
        wide_rows += split(grad * inv + unit * along)

    lane_atom = jnp.where(iota((ATOMS, EDGES), 0) % GROUP == of_lane[0:1], 1.0, 0.0).astype(BF16)
    sums = nt(jnp.concatenate(wide_rows, axis=0).astype(BF16), lane_atom)
    here = iota((CHUNKS, 128), 1) // GROUP == iota((CHUNKS, 128), 0)
    own_rows = []
    for number in range(3):
        both = sums[32 * number : 32 * number + 16] + sums[32 * number + 16 : 32 * number + 32]
        own_rows.append(jnp.sum(jnp.where(here, both, 0.0), axis=0, keepdims=True))

    upper, lower = nbr >> 6, nbr & 63
    left, right = [], []
    for g in range(CHUNKS):
        here = iota((8, EDGES), 0) == upper[g : g + 1]
        left.append(
            jnp.concatenate([jnp.where(here, v[g : g + 1], 0.0) for v in wide_rows], axis=0).astype(BF16)
        )
        right.append(onehot(lower[g : g + 1], 64))
    both = nt(jnp.concatenate(left, axis=1), jnp.concatenate(right, axis=1))
    coords = []
    for number in range(3):
        value = both[16 * number : 16 * number + 8] + both[16 * number + 8 : 16 * number + 16]
        coords.append(jnp.concatenate([value[k : k + 1] for k in range(8)], axis=1))
    total = jnp.concatenate(coords, axis=0)
    own_rows = jnp.concatenate(own_rows, axis=0)

    def six(value):
        high, low = split(value)
        return jnp.concatenate([high, low, jnp.zeros((2, value.shape[1]), F32)], axis=0).astype(BF16)

    def three(value):
        return value[0:3] + value[3:6]

    pad = jnp.zeros((5, 128), F32)
    for number, start in ((0, 256), (1, 384)):
        spread = three(nt(six(total[:, start : start + 128]), ohy[number]))
        p_out[number] = jnp.concatenate([spread[:, 0:128], pad], axis=0)
        p_piece[2 * number] = jnp.concatenate([spread[:, 128:256], pad], axis=0)
    p_piece[1] = jnp.concatenate([total[:, 128:256], pad], axis=0)

    def p_parts(side):
        dx, dy = side
        if dx == 0:
            return p_out.at[(1 + dy) // 2], p_own.at[(1 - dy) // 2]
        return p_piece.at[1 + dy], p_pin.at[1 - dy, (1 + dx) // 2]

    finish(exchange(3, p_parts))
    up = p_pin[0, 0] + p_pin[1, 0] + p_pin[2, 0]
    down = p_pin[0, 1] + p_pin[1, 1] + p_pin[2, 1]
    piece = jnp.where(iota((8, 128), 1) < 64, up, down)[0:3]
    result = total[:, 0:128] - own_rows + p_own[0][0:3] + p_own[1][0:3]
    result += three(nt(six(piece), ohx[...]))
    out_ref[...] = jnp.concatenate([energy, -result, jnp.zeros((4, 128), F32)], axis=0)


def divide(out_ref, energy_ref, forces_ref):
    energy_ref[...] = out_ref[0:1]
    forces_ref[...] = out_ref[1:4]


def body(remote, positions, species, neighbours, counts, send_x, send_y, embed, radial_w, update_w, out_w):
    kinds = embed.shape[0] * NB
    whole = (128, CHUNKS * EDGES)
    scratch = [
        pltpu.VMEM((2, 8, 128), F32),
        pltpu.VMEM((8, 128), F32),
        pltpu.VMEM((3, 8, 128), F32),
        pltpu.VMEM((3, 2, 8, 128), F32),
        pltpu.VMEM((3, 256, 128), BF16),
        pltpu.VMEM((128, 128), BF16),
        pltpu.VMEM((128, 128), BF16),
        pltpu.VMEM((3, 256, 128), BF16),
        pltpu.VMEM((2, 128, 128), BF16),
        pltpu.VMEM((3, 128, 128), BF16),
        pltpu.VMEM((2, 8, 128), F32),
        pltpu.VMEM((3, 8, 128), F32),
        pltpu.VMEM((2, 8, 128), F32),
        pltpu.VMEM((3, 2, 8, 128), F32),
        pltpu.VMEM((ATOMS, SLOTS), I32),
        pltpu.VMEM((CHUNKS, EDGES), I32),
        pltpu.VMEM((CHUNKS, EDGES), I32),
        pltpu.VMEM((6, CHUNKS, EDGES), F32),
        pltpu.VMEM((8, CHUNKS, EDGES), F32),
        pltpu.VMEM((EXT, CHUNKS * EDGES), BF16),
        pltpu.VMEM((CHUNKS, 160, EDGES), BF16),
        pltpu.VMEM((CHUNKS, 32, EDGES), BF16),
        pltpu.VMEM((CHUNKS, kinds, EDGES), BF16),
        pltpu.VMEM(whole, F32),
        pltpu.VMEM(whole, BF16),
        pltpu.VMEM(whole, BF16),
        pltpu.VMEM(whole, BF16),
        pltpu.VMEM((9, 128, kinds), F32),
        pltpu.VMEM((9, 128, 128), F32),
        pltpu.VMEM((9, 128, 128), F32),
        pltpu.VMEM((9, 128, 128), F32),
        pltpu.VMEM((128, 128), F32),
        pltpu.VMEM((128, 128), F32),
        pltpu.VMEM((9, CHUNKS, EDGES), F32),
        pltpu.VMEM((128, 128), BF16),
        pltpu.VMEM((128, 128), BF16),
        pltpu.VMEM((2, 256, 128), BF16),
        pltpu.VMEM((2, 128, 256), BF16),
        pltpu.SemaphoreType.DMA((10,)),
        pltpu.SemaphoreType.DMA((4, 8)),
        pltpu.SemaphoreType.DMA((4, 8)),
    ]
    inputs = (
        positions,
        species.reshape(1, ATOMS),
        neighbours.T,
        counts.reshape(1, ATOMS),
        send_x.reshape(2, 64),
        send_y.reshape(2, 128),
        embed,
        radial_w,
        update_w,
        out_w.reshape(1, WIDTH),
    )
    out = pl.pallas_call(
        functools.partial(kernel, remote),
        out_shape=jax.ShapeDtypeStruct((8, ATOMS), F32),
        in_specs=[pl.BlockSpec(memory_space=pl.ANY)] * len(inputs),
        out_specs=pl.BlockSpec(memory_space=pltpu.VMEM),
        scratch_shapes=[pltpu.VMEM(v.shape, v.dtype) for v in inputs] + scratch,
        compiler_params=pltpu.CompilerParams(
            collective_id=0 if remote else None,
            has_side_effects=remote,
            vmem_limit_bytes=60 * 1024 * 1024,
        ),
    )(*inputs)
    energy, forces = pl.pallas_call(
        divide,
        out_shape=(
            jax.ShapeDtypeStruct((1, ATOMS), F32),
            jax.ShapeDtypeStruct((3, ATOMS), F32),
        ),
    )(out)
    return energy.reshape(ATOMS), forces


def solution(mesh):
    return jax.shard_map(
        functools.partial(body, True),
        mesh=mesh,
        in_specs=(
            P(None, ("gx", "gy")),
            P(("gx", "gy")),
            P(("gx", "gy"), None),
            P(("gx", "gy")),
            P(("gx", "gy"), None, None),
            P(("gx", "gy"), None, None),
            P(),
            P(),
            P(),
            P(),
        ),
        out_specs=(P(("gx", "gy")), P(None, ("gx", "gy"))),
        check_vma=False,
    )
```

```python
import functools
import math

import jax
import jax.numpy as jnp
from jax import lax
from jax.experimental import pallas as pl
from jax.experimental.pallas import tpu as pltpu
from jax.sharding import PartitionSpec as P

F32 = jnp.float32
BF16 = jnp.bfloat16
I32 = jnp.int32
MESH = pl.DeviceIdType.MESH

ATOMS = 128
SLOTS = 48
GROUP = 8
CHUNKS = ATOMS // GROUP
PAIRS = CHUNKS // 2
EDGES = GROUP * SLOTS
WIDTH = 128
EXT = 512
NB = 8
BOX = 8.0
SCALE = 0.25
SIDES = ((0, 1), (0, -1), (1, 1), (1, -1), (-1, 1), (-1, -1), (1, 0), (-1, 0))
R3, R5, R15 = math.sqrt(3.0), math.sqrt(5.0), math.sqrt(15.0)


def mm(a, b):
    return lax.dot_general(a, b, (((1,), (0,)), ((), ())), preferred_element_type=F32)


def nt(a, b):
    return lax.dot_general(a, b, (((1,), (1,)), ((), ())), preferred_element_type=F32)


def iota(shape, axis):
    return lax.broadcasted_iota(I32, shape, axis)


def split(value):
    high = value.astype(BF16).astype(F32)
    return high, value - high


def onehot(index, total):
    shape = (total, index.shape[1])
    return jnp.where(iota(shape, 0) == index, 1.0, 0.0).astype(BF16)


def lanes_take(row, index):
    return jnp.take_along_axis(jnp.broadcast_to(row, index.shape), index, axis=1)


def kernel(
    remote,
    *refs,
):
    inputs, en_ref, fo_ref, held, refs = refs[:10], refs[10], refs[11], refs[12:22], refs[22:]
    pos_ref, spc_ref, nbr_ref, cnt_ref, sx_ref, sy_ref, emb_ref, rw_ref, uw_ref, ow_ref = held
    (geo_out, geo_x, geo_in, geo_xin,
    h_sec, h_own, h_piece,
    g_sec, g_own, g_piece,
    p_out, p_piece, p_own, p_pin,
    nbr_t, nbr_d, spc_d, vec_d, harm_t, hot, low_hot, hmat, basis, phi, rad2, gat2, gms, rows_t,
    kinds_amps, amps1, amps2, gamps, z1_ref, gext, gharm, gdist, ohx, ohxt, ohy, ohyt,
    in_sem, send_sem, recv_sem) = refs
    loads = [
        pltpu.make_async_copy(src, dst, in_sem.at[number])
        for number, (src, dst) in enumerate(zip(inputs, held))
    ]
    if remote:
        nx, ny = lax.axis_size("gx"), lax.axis_size("gy")
        me_x, me_y = lax.axis_index("gx"), lax.axis_index("gy")

        def place(side):
            return (lax.rem(me_x + side[0] + nx, nx), lax.rem(me_y + side[1] + ny, ny))

        barrier = pltpu.get_barrier_semaphore()
        for side in SIDES:
            pl.semaphore_signal(barrier, inc=1, device_id=place(side), device_id_type=MESH)

    def exchange(phase, parts, only=None):
        copies = []
        for number, side in enumerate(SIDES):
            if only is not None and not only(side):
                continue
            src, dst = parts(side)
            if remote:
                copy = pltpu.make_async_remote_copy(
                    src_ref=src, dst_ref=dst,
                    send_sem=send_sem.at[phase, number], recv_sem=recv_sem.at[phase, number],
                    device_id=place(side), device_id_type=MESH,
                )
            else:
                copy = pltpu.make_async_copy(src, dst, recv_sem.at[phase, number])
            copy.start()
            copies.append(copy)
        return copies

    def finish(copies):
        for copy in copies:
            copy.wait()

    for number in (0, 1, 4, 5, 2, 3, 6, 7, 9, 8):
        loads[number].start()
    for number in (0, 1, 4, 5):
        loads[number].wait()

    sx = jnp.concatenate([sx_ref[0:1, :], sx_ref[1:2, :]], axis=1)
    sel = jnp.where(iota((ATOMS, 128), 0) == sx, 1.0, 0.0)
    ohx[...] = sel.astype(BF16)
    ohxt[...] = sel.T.astype(BF16)

    spc = spc_ref[...].astype(F32)
    pos = pos_ref[...].astype(F32)
    zero = jnp.zeros((1, 128), F32)
    geo = jnp.concatenate([pos, spc, zero, zero, zero, zero], axis=0)
    sy = sy_ref[...].astype(F32)
    geo_out[0] = jnp.concatenate([pos, spc, sy[1:2], zero, zero, zero], axis=0)
    geo_out[1] = jnp.concatenate([pos, spc, sy[0:1], zero, zero, zero], axis=0)
    geo_x[...] = mm(geo.astype(BF16), ohx[...])

    if remote:
        pl.semaphore_wait(barrier, len(SIDES))

    def geo_parts(side):
        dx, dy = side
        if dx == 0:
            return geo_out.at[(1 + dy) // 2], geo_in.at[1 - dy]
        return geo_x, geo_xin.at[1 - dy, (1 - dx) // 2]

    copies = exchange(0, geo_parts)

    loads[2].wait()
    nbr_t[...] = nbr_ref[...].T
    nbr_d[...] = jnp.concatenate(
        [nbr_t[pl.ds(a, CHUNKS, stride=GROUP), :] for a in range(GROUP)], axis=1
    )

    def lanes(g, count=1):
        return pl.ds(pl.multiple_of(g * (count * EDGES), 128), count * EDGES)

    def build(g, carry):
        index = jnp.broadcast_to(nbr_d[pl.ds(g, 1), :], (16, EDGES)).astype(jnp.int16)
        one, none = jnp.ones((16, EDGES), BF16), jnp.zeros((16, EDGES), BF16)
        first_rows = iota((16, EDGES), 0).astype(jnp.int16)
        for block in range(EXT // 16):
            hot[16 * block : 16 * block + 16, lanes(g)] = jnp.where(
                index - jnp.int16(16 * block) == first_rows, one, none
            )
        lower = index & jnp.int16(63)
        for block in range(4):
            low_hot[16 * block : 16 * block + 16, lanes(g)] = jnp.where(
                lower - jnp.int16(16 * block) == first_rows, one, none
            )
        return carry

    lax.fori_loop(0, CHUNKS, build, 0, unroll=8)

    lane = iota((CHUNKS, EDGES), 1)
    of_lane = jnp.zeros((CHUNKS, EDGES), I32)
    for a in range(1, GROUP):
        of_lane += (lane >= a * SLOTS).astype(I32)
    slot = lane - of_lane * SLOTS
    atom = iota((CHUNKS, EDGES), 0) * GROUP + of_lane
    mask = of_lane[:GROUP] == iota((GROUP, EDGES), 0)

    for number in (3, 6, 7, 9):
        loads[number].wait()
    high, low = split(rw_ref[1])
    w_t = jnp.concatenate([high, high, low, jnp.zeros_like(high)], axis=0).T.astype(BF16)
    w_rows = jnp.concatenate([high, low], axis=0).astype(BF16)
    embed = emb_ref[...].astype(F32)
    species = embed.shape[0]
    kind_w = jnp.concatenate([rw_ref[0] * embed[k : k + 1] for k in range(species)], axis=0)
    kind_high, kind_low = (v.astype(BF16) for v in split(kind_w))

    finish(copies)

    def section(j):
        own = geo if j == 0 else geo_in[1 + j]
        keep = iota((8, 128), 1) < 64
        row = iota((8, 128), 0)
        got = jnp.where(keep, geo_xin[1 + j, 0], geo_xin[1 + j, 1])
        got += jnp.where(row == 0, jnp.where(keep, -BOX, BOX), 0.0)
        return own, got

    row = iota((8, 128), 0)
    blocks = list(section(0))
    for number, j in enumerate((-1, 1)):
        own, got = section(j)
        index = own[4:5].astype(I32)
        chosen = jnp.where(iota((256, 128), 0) == index, 1.0, 0.0)
        ohy[number] = chosen.astype(BF16)
        ohyt[number] = chosen.T.astype(BF16)
        whole = jnp.concatenate([own, got], axis=1)
        whole = jnp.where(iota((8, 256), 0) < 4, whole, 0.0)
        picked = mm(whole.astype(BF16), ohy[number])
        blocks.append(picked + jnp.where(row == 1, BOX * j, 0.0))

    packed = []
    for block in blocks:
        x = ((block[0:1] + BOX) * 16.0).astype(I32)
        y = ((block[1:2] + BOX) * 16.0).astype(I32)
        zc = (block[2:3] * 16.0).astype(I32)
        packed.append(x + y * 512 + zc * 262144 + block[3:4].astype(I32) * 33554432)

    nbr = nbr_d[...]
    near = nbr & 127
    which = nbr >> 7
    far, mine, live = [], [], []
    for t in range(EDGES // 128):
        cut = slice(t * 128, (t + 1) * 128)
        value = lanes_take(packed[0], near[:, cut])
        for b in range(1, 4):
            value = jnp.where(which[:, cut] == b, lanes_take(packed[b], near[:, cut]), value)
        far.append(value)
        mine.append(lanes_take(packed[0], atom[:, cut]))
        live.append(lanes_take(cnt_ref[...], atom[:, cut]))
    far = jnp.concatenate(far, axis=1)
    mine = jnp.concatenate(mine, axis=1)
    live = jnp.where(slot < jnp.concatenate(live, axis=1), 1.0, 0.0)

    def coordinates(value):
        return value & 511, (value >> 9) & 511, (value >> 18) & 127

    rel = [
        (p - q).astype(F32) * (1.0 / 16.0)
        for p, q in zip(coordinates(far), coordinates(mine))
    ]
    square = rel[0] * rel[0] + rel[1] * rel[1] + rel[2] * rel[2] + 1.0
    dist = jnp.sqrt(square)
    inverse = 1.0 / dist
    ux, uy, uz = (r * inverse for r in rel)
    spc_d[...] = far >> 25
    for number, value in enumerate((dist, live, inverse, ux, uy, uz)):
        vec_d[number] = value
    harm = (
        R3 * ux, R3 * uy, R3 * uz, R15 * ux * uy, R15 * uy * uz,
        0.5 * R5 * (3.0 * uz * uz - 1.0), R15 * ux * uz, 0.5 * R15 * (ux * ux - uy * uy),
    )
    for number, value in enumerate(harm):
        harm_t[number], harm_t[8 + number] = split(SCALE * value)

    def radial_basis(g):
        centers = 1.0 + 2.0 * iota((NB, EDGES), 0).astype(F32)
        away = vec_d[0, pl.ds(g, 1), :] - centers
        return away, jnp.exp(-0.125 * away * away) * vec_d[1, pl.ds(g, 1), :]

    def sums_of(g, high, low):
        fill = jnp.zeros((128 - high.shape[0], EDGES), BF16)
        right = [high, low] if high.shape[0] == 128 else [high, fill, low]
        both = nt(hmat[g], jnp.concatenate(right, axis=0))
        n = high.shape[0]
        return both[:80, :n] + both[:80, 128 : 128 + n] + both[80:, :n]

    def store_sums(ref, g, sums):
        at = pl.ds(pl.multiple_of(g * GROUP, GROUP), GROUP)
        for m in range(9):
            ref[m, at, :] = sums[m * GROUP : (m + 1) * GROUP]

    def first(g, carry):
        none = jnp.zeros((GROUP, EDGES), F32)
        rows = [jnp.where(mask, SCALE, 0.0)]
        fine = [none]
        for m in range(8):
            rows.append(jnp.where(mask, harm_t[m, pl.ds(g, 1), :], 0.0))
            fine.append(jnp.where(mask, harm_t[8 + m, pl.ds(g, 1), :], 0.0))
        hmat[g, 0:80] = jnp.concatenate(rows + [none], axis=0).astype(BF16)
        hmat[g, 80:160] = jnp.concatenate(fine + [none], axis=0).astype(BF16)
        high, low = split(radial_basis(g)[1])
        basis[g] = jnp.concatenate([high, low, high, none], axis=0).astype(BF16)
        kind = jnp.broadcast_to(spc_d[pl.ds(g, 1), :], (16, EDGES)).astype(jnp.int16)
        kind -= (iota((16, EDGES), 0) >= 8).astype(jnp.int16)
        high, low = (jnp.concatenate([v, v], axis=0).astype(BF16) for v in (high, low))
        none = jnp.zeros((16, EDGES), BF16)
        phi_low = []
        for pair in range(species // 2):
            here = kind == jnp.int16(2 * pair)
            phi[g, 16 * pair : 16 * pair + 16] = jnp.where(here, high, none)
            phi_low.append(jnp.where(here, low, none))
        phi_low = jnp.concatenate(phi_low, axis=0)
        store_sums(kinds_amps, g, sums_of(g, phi[g], phi_low))
        return carry

    lax.fori_loop(0, CHUNKS, first, 0, unroll=8)
    for m in range(9):
        high, low = (v.astype(BF16) for v in split(kinds_amps[m]))
        amps1[m] = mm(high, kind_high) + mm(low, kind_high) + mm(high, kind_low)
    loads[8].wait()

    def update(amps, old, t):
        one = amps[1] * amps[1] + amps[2] * amps[2] + amps[3] * amps[3]
        two = amps[4] * amps[4] + amps[5] * amps[5] + amps[6] * amps[6]
        two += amps[7] * amps[7] + amps[8] * amps[8]
        flat = jnp.concatenate([amps[0], one, two], axis=1).astype(BF16)
        z = mm(flat, uw_ref[t])
        return z, (old + z * jax.nn.sigmoid(z)).astype(BF16)

    def back(amps, z, grad, t):
        sig = jax.nn.sigmoid(z)
        grad_z = grad * (sig * (1.0 + z * (1.0 - sig)))
        grad_inv = nt(grad_z.astype(BF16), uw_ref[t])
        gamps[0] = grad_inv[:, :128]
        for m in range(1, 9):
            part = grad_inv[:, 128:256] if m < 4 else grad_inv[:, 256:]
            gamps[m] = 2.0 * amps[m] * part

    kinds_own = onehot(spc_ref[...], 16).astype(F32).T.astype(BF16)
    h0_own = mm(
        kinds_own, jnp.concatenate([embed, jnp.zeros((16 - species, 128), F32)], axis=0).astype(BF16)
    )
    z1, h1 = update(amps1, h0_own, 0)
    z1_ref[...] = z1
    h_sec[1, 0:128] = h1
    h_own[...] = h1

    def h_parts(side):
        dx, dy = side
        if dx == 0:
            return h_own, h_sec.at[1 - dy, pl.ds(0, 128)]
        if dx == 1:
            return h_piece.at[pl.ds(0, 64)], h_sec.at[1 - dy, pl.ds(128, 64)]
        return h_piece.at[pl.ds(64, 64)], h_sec.at[1 - dy, pl.ds(192, 64)]

    copies = exchange(1, h_parts, lambda side: side[0] == 0)
    h_piece[...] = mm(ohxt[...], h1).astype(BF16)
    copies += exchange(1, h_parts, lambda side: side[0] != 0)

    def second_radial(g, carry):
        rad2[:, lanes(g)] = mm(w_t, basis[g])
        return carry

    lax.fori_loop(0, CHUNKS, second_radial, 0, unroll=8)
    own_t = h1.astype(F32).T
    finish(copies)

    got_t = h_sec[1, 128:256].astype(F32).T
    low_t = mm(ohyt[0], h_sec[0]).T
    high_t = mm(ohyt[1], h_sec[2]).T
    h_t = jnp.concatenate([own_t, got_t, low_t, high_t], axis=1).astype(BF16)

    def gather(p):
        gathered = mm(h_t, hot[:, lanes(p, 2)])
        gat2[:, lanes(p, 2)] = gathered.astype(BF16)

    def second(p, last):
        if not last:
            gather(p + 1)
        for half in range(2):
            g = 2 * p + half
            high, low = (
                v.astype(BF16) for v in split(gat2[:, lanes(g)].astype(F32) * rad2[:, lanes(g)])
            )
            store_sums(amps2, g, sums_of(g, high, low))

    gather(0)
    for p in range(PAIRS):
        second(p, p == PAIRS - 1)
    z2, h2 = update(amps2, h1.astype(F32), 1)
    out_w = ow_ref[...]
    back(amps2, z2, out_w, 1)

    def chunk_rows(ref, g):
        at = pl.ds(pl.multiple_of(g * GROUP, GROUP), GROUP)
        rows = [ref[m, at, :] for m in range(9)]
        return jnp.concatenate(rows + [jnp.zeros_like(rows[0])], axis=0)

    def features(p):
        for g in (2 * p, 2 * p + 1):
            grad = mm(chunk_rows(gamps, g).T.astype(BF16), hmat[g, 0:80])
            gms[:, lanes(g)] = grad.astype(BF16)
            rows_t[:, lanes(g)] = (grad * rad2[:, lanes(g)]).astype(BF16)

    features(0)
    far_rows = jnp.zeros((256, 128), F32)
    for p in range(PAIRS):
        if p + 1 < PAIRS:
            features(p + 1)
        far_rows += nt(hot[256:512, lanes(p, 2)], rows_t[:, lanes(p, 2)])
    far_rows = far_rows.astype(BF16)
    for number in range(2):
        g_sec[2 * number] = mm(ohy[number], far_rows[128 * number : 128 * number + 128]).astype(BF16)

    def g_parts(side):
        dx, dy = side
        if dx == 0:
            return g_sec.at[1 + dy, pl.ds(0, 128)], g_own.at[(1 - dy) // 2]
        if dx == -1:
            return g_sec.at[1 + dy, pl.ds(128, 64)], g_piece.at[1 - dy, pl.ds(0, 64)]
        return g_sec.at[1 + dy, pl.ds(192, 64)], g_piece.at[1 - dy, pl.ds(64, 64)]

    copies = exchange(2, g_parts, lambda side: side[1] != 0)
    near_rows = nt(hot[0:256], rows_t[...])
    g_sec[1, 128:256] = near_rows[128:256].astype(BF16)
    copies += exchange(2, g_parts, lambda side: side[1] == 0)
    gext[...] = near_rows[0:128]

    high, rest = split(out_w)
    mid, low = split(rest)
    readout = jnp.concatenate([high, mid, low, jnp.zeros((5, 128), F32)], axis=0).astype(BF16)
    parts = nt(readout, h2)
    en_ref[...] = parts[0:1] + parts[1:2] + parts[2:3]

    def harmonic_rows(wide):
        which = of_lane[:GROUP]
        result = jnp.zeros((8, EDGES), F32)
        for m in range(8):
            part = wide[(m + 1) * GROUP : (m + 2) * GROUP]
            part = jnp.concatenate(
                [
                    jnp.take_along_axis(part[:, t : t + 128], which[:, t : t + 128], axis=0)
                    for t in range(0, EDGES, 128)
                ],
                axis=1,
            )
            result = jnp.where(iota((8, EDGES), 0) == m, part, result)
        return result

    def distance_row(g, by_basis):
        away, value = radial_basis(g)
        return jnp.sum(by_basis * (-0.25 * away * value), axis=0, keepdims=True)

    def geometry_two(g, carry):
        gathered = gat2[:, lanes(g)].astype(F32)
        message = (gathered * rad2[:, lanes(g)]).astype(BF16)
        gharm[g] = harmonic_rows(mm(chunk_rows(gamps, g).astype(BF16), message))
        two = mm(w_rows, (gms[:, lanes(g)].astype(F32) * gathered).astype(BF16))
        gdist[pl.ds(g, 1), :] = distance_row(g, two[0:NB] + two[NB:])
        return carry

    lax.fori_loop(0, CHUNKS, geometry_two, 0, unroll=8)
    finish(copies)

    grad_h1 = gext[...] + out_w + g_own[0].astype(F32) + g_own[1].astype(F32)
    piece = g_piece[0].astype(F32) + g_piece[1].astype(F32) + g_piece[2].astype(F32)
    grad_h1 += mm(ohx[...], piece.astype(BF16))
    back(amps1, z1_ref[...], grad_h1, 0)

    for m in range(9):
        kinds_amps[m] = nt(gamps[m].astype(BF16), kind_high)

    def geometry_one(g, carry):
        grads = chunk_rows(kinds_amps, g)
        gharm[g] += harmonic_rows(mm(grads.astype(BF16), phi[g]))
        by_kind = mm(grads.T.astype(BF16), hmat[g, 0:80])
        kind = jnp.broadcast_to(spc_d[pl.ds(g, 1), :], (NB, EDGES))
        by_basis = jnp.where(kind == 0, by_kind[0:NB], 0.0)
        for k in range(1, species):
            by_basis += jnp.where(kind == k, by_kind[k * NB : (k + 1) * NB], 0.0)
        gdist[pl.ds(g, 1), :] += distance_row(g, by_basis)
        return carry

    lax.fori_loop(0, CHUNKS, geometry_one, 0, unroll=8)

    inv, vx, vy, vz = (vec_d[n] for n in range(2, 6))
    g1, g2, g3, g4, g5, g6, g7, g8 = (SCALE * gharm[:, n, :] for n in range(8))
    gx = R3 * g1 + R15 * (vy * g4 + vz * g7 + vx * g8)
    gy = R3 * g2 + R15 * (vx * g4 + vz * g5 - vy * g8)
    gz = R3 * g3 + R15 * (vy * g5 + vx * g7) + 3.0 * R5 * vz * g6
    along = gdist[...] - inv * (gx * vx + gy * vy + gz * vz)
    wide_rows = []
    for grad, unit in ((gx, vx), (gy, vy), (gz, vz)):
        wide_rows += split(grad * inv + unit * along)

    lane_atom = jnp.where(iota((ATOMS, EDGES), 0) % GROUP == of_lane[0:1], 1.0, 0.0).astype(BF16)
    sums = nt(jnp.concatenate(wide_rows, axis=0).astype(BF16), lane_atom)
    here = iota((CHUNKS, 128), 1) // GROUP == iota((CHUNKS, 128), 0)
    own_rows = []
    for number in range(3):
        both = sums[32 * number : 32 * number + 16] + sums[32 * number + 16 : 32 * number + 32]
        own_rows.append(jnp.sum(jnp.where(here, both, 0.0), axis=0, keepdims=True))

    upper = nbr >> 6
    left = []
    for g in range(CHUNKS):
        here = iota((8, EDGES), 0) == upper[g : g + 1]
        left.append(
            jnp.concatenate([jnp.where(here, v[g : g + 1], 0.0) for v in wide_rows], axis=0).astype(BF16)
        )
    both = nt(jnp.concatenate(left, axis=1), low_hot[...])
    coords = []
    for number in range(3):
        value = both[16 * number : 16 * number + 8] + both[16 * number + 8 : 16 * number + 16]
        coords.append(jnp.concatenate([value[k : k + 1] for k in range(8)], axis=1))
    total = jnp.concatenate(coords, axis=0)
    own_rows = jnp.concatenate(own_rows, axis=0)

    def six(value):
        high, low = split(value)
        return jnp.concatenate([high, low, jnp.zeros((2, value.shape[1]), F32)], axis=0).astype(BF16)

    def three(value):
        return value[0:3] + value[3:6]

    pad = jnp.zeros((5, 128), F32)
    for number, start in ((0, 256), (1, 384)):
        spread = three(nt(six(total[:, start : start + 128]), ohy[number]))
        p_out[number] = jnp.concatenate([spread[:, 0:128], pad], axis=0)
        p_piece[2 * number] = jnp.concatenate([spread[:, 128:256], pad], axis=0)
    p_piece[1] = jnp.concatenate([total[:, 128:256], pad], axis=0)

    def p_parts(side):
        dx, dy = side
        if dx == 0:
            return p_out.at[(1 + dy) // 2], p_own.at[(1 - dy) // 2]
        return p_piece.at[1 + dy], p_pin.at[1 - dy, (1 + dx) // 2]

    finish(exchange(3, p_parts))
    up = p_pin[0, 0] + p_pin[1, 0] + p_pin[2, 0]
    down = p_pin[0, 1] + p_pin[1, 1] + p_pin[2, 1]
    piece = jnp.where(iota((8, 128), 1) < 64, up, down)[0:3]
    result = total[:, 0:128] - own_rows + p_own[0][0:3] + p_own[1][0:3]
    result += three(nt(six(piece), ohx[...]))
    fo_ref[...] = -result


def place_outputs(energy_in, forces_in, energy_ref, forces_ref, sems):
    copies = [
        pltpu.make_async_copy(energy_in, energy_ref, sems.at[0]),
        pltpu.make_async_copy(forces_in, forces_ref, sems.at[1]),
    ]
    for copy in copies:
        copy.start()
    for copy in copies:
        copy.wait()


def body(remote, positions, species, neighbours, counts, send_x, send_y, embed, radial_w, update_w, out_w):
    kinds = embed.shape[0] * NB
    whole = (128, CHUNKS * EDGES)
    scratch = [
        pltpu.VMEM((2, 8, 128), F32),
        pltpu.VMEM((8, 128), F32),
        pltpu.VMEM((3, 8, 128), F32),
        pltpu.VMEM((3, 2, 8, 128), F32),
        pltpu.VMEM((3, 256, 128), BF16),
        pltpu.VMEM((128, 128), BF16),
        pltpu.VMEM((128, 128), BF16),
        pltpu.VMEM((3, 256, 128), BF16),
        pltpu.VMEM((2, 128, 128), BF16),
        pltpu.VMEM((3, 128, 128), BF16),
        pltpu.VMEM((2, 8, 128), F32),
        pltpu.VMEM((3, 8, 128), F32),
        pltpu.VMEM((2, 8, 128), F32),
        pltpu.VMEM((3, 2, 8, 128), F32),
        pltpu.VMEM((ATOMS, SLOTS), I32),
        pltpu.VMEM((CHUNKS, EDGES), I32),
        pltpu.VMEM((CHUNKS, EDGES), I32),
        pltpu.VMEM((6, CHUNKS, EDGES), F32),
        pltpu.VMEM((16, CHUNKS, EDGES), F32),
        pltpu.VMEM((EXT, CHUNKS * EDGES), BF16),
        pltpu.VMEM((64, CHUNKS * EDGES), BF16),
        pltpu.VMEM((CHUNKS, 160, EDGES), BF16),
        pltpu.VMEM((CHUNKS, 32, EDGES), BF16),
        pltpu.VMEM((CHUNKS, kinds, EDGES), BF16),
        pltpu.VMEM(whole, F32),
        pltpu.VMEM(whole, BF16),
        pltpu.VMEM(whole, BF16),
        pltpu.VMEM(whole, BF16),
        pltpu.VMEM((9, 128, kinds), F32),
        pltpu.VMEM((9, 128, 128), F32),
        pltpu.VMEM((9, 128, 128), F32),
        pltpu.VMEM((9, 128, 128), F32),
        pltpu.VMEM((128, 128), F32),
        pltpu.VMEM((128, 128), F32),
        pltpu.VMEM((CHUNKS, 8, EDGES), F32),
        pltpu.VMEM((CHUNKS, EDGES), F32),
        pltpu.VMEM((128, 128), BF16),
        pltpu.VMEM((128, 128), BF16),
        pltpu.VMEM((2, 256, 128), BF16),
        pltpu.VMEM((2, 128, 256), BF16),
        pltpu.SemaphoreType.DMA((10,)),
        pltpu.SemaphoreType.DMA((4, 8)),
        pltpu.SemaphoreType.DMA((4, 8)),
    ]
    inputs = (
        positions,
        species.reshape(1, ATOMS),
        neighbours.T,
        counts.reshape(1, ATOMS),
        send_x.reshape(2, 64),
        send_y.reshape(2, 128),
        embed,
        radial_w,
        update_w,
        out_w.reshape(1, WIDTH),
    )
    shapes = (
        jax.ShapeDtypeStruct((1, ATOMS), F32),
        jax.ShapeDtypeStruct((3, ATOMS), F32),
    )
    results = pl.pallas_call(
        functools.partial(kernel, remote),
        out_shape=shapes,
        in_specs=[pl.BlockSpec(memory_space=pl.ANY)] * len(inputs),
        out_specs=(pl.BlockSpec(memory_space=pltpu.VMEM), pl.BlockSpec(memory_space=pltpu.VMEM)),
        scratch_shapes=[pltpu.VMEM(v.shape, v.dtype) for v in inputs] + scratch,
        compiler_params=pltpu.CompilerParams(
            collective_id=0 if remote else None,
            has_side_effects=remote,
            vmem_limit_bytes=60 * 1024 * 1024,
        ),
    )(*inputs)
    anywhere = pl.BlockSpec(memory_space=pl.ANY)
    energy, forces = pl.pallas_call(
        place_outputs,
        out_shape=shapes,
        in_specs=[anywhere, anywhere],
        out_specs=(anywhere, anywhere),
        scratch_shapes=[pltpu.SemaphoreType.DMA((2,))],
        compiler_params=pltpu.CompilerParams(vmem_limit_bytes=60 * 1024 * 1024),
    )(*results)
    return energy.reshape(ATOMS), forces


def solution(mesh):
    return jax.shard_map(
        functools.partial(body, True),
        mesh=mesh,
        in_specs=(
            P(None, ("gx", "gy")),
            P(("gx", "gy")),
            P(("gx", "gy"), None),
            P(("gx", "gy")),
            P(("gx", "gy"), None, None),
            P(("gx", "gy"), None, None),
            P(),
            P(),
            P(),
            P(),
        ),
        out_specs=(P(("gx", "gy")), P(None, ("gx", "gy"))),
        check_vma=False,
    )
```

```python
import functools
import math

import jax
import jax.numpy as jnp
from jax import lax
from jax.experimental import pallas as pl
from jax.experimental.pallas import tpu as pltpu
from jax.sharding import PartitionSpec as P

F32 = jnp.float32
BF16 = jnp.bfloat16
I32 = jnp.int32
MESH = pl.DeviceIdType.MESH

ATOMS = 128
SLOTS = 48
GROUP = 8
CHUNKS = ATOMS // GROUP
PAIRS = CHUNKS // 2
EDGES = GROUP * SLOTS
WIDTH = 128
EXT = 512
NB = 8
BOX = 8.0
SCALE = 0.25
SIDES = ((0, 1), (0, -1), (1, 1), (1, -1), (-1, 1), (-1, -1), (1, 0), (-1, 0))
R3, R5, R15 = math.sqrt(3.0), math.sqrt(5.0), math.sqrt(15.0)


def mm(a, b):
    return lax.dot_general(a, b, (((1,), (0,)), ((), ())), preferred_element_type=F32)


def nt(a, b):
    return lax.dot_general(a, b, (((1,), (1,)), ((), ())), preferred_element_type=F32)


def iota(shape, axis):
    return lax.broadcasted_iota(I32, shape, axis)


def split(value):
    high = value.astype(BF16).astype(F32)
    return high, value - high


def onehot(index, total):
    shape = (total, index.shape[1])
    return jnp.where(iota(shape, 0) == index, 1.0, 0.0).astype(BF16)


def lanes_take(row, index):
    return jnp.take_along_axis(jnp.broadcast_to(row, index.shape), index, axis=1)


def kernel(
    remote,
    *refs,
):
    inputs, en_ref, fo_ref, held, refs = refs[:10], refs[10], refs[11], refs[12:22], refs[22:]
    pos_ref, spc_ref, nbr_ref, cnt_ref, sx_ref, sy_ref, emb_ref, rw_ref, uw_ref, ow_ref = held
    (geo_out, geo_x, geo_in, geo_xin,
    h_sec, h_own, h_piece,
    g_sec, g_own, g_piece,
    p_out, p_piece, p_own, p_pin,
    nbr_t, nbr_d, spc_d, vec_d, harm_t, hot, low_hot, hmat, basis, phi, rad2, gat2, gms, rows_t,
    kinds_amps, amps1, amps2, gamps, z1_ref, gext, gharm, gdist, ohx, ohxt, ohy, ohyt,
    in_sem, send_sem, recv_sem) = refs
    loads = [
        pltpu.make_async_copy(src, dst, in_sem.at[number])
        for number, (src, dst) in enumerate(zip(inputs, held))
    ]
    if remote:
        nx, ny = lax.axis_size("gx"), lax.axis_size("gy")
        me_x, me_y = lax.axis_index("gx"), lax.axis_index("gy")

        xs = (me_x, lax.rem(me_x + 1, nx), lax.rem(me_x + nx - 1, nx))
        ys = (me_y, lax.rem(me_y + 1, ny), lax.rem(me_y + ny - 1, ny))

        def place(side):
            return (xs[side[0]], ys[side[1]])

        barrier = pltpu.get_barrier_semaphore()
        for side in SIDES:
            pl.semaphore_signal(barrier, inc=1, device_id=place(side), device_id_type=MESH)

    def exchange(phase, parts, only=None):
        copies = []
        for number, side in enumerate(SIDES):
            if only is not None and not only(side):
                continue
            src, dst = parts(side)
            if remote:
                copy = pltpu.make_async_remote_copy(
                    src_ref=src, dst_ref=dst,
                    send_sem=send_sem.at[phase, number], recv_sem=recv_sem.at[phase, number],
                    device_id=place(side), device_id_type=MESH,
                )
            else:
                copy = pltpu.make_async_copy(src, dst, recv_sem.at[phase, number])
            copy.start()
            copies.append(copy)
        return copies

    def finish(copies):
        for copy in copies:
            copy.wait()

    for number in (0, 1, 4, 5, 2, 3, 6, 7, 9, 8):
        loads[number].start()
    for number in (0, 1, 4, 5):
        loads[number].wait()

    sx = jnp.concatenate([sx_ref[0:1, :], sx_ref[1:2, :]], axis=1)
    sel = jnp.where(iota((ATOMS, 128), 0) == sx, 1.0, 0.0)
    ohx[...] = sel.astype(BF16)
    ohxt[...] = sel.T.astype(BF16)

    spc = spc_ref[...].astype(F32)
    pos = pos_ref[...].astype(F32)
    zero = jnp.zeros((1, 128), F32)
    geo = jnp.concatenate([pos, spc, zero, zero, zero, zero], axis=0)
    sy = sy_ref[...].astype(F32)
    geo_out[0] = jnp.concatenate([pos, spc, sy[1:2], zero, zero, zero], axis=0)
    geo_out[1] = jnp.concatenate([pos, spc, sy[0:1], zero, zero, zero], axis=0)
    geo_x[...] = mm(geo.astype(BF16), ohx[...])

    if remote:
        pl.semaphore_wait(barrier, len(SIDES))

    def geo_parts(side):
        dx, dy = side
        if dx == 0:
            return geo_out.at[(1 + dy) // 2], geo_in.at[1 - dy]
        return geo_x, geo_xin.at[1 - dy, (1 - dx) // 2]

    copies = exchange(0, geo_parts)

    loads[2].wait()
    nbr_t[...] = nbr_ref[...].T
    nbr_d[...] = jnp.concatenate(
        [nbr_t[pl.ds(a, CHUNKS, stride=GROUP), :] for a in range(GROUP)], axis=1
    )

    def lanes(g, count=1):
        return pl.ds(pl.multiple_of(g * (count * EDGES), 128), count * EDGES)

    def build(g, carry):
        index = jnp.broadcast_to(nbr_d[pl.ds(g, 1), :], (16, EDGES)).astype(jnp.int16)
        one, none = jnp.ones((16, EDGES), BF16), jnp.zeros((16, EDGES), BF16)
        first_rows = iota((16, EDGES), 0).astype(jnp.int16)
        for block in range(EXT // 16):
            hot[16 * block : 16 * block + 16, lanes(g)] = jnp.where(
                index - jnp.int16(16 * block) == first_rows, one, none
            )
        lower = index & jnp.int16(63)
        for block in range(4):
            low_hot[16 * block : 16 * block + 16, lanes(g)] = jnp.where(
                lower - jnp.int16(16 * block) == first_rows, one, none
            )
        return carry

    lax.fori_loop(0, CHUNKS, build, 0, unroll=8)

    lane = iota((CHUNKS, EDGES), 1)
    of_lane = jnp.zeros((CHUNKS, EDGES), I32)
    for a in range(1, GROUP):
        of_lane += (lane >= a * SLOTS).astype(I32)
    slot = lane - of_lane * SLOTS
    atom = iota((CHUNKS, EDGES), 0) * GROUP + of_lane
    mask = of_lane[:GROUP] == iota((GROUP, EDGES), 0)

    for number in (3, 6, 7, 9):
        loads[number].wait()
    high, low = split(rw_ref[1])
    w_t = jnp.concatenate([high, high, low, jnp.zeros_like(high)], axis=0).T.astype(BF16)
    w_rows = jnp.concatenate([high, low], axis=0).astype(BF16)
    embed = emb_ref[...].astype(F32)
    species = embed.shape[0]
    kind_w = jnp.concatenate([rw_ref[0] * embed[k : k + 1] for k in range(species)], axis=0)
    kind_high, kind_low = (v.astype(BF16) for v in split(kind_w))

    finish(copies)

    def section(j):
        own = geo if j == 0 else geo_in[1 + j]
        keep = iota((8, 128), 1) < 64
        row = iota((8, 128), 0)
        got = jnp.where(keep, geo_xin[1 + j, 0], geo_xin[1 + j, 1])
        got += jnp.where(row == 0, jnp.where(keep, -BOX, BOX), 0.0)
        return own, got

    row = iota((8, 128), 0)
    blocks = list(section(0))
    for number, j in enumerate((-1, 1)):
        own, got = section(j)
        index = own[4:5].astype(I32)
        chosen = jnp.where(iota((256, 128), 0) == index, 1.0, 0.0)
        ohy[number] = chosen.astype(BF16)
        ohyt[number] = chosen.T.astype(BF16)
        whole = jnp.concatenate([own, got], axis=1)
        whole = jnp.where(iota((8, 256), 0) < 4, whole, 0.0)
        picked = mm(whole.astype(BF16), ohy[number])
        blocks.append(picked + jnp.where(row == 1, BOX * j, 0.0))

    packed = []
    for block in blocks:
        x = ((block[0:1] + BOX) * 16.0).astype(I32)
        y = ((block[1:2] + BOX) * 16.0).astype(I32)
        zc = (block[2:3] * 16.0).astype(I32)
        packed.append(x + y * 512 + zc * 262144 + block[3:4].astype(I32) * 33554432)

    nbr = nbr_d[...]
    near = nbr & 127
    which = nbr >> 7
    far, mine, live = [], [], []
    for t in range(EDGES // 128):
        cut = slice(t * 128, (t + 1) * 128)
        value = lanes_take(packed[0], near[:, cut])
        for b in range(1, 4):
            value = jnp.where(which[:, cut] == b, lanes_take(packed[b], near[:, cut]), value)
        far.append(value)
        mine.append(lanes_take(packed[0], atom[:, cut]))
        live.append(lanes_take(cnt_ref[...], atom[:, cut]))
    far = jnp.concatenate(far, axis=1)
    mine = jnp.concatenate(mine, axis=1)
    live = jnp.where(slot < jnp.concatenate(live, axis=1), 1.0, 0.0)

    def coordinates(value):
        return value & 511, (value >> 9) & 511, (value >> 18) & 127

    rel = [
        (p - q).astype(F32) * (1.0 / 16.0)
        for p, q in zip(coordinates(far), coordinates(mine))
    ]
    square = rel[0] * rel[0] + rel[1] * rel[1] + rel[2] * rel[2] + 1.0
    dist = jnp.sqrt(square)
    inverse = 1.0 / dist
    ux, uy, uz = (r * inverse for r in rel)
    spc_d[...] = far >> 25
    for number, value in enumerate((dist, live, inverse, ux, uy, uz)):
        vec_d[number] = value
    harm = (
        R3 * ux, R3 * uy, R3 * uz, R15 * ux * uy, R15 * uy * uz,
        0.5 * R5 * (3.0 * uz * uz - 1.0), R15 * ux * uz, 0.5 * R15 * (ux * ux - uy * uy),
    )
    for number, value in enumerate(harm):
        harm_t[number], harm_t[8 + number] = split(SCALE * value)

    def radial_basis(g):
        centers = 1.0 + 2.0 * iota((NB, EDGES), 0).astype(F32)
        away = vec_d[0, pl.ds(g, 1), :] - centers
        return away, jnp.exp(-0.125 * away * away) * vec_d[1, pl.ds(g, 1), :]

    def sums_of(g, high, low):
        fill = jnp.zeros((128 - high.shape[0], EDGES), BF16)
        right = [high, low] if high.shape[0] == 128 else [high, fill, low]
        both = nt(hmat[g], jnp.concatenate(right, axis=0))
        n = high.shape[0]
        return both[:80, :n] + both[:80, 128 : 128 + n] + both[80:, :n]

    def store_sums(ref, g, sums):
        at = pl.ds(pl.multiple_of(g * GROUP, GROUP), GROUP)
        for m in range(9):
            ref[m, at, :] = sums[m * GROUP : (m + 1) * GROUP]

    def first(g, carry):
        none = jnp.zeros((GROUP, EDGES), F32)
        rows = [jnp.where(mask, SCALE, 0.0)]
        fine = [none]
        for m in range(8):
            rows.append(jnp.where(mask, harm_t[m, pl.ds(g, 1), :], 0.0))
            fine.append(jnp.where(mask, harm_t[8 + m, pl.ds(g, 1), :], 0.0))
        hmat[g, 0:80] = jnp.concatenate(rows + [none], axis=0).astype(BF16)
        hmat[g, 80:160] = jnp.concatenate(fine + [none], axis=0).astype(BF16)
        high, low = split(radial_basis(g)[1])
        basis[g] = jnp.concatenate([high, low, high, none], axis=0).astype(BF16)
        kind = jnp.broadcast_to(spc_d[pl.ds(g, 1), :], (16, EDGES)).astype(jnp.int16)
        kind -= (iota((16, EDGES), 0) >= 8).astype(jnp.int16)
        high, low = (jnp.concatenate([v, v], axis=0).astype(BF16) for v in (high, low))
        none = jnp.zeros((16, EDGES), BF16)
        phi_low = []
        for pair in range(species // 2):
            here = kind == jnp.int16(2 * pair)
            phi[g, 16 * pair : 16 * pair + 16] = jnp.where(here, high, none)
            phi_low.append(jnp.where(here, low, none))
        phi_low = jnp.concatenate(phi_low, axis=0)
        store_sums(kinds_amps, g, sums_of(g, phi[g], phi_low))
        return carry

    lax.fori_loop(0, CHUNKS, first, 0, unroll=8)
    for m in range(9):
        high, low = (v.astype(BF16) for v in split(kinds_amps[m]))
        amps1[m] = mm(high, kind_high) + mm(low, kind_high) + mm(high, kind_low)
    loads[8].wait()

    def update(amps, old, t):
        one = amps[1] * amps[1] + amps[2] * amps[2] + amps[3] * amps[3]
        two = amps[4] * amps[4] + amps[5] * amps[5] + amps[6] * amps[6]
        two += amps[7] * amps[7] + amps[8] * amps[8]
        flat = jnp.concatenate([amps[0], one, two], axis=1).astype(BF16)
        z = mm(flat, uw_ref[t])
        return z, (old + z * jax.nn.sigmoid(z)).astype(BF16)

    def slope(z):
        sig = jax.nn.sigmoid(z)
        return sig * (1.0 + z * (1.0 - sig))

    def back(amps, steep, grad, t):
        grad_z = grad * steep
        grad_inv = nt(grad_z.astype(BF16), uw_ref[t])
        gamps[0] = grad_inv[:, :128]
        for m in range(1, 9):
            part = grad_inv[:, 128:256] if m < 4 else grad_inv[:, 256:]
            gamps[m] = 2.0 * amps[m] * part

    kinds_own = onehot(spc_ref[...], 16).astype(F32).T.astype(BF16)
    h0_own = mm(
        kinds_own, jnp.concatenate([embed, jnp.zeros((16 - species, 128), F32)], axis=0).astype(BF16)
    )
    z1, h1 = update(amps1, h0_own, 0)
    h_sec[1, 0:128] = h1
    h_own[...] = h1

    def h_parts(side):
        dx, dy = side
        if dx == 0:
            return h_own, h_sec.at[1 - dy, pl.ds(0, 128)]
        if dx == 1:
            return h_piece.at[pl.ds(0, 64)], h_sec.at[1 - dy, pl.ds(128, 64)]
        return h_piece.at[pl.ds(64, 64)], h_sec.at[1 - dy, pl.ds(192, 64)]

    copies = exchange(1, h_parts, lambda side: side[0] == 0)
    h_piece[...] = mm(ohxt[...], h1).astype(BF16)
    copies += exchange(1, h_parts, lambda side: side[0] != 0)
    z1_ref[...] = slope(z1)

    def second_radial(g, carry):
        rad2[:, lanes(g)] = mm(w_t, basis[g])
        return carry

    lax.fori_loop(0, CHUNKS, second_radial, 0, unroll=8)
    own_t = h1.astype(F32).T
    finish(copies)

    got_t = h_sec[1, 128:256].astype(F32).T
    low_t = mm(ohyt[0], h_sec[0]).T
    high_t = mm(ohyt[1], h_sec[2]).T
    h_t = jnp.concatenate([own_t, got_t, low_t, high_t], axis=1).astype(BF16)

    def gather(p):
        gathered = mm(h_t, hot[:, lanes(p, 2)])
        gat2[:, lanes(p, 2)] = gathered.astype(BF16)

    def second(p, last):
        if not last:
            gather(p + 1)
        for half in range(2):
            g = 2 * p + half
            high, low = (
                v.astype(BF16) for v in split(gat2[:, lanes(g)].astype(F32) * rad2[:, lanes(g)])
            )
            store_sums(amps2, g, sums_of(g, high, low))

    gather(0)
    for p in range(PAIRS):
        second(p, p == PAIRS - 1)
    z2, h2 = update(amps2, h1.astype(F32), 1)
    out_w = ow_ref[...]
    back(amps2, slope(z2), out_w, 1)

    def chunk_rows(ref, g):
        at = pl.ds(pl.multiple_of(g * GROUP, GROUP), GROUP)
        rows = [ref[m, at, :] for m in range(9)]
        return jnp.concatenate(rows + [jnp.zeros_like(rows[0])], axis=0)

    def features(p):
        for g in (2 * p, 2 * p + 1):
            grad = mm(chunk_rows(gamps, g).T.astype(BF16), hmat[g, 0:80])
            gms[:, lanes(g)] = grad.astype(BF16)
            rows_t[:, lanes(g)] = (grad * rad2[:, lanes(g)]).astype(BF16)

    features(0)
    far_rows = jnp.zeros((256, 128), F32)
    for p in range(PAIRS):
        if p + 1 < PAIRS:
            features(p + 1)
        far_rows += nt(hot[256:512, lanes(p, 2)], rows_t[:, lanes(p, 2)])
    far_rows = far_rows.astype(BF16)
    for number in range(2):
        g_sec[2 * number] = mm(ohy[number], far_rows[128 * number : 128 * number + 128]).astype(BF16)

    def g_parts(side):
        dx, dy = side
        if dx == 0:
            return g_sec.at[1 + dy, pl.ds(0, 128)], g_own.at[(1 - dy) // 2]
        if dx == -1:
            return g_sec.at[1 + dy, pl.ds(128, 64)], g_piece.at[1 - dy, pl.ds(0, 64)]
        return g_sec.at[1 + dy, pl.ds(192, 64)], g_piece.at[1 - dy, pl.ds(64, 64)]

    copies = exchange(2, g_parts, lambda side: side[1] != 0)
    near_rows = nt(hot[0:256], rows_t[...])
    g_sec[1, 128:256] = near_rows[128:256].astype(BF16)
    copies += exchange(2, g_parts, lambda side: side[1] == 0)
    gext[...] = near_rows[0:128]

    high, rest = split(out_w)
    mid, low = split(rest)
    readout = jnp.concatenate([high, mid, low, jnp.zeros((5, 128), F32)], axis=0).astype(BF16)
    parts = nt(readout, h2)
    en_ref[...] = parts[0:1] + parts[1:2] + parts[2:3]

    def harmonic_rows(wide):
        which = of_lane[:GROUP]
        result = jnp.zeros((8, EDGES), F32)
        for m in range(8):
            part = wide[(m + 1) * GROUP : (m + 2) * GROUP]
            part = jnp.concatenate(
                [
                    jnp.take_along_axis(part[:, t : t + 128], which[:, t : t + 128], axis=0)
                    for t in range(0, EDGES, 128)
                ],
                axis=1,
            )
            result = jnp.where(iota((8, EDGES), 0) == m, part, result)
        return result

    def distance_row(g, by_basis):
        away, value = radial_basis(g)
        return jnp.sum(by_basis * (-0.25 * away * value), axis=0, keepdims=True)

    def geometry_two(g, carry):
        gathered = gat2[:, lanes(g)].astype(F32)
        message = (gathered * rad2[:, lanes(g)]).astype(BF16)
        gharm[g] = harmonic_rows(mm(chunk_rows(gamps, g).astype(BF16), message))
        two = mm(w_rows, (gms[:, lanes(g)].astype(F32) * gathered).astype(BF16))
        gdist[pl.ds(g, 1), :] = distance_row(g, two[0:NB] + two[NB:])
        return carry

    lax.fori_loop(0, CHUNKS, geometry_two, 0, unroll=8)
    finish(copies)

    grad_h1 = gext[...] + out_w + g_own[0].astype(F32) + g_own[1].astype(F32)
    piece = g_piece[0].astype(F32) + g_piece[1].astype(F32) + g_piece[2].astype(F32)
    grad_h1 += mm(ohx[...], piece.astype(BF16))
    back(amps1, z1_ref[...], grad_h1, 0)

    for m in range(9):
        kinds_amps[m] = nt(gamps[m].astype(BF16), kind_high)

    def geometry_one(g, carry):
        grads = chunk_rows(kinds_amps, g)
        gharm[g] += harmonic_rows(mm(grads.astype(BF16), phi[g]))
        by_kind = mm(grads.T.astype(BF16), hmat[g, 0:80])
        kind = jnp.broadcast_to(spc_d[pl.ds(g, 1), :], (NB, EDGES))
        blocks = [by_kind[k * NB : (k + 1) * NB] for k in range(species)]
        bit = 1
        while len(blocks) > 1:
            odd = (kind & bit) != 0
            blocks = [
                jnp.where(odd, blocks[k + 1], blocks[k]) if k + 1 < len(blocks) else blocks[k]
                for k in range(0, len(blocks), 2)
            ]
            bit *= 2
        by_basis = blocks[0]
        gdist[pl.ds(g, 1), :] += distance_row(g, by_basis)
        return carry

    lax.fori_loop(0, CHUNKS, geometry_one, 0, unroll=8)

    inv, vx, vy, vz = (vec_d[n] for n in range(2, 6))
    g1, g2, g3, g4, g5, g6, g7, g8 = (SCALE * gharm[:, n, :] for n in range(8))
    gx = R3 * g1 + R15 * (vy * g4 + vz * g7 + vx * g8)
    gy = R3 * g2 + R15 * (vx * g4 + vz * g5 - vy * g8)
    gz = R3 * g3 + R15 * (vy * g5 + vx * g7) + 3.0 * R5 * vz * g6
    along = gdist[...] - inv * (gx * vx + gy * vy + gz * vz)
    wide_rows = []
    for grad, unit in ((gx, vx), (gy, vy), (gz, vz)):
        wide_rows += split(grad * inv + unit * along)

    lane_atom = jnp.where(iota((ATOMS, EDGES), 0) % GROUP == of_lane[0:1], 1.0, 0.0).astype(BF16)
    sums = nt(jnp.concatenate(wide_rows, axis=0).astype(BF16), lane_atom)
    here = iota((CHUNKS, 128), 1) // GROUP == iota((CHUNKS, 128), 0)
    own_rows = []
    for number in range(3):
        both = sums[32 * number : 32 * number + 16] + sums[32 * number + 16 : 32 * number + 32]
        own_rows.append(jnp.sum(jnp.where(here, both, 0.0), axis=0, keepdims=True))

    upper = nbr >> 6
    left = []
    for g in range(CHUNKS):
        here = iota((8, EDGES), 0) == upper[g : g + 1]
        left.append(
            jnp.concatenate([jnp.where(here, v[g : g + 1], 0.0) for v in wide_rows], axis=0).astype(BF16)
        )
    both = nt(jnp.concatenate(left, axis=1), low_hot[...])
    coords = []
    for number in range(3):
        value = both[16 * number : 16 * number + 8] + both[16 * number + 8 : 16 * number + 16]
        coords.append(jnp.concatenate([value[k : k + 1] for k in range(8)], axis=1))
    total = jnp.concatenate(coords, axis=0)
    own_rows = jnp.concatenate(own_rows, axis=0)

    def six(value):
        high, low = split(value)
        return jnp.concatenate([high, low, jnp.zeros((2, value.shape[1]), F32)], axis=0).astype(BF16)

    def three(value):
        return value[0:3] + value[3:6]

    pad = jnp.zeros((5, 128), F32)
    for number, start in ((0, 256), (1, 384)):
        spread = three(nt(six(total[:, start : start + 128]), ohy[number]))
        p_out[number] = jnp.concatenate([spread[:, 0:128], pad], axis=0)
        p_piece[2 * number] = jnp.concatenate([spread[:, 128:256], pad], axis=0)
    p_piece[1] = jnp.concatenate([total[:, 128:256], pad], axis=0)

    def p_parts(side):
        dx, dy = side
        if dx == 0:
            return p_out.at[(1 + dy) // 2], p_own.at[(1 - dy) // 2]
        return p_piece.at[1 + dy], p_pin.at[1 - dy, (1 + dx) // 2]

    finish(exchange(3, p_parts))
    up = p_pin[0, 0] + p_pin[1, 0] + p_pin[2, 0]
    down = p_pin[0, 1] + p_pin[1, 1] + p_pin[2, 1]
    piece = jnp.where(iota((8, 128), 1) < 64, up, down)[0:3]
    result = total[:, 0:128] - own_rows + p_own[0][0:3] + p_own[1][0:3]
    result += three(nt(six(piece), ohx[...]))
    fo_ref[...] = -result


def place_outputs(energy_in, forces_in, energy_ref, forces_ref, sems):
    copies = [
        pltpu.make_async_copy(energy_in, energy_ref, sems.at[0]),
        pltpu.make_async_copy(forces_in, forces_ref, sems.at[1]),
    ]
    for copy in copies:
        copy.start()
    for copy in copies:
        copy.wait()


def body(remote, positions, species, neighbours, counts, send_x, send_y, embed, radial_w, update_w, out_w):
    kinds = embed.shape[0] * NB
    whole = (128, CHUNKS * EDGES)
    scratch = [
        pltpu.VMEM((2, 8, 128), F32),
        pltpu.VMEM((8, 128), F32),
        pltpu.VMEM((3, 8, 128), F32),
        pltpu.VMEM((3, 2, 8, 128), F32),
        pltpu.VMEM((3, 256, 128), BF16),
        pltpu.VMEM((128, 128), BF16),
        pltpu.VMEM((128, 128), BF16),
        pltpu.VMEM((3, 256, 128), BF16),
        pltpu.VMEM((2, 128, 128), BF16),
        pltpu.VMEM((3, 128, 128), BF16),
        pltpu.VMEM((2, 8, 128), F32),
        pltpu.VMEM((3, 8, 128), F32),
        pltpu.VMEM((2, 8, 128), F32),
        pltpu.VMEM((3, 2, 8, 128), F32),
        pltpu.VMEM((ATOMS, SLOTS), I32),
        pltpu.VMEM((CHUNKS, EDGES), I32),
        pltpu.VMEM((CHUNKS, EDGES), I32),
        pltpu.VMEM((6, CHUNKS, EDGES), F32),
        pltpu.VMEM((16, CHUNKS, EDGES), F32),
        pltpu.VMEM((EXT, CHUNKS * EDGES), BF16),
        pltpu.VMEM((64, CHUNKS * EDGES), BF16),
        pltpu.VMEM((CHUNKS, 160, EDGES), BF16),
        pltpu.VMEM((CHUNKS, 32, EDGES), BF16),
        pltpu.VMEM((CHUNKS, kinds, EDGES), BF16),
        pltpu.VMEM(whole, F32),
        pltpu.VMEM(whole, BF16),
        pltpu.VMEM(whole, BF16),
        pltpu.VMEM(whole, BF16),
        pltpu.VMEM((9, 128, kinds), F32),
        pltpu.VMEM((9, 128, 128), F32),
        pltpu.VMEM((9, 128, 128), F32),
        pltpu.VMEM((9, 128, 128), F32),
        pltpu.VMEM((128, 128), F32),
        pltpu.VMEM((128, 128), F32),
        pltpu.VMEM((CHUNKS, 8, EDGES), F32),
        pltpu.VMEM((CHUNKS, EDGES), F32),
        pltpu.VMEM((128, 128), BF16),
        pltpu.VMEM((128, 128), BF16),
        pltpu.VMEM((2, 256, 128), BF16),
        pltpu.VMEM((2, 128, 256), BF16),
        pltpu.SemaphoreType.DMA((10,)),
        pltpu.SemaphoreType.DMA((4, 8)),
        pltpu.SemaphoreType.DMA((4, 8)),
    ]
    inputs = (
        positions,
        species.reshape(1, ATOMS),
        neighbours.T,
        counts.reshape(1, ATOMS),
        send_x.reshape(2, 64),
        send_y.reshape(2, 128),
        embed,
        radial_w,
        update_w,
        out_w.reshape(1, WIDTH),
    )
    shapes = (
        jax.ShapeDtypeStruct((1, ATOMS), F32),
        jax.ShapeDtypeStruct((3, ATOMS), F32),
    )
    inputs = tuple(pltpu.with_memory_space_constraint(v, pltpu.HBM) for v in inputs)
    results = pl.pallas_call(
        functools.partial(kernel, remote),
        out_shape=shapes,
        in_specs=[pl.BlockSpec(memory_space=pltpu.HBM)] * len(inputs),
        out_specs=(pl.BlockSpec(memory_space=pltpu.VMEM), pl.BlockSpec(memory_space=pltpu.VMEM)),
        scratch_shapes=[pltpu.VMEM(v.shape, v.dtype) for v in inputs] + scratch,
        compiler_params=pltpu.CompilerParams(
            collective_id=0 if remote else None,
            has_side_effects=remote,
            vmem_limit_bytes=44 * 1024 * 1024,
        ),
    )(*inputs)
    anywhere = pl.BlockSpec(memory_space=pl.ANY)
    vmem = pl.BlockSpec(memory_space=pltpu.VMEM)
    energy, forces = pl.pallas_call(
        place_outputs,
        out_shape=shapes,
        in_specs=[vmem, vmem],
        out_specs=(anywhere, anywhere),
        scratch_shapes=[pltpu.SemaphoreType.DMA((2,))],
        compiler_params=pltpu.CompilerParams(vmem_limit_bytes=1024 * 1024),
    )(*results)
    return energy.reshape(ATOMS), forces


def solution(mesh):
    return jax.shard_map(
        functools.partial(body, True),
        mesh=mesh,
        in_specs=(
            P(None, ("gx", "gy")),
            P(("gx", "gy")),
            P(("gx", "gy"), None),
            P(("gx", "gy")),
            P(("gx", "gy"), None, None),
            P(("gx", "gy"), None, None),
            P(),
            P(),
            P(),
            P(),
        ),
        out_specs=(P(("gx", "gy")), P(None, ("gx", "gy"))),
        check_vma=False,
    )
```

```python
import functools
import math

import jax
import jax.numpy as jnp
from jax import lax
from jax.experimental import pallas as pl
from jax.experimental.pallas import tpu as pltpu
from jax.sharding import PartitionSpec as P

F32 = jnp.float32
BF16 = jnp.bfloat16
I32 = jnp.int32
MESH = pl.DeviceIdType.MESH

ATOMS = 128
SLOTS = 48
GROUP = 8
CHUNKS = ATOMS // GROUP
PAIRS = CHUNKS // 2
EDGES = GROUP * SLOTS
WIDTH = 128
EXT = 512
NB = 8
BOX = 8.0
SCALE = 0.25
SIDES = ((0, 1), (0, -1), (1, 1), (1, -1), (-1, 1), (-1, -1), (1, 0), (-1, 0))
R3, R5, R15 = math.sqrt(3.0), math.sqrt(5.0), math.sqrt(15.0)


def mm(a, b):
    return lax.dot_general(a, b, (((1,), (0,)), ((), ())), preferred_element_type=F32)


def nt(a, b):
    return lax.dot_general(a, b, (((1,), (1,)), ((), ())), preferred_element_type=F32)


def iota(shape, axis):
    return lax.broadcasted_iota(I32, shape, axis)


def split(value):
    high = value.astype(BF16).astype(F32)
    return high, value - high


def onehot(index, total):
    shape = (total, index.shape[1])
    return jnp.where(iota(shape, 0) == index, 1.0, 0.0).astype(BF16)


def lanes_take(row, index):
    return jnp.take_along_axis(jnp.broadcast_to(row, index.shape), index, axis=1)


def kernel(
    remote,
    *refs,
):
    inputs, en_ref, fo_ref, held, refs = refs[:10], refs[10], refs[11], refs[12:22], refs[22:]
    pos_ref, spc_ref, nbr_ref, cnt_ref, sx_ref, sy_ref, emb_ref, rw_ref, uw_ref, ow_ref = held
    (geo_out, geo_x, geo_in, geo_xin,
    h_sec, h_own, h_piece,
    g_sec, g_own, g_piece,
    p_out, p_piece, p_own, p_pin,
    nbr_t, nbr_d, spc_d, vec_d, harm_t, hot, low_hot, hmat, basis, phi, rad2, gat2, gms, rows_t,
    kinds_amps, amps1, amps2, gamps, z1_ref, gext, gharm, gdist, ohx, ohxt, ohy, ohyt,
    in_sem, send_sem, recv_sem) = refs
    loads = [
        pltpu.make_async_copy(src, dst, in_sem.at[number])
        for number, (src, dst) in enumerate(zip(inputs, held))
    ]
    if remote:
        nx, ny = lax.axis_size("gx"), lax.axis_size("gy")
        me_x, me_y = lax.axis_index("gx"), lax.axis_index("gy")

        xs = (me_x, lax.rem(me_x + 1, nx), lax.rem(me_x + nx - 1, nx))
        ys = (me_y, lax.rem(me_y + 1, ny), lax.rem(me_y + ny - 1, ny))

        def place(side):
            return (xs[side[0]], ys[side[1]])

        barrier = pltpu.get_barrier_semaphore()
        for side in SIDES:
            pl.semaphore_signal(barrier, inc=1, device_id=place(side), device_id_type=MESH)

    def exchange(phase, parts, only=None):
        copies = []
        for number, side in enumerate(SIDES):
            if only is not None and not only(side):
                continue
            src, dst = parts(side)
            if remote:
                copy = pltpu.make_async_remote_copy(
                    src_ref=src, dst_ref=dst,
                    send_sem=send_sem.at[phase, number], recv_sem=recv_sem.at[phase, number],
                    device_id=place(side), device_id_type=MESH,
                )
            else:
                copy = pltpu.make_async_copy(src, dst, recv_sem.at[phase, number])
            copy.start()
            copies.append(copy)
        return copies

    def finish(copies):
        for copy in copies:
            copy.wait()

    for number in (0, 1, 4, 5, 2, 3, 6, 7, 9, 8):
        loads[number].start()
    for number in (0, 1, 4, 5):
        loads[number].wait()

    sx = jnp.concatenate([sx_ref[0:1, :], sx_ref[1:2, :]], axis=1)
    sel = jnp.where(iota((ATOMS, 128), 0) == sx, 1.0, 0.0)
    ohx[...] = sel.astype(BF16)
    ohxt[...] = sel.T.astype(BF16)

    spc = spc_ref[...].astype(F32)
    pos = pos_ref[...].astype(F32)
    zero = jnp.zeros((1, 128), F32)
    geo = jnp.concatenate([pos, spc, zero, zero, zero, zero], axis=0)
    sy = sy_ref[...].astype(F32)
    geo_out[0] = jnp.concatenate([pos, spc, sy[1:2], zero, zero, zero], axis=0)
    geo_out[1] = jnp.concatenate([pos, spc, sy[0:1], zero, zero, zero], axis=0)
    geo_x[...] = mm(geo.astype(BF16), ohx[...])

    if remote:
        pl.semaphore_wait(barrier, len(SIDES))

    def geo_parts(side):
        dx, dy = side
        if dx == 0:
            return geo_out.at[(1 + dy) // 2], geo_in.at[1 - dy]
        return geo_x, geo_xin.at[1 - dy, (1 - dx) // 2]

    copies = exchange(0, geo_parts)

    loads[2].wait()
    nbr_t[...] = nbr_ref[...].T
    nbr_d[...] = jnp.concatenate(
        [nbr_t[pl.ds(a, CHUNKS, stride=GROUP), :] for a in range(GROUP)], axis=1
    )

    def lanes(g, count=1):
        return pl.ds(pl.multiple_of(g * (count * EDGES), 128), count * EDGES)

    def build(g, carry):
        index = jnp.broadcast_to(nbr_d[pl.ds(g, 1), :], (16, EDGES)).astype(jnp.int16)
        one, none = jnp.ones((16, EDGES), BF16), jnp.zeros((16, EDGES), BF16)
        first_rows = iota((16, EDGES), 0).astype(jnp.int16)
        for block in range(EXT // 16):
            hot[16 * block : 16 * block + 16, lanes(g)] = jnp.where(
                index - jnp.int16(16 * block) == first_rows, one, none
            )
        lower = index & jnp.int16(63)
        for block in range(4):
            low_hot[16 * block : 16 * block + 16, lanes(g)] = jnp.where(
                lower - jnp.int16(16 * block) == first_rows, one, none
            )
        return carry

    lax.fori_loop(0, CHUNKS, build, 0, unroll=8)

    lane = iota((CHUNKS, EDGES), 1)
    of_lane = jnp.zeros((CHUNKS, EDGES), I32)
    for a in range(1, GROUP):
        of_lane += (lane >= a * SLOTS).astype(I32)
    slot = lane - of_lane * SLOTS
    atom = iota((CHUNKS, EDGES), 0) * GROUP + of_lane
    mask = of_lane[:GROUP] == iota((GROUP, EDGES), 0)

    for number in (3, 6, 7, 9):
        loads[number].wait()
    high, low = split(rw_ref[1])
    w_t = jnp.concatenate([high, high, low, jnp.zeros_like(high)], axis=0).T.astype(BF16)
    w_rows = jnp.concatenate([high, low], axis=0).astype(BF16)
    embed = emb_ref[...].astype(F32)
    species = embed.shape[0]
    kind_w = jnp.concatenate([rw_ref[0] * embed[k : k + 1] for k in range(species)], axis=0)
    kind_high, kind_low = (v.astype(BF16) for v in split(kind_w))

    finish(copies)

    def section(j):
        own = geo if j == 0 else geo_in[1 + j]
        keep = iota((8, 128), 1) < 64
        row = iota((8, 128), 0)
        got = jnp.where(keep, geo_xin[1 + j, 0], geo_xin[1 + j, 1])
        got += jnp.where(row == 0, jnp.where(keep, -BOX, BOX), 0.0)
        return own, got

    row = iota((8, 128), 0)
    blocks = list(section(0))
    for number, j in enumerate((-1, 1)):
        own, got = section(j)
        index = own[4:5].astype(I32)
        chosen = jnp.where(iota((256, 128), 0) == index, 1.0, 0.0)
        ohy[number] = chosen.astype(BF16)
        ohyt[number] = chosen.T.astype(BF16)
        whole = jnp.concatenate([own, got], axis=1)
        whole = jnp.where(iota((8, 256), 0) < 4, whole, 0.0)
        picked = mm(whole.astype(BF16), ohy[number])
        blocks.append(picked + jnp.where(row == 1, BOX * j, 0.0))

    packed = []
    for block in blocks:
        x = ((block[0:1] + BOX) * 16.0).astype(I32)
        y = ((block[1:2] + BOX) * 16.0).astype(I32)
        zc = (block[2:3] * 16.0).astype(I32)
        packed.append(x + y * 512 + zc * 262144 + block[3:4].astype(I32) * 33554432)

    nbr = nbr_d[...]
    near = nbr & 127
    which = nbr >> 7
    far, mine, live = [], [], []
    for t in range(EDGES // 128):
        cut = slice(t * 128, (t + 1) * 128)
        value = lanes_take(packed[0], near[:, cut])
        for b in range(1, 4):
            value = jnp.where(which[:, cut] == b, lanes_take(packed[b], near[:, cut]), value)
        far.append(value)
        mine.append(lanes_take(packed[0], atom[:, cut]))
        live.append(lanes_take(cnt_ref[...], atom[:, cut]))
    far = jnp.concatenate(far, axis=1)
    mine = jnp.concatenate(mine, axis=1)
    live = jnp.where(slot < jnp.concatenate(live, axis=1), 1.0, 0.0)

    def coordinates(value):
        return value & 511, (value >> 9) & 511, (value >> 18) & 127

    rel = [
        (p - q).astype(F32) * (1.0 / 16.0)
        for p, q in zip(coordinates(far), coordinates(mine))
    ]
    square = rel[0] * rel[0] + rel[1] * rel[1] + rel[2] * rel[2] + 1.0
    dist = jnp.sqrt(square)
    inverse = 1.0 / dist
    ux, uy, uz = (r * inverse for r in rel)
    spc_d[...] = far >> 25
    for number, value in enumerate((dist, live, inverse, ux, uy, uz)):
        vec_d[number] = value
    harm = (
        R3 * ux, R3 * uy, R3 * uz, R15 * ux * uy, R15 * uy * uz,
        0.5 * R5 * (3.0 * uz * uz - 1.0), R15 * ux * uz, 0.5 * R15 * (ux * ux - uy * uy),
    )
    for number, value in enumerate(harm):
        harm_t[number], harm_t[8 + number] = split(SCALE * value)

    def radial_basis(g):
        centers = 1.0 + 2.0 * iota((NB, EDGES), 0).astype(F32)
        away = vec_d[0, pl.ds(g, 1), :] - centers
        return away, jnp.exp(-0.125 * away * away) * vec_d[1, pl.ds(g, 1), :]

    def sums_of(g, high, low):
        fill = jnp.zeros((128 - high.shape[0], EDGES), BF16)
        right = [high, low] if high.shape[0] == 128 else [high, fill, low]
        both = nt(hmat[g], jnp.concatenate(right, axis=0))
        n = high.shape[0]
        return both[:80, :n] + both[:80, 128 : 128 + n] + both[80:, :n]

    def store_sums(ref, g, sums):
        at = pl.ds(pl.multiple_of(g * GROUP, GROUP), GROUP)
        for m in range(9):
            ref[m, at, :] = sums[m * GROUP : (m + 1) * GROUP]

    def first(g, carry):
        none = jnp.zeros((GROUP, EDGES), F32)
        rows = [jnp.where(mask, SCALE, 0.0)]
        fine = [none]
        for m in range(8):
            rows.append(jnp.where(mask, harm_t[m, pl.ds(g, 1), :], 0.0))
            fine.append(jnp.where(mask, harm_t[8 + m, pl.ds(g, 1), :], 0.0))
        hmat[g, 0:80] = jnp.concatenate(rows + [none], axis=0).astype(BF16)
        hmat[g, 80:160] = jnp.concatenate(fine + [none], axis=0).astype(BF16)
        high, low = split(radial_basis(g)[1])
        basis[g] = jnp.concatenate([high, low, high, none], axis=0).astype(BF16)
        kind = jnp.broadcast_to(spc_d[pl.ds(g, 1), :], (16, EDGES)).astype(jnp.int16)
        kind -= (iota((16, EDGES), 0) >= 8).astype(jnp.int16)
        high, low = (jnp.concatenate([v, v], axis=0).astype(BF16) for v in (high, low))
        none = jnp.zeros((16, EDGES), BF16)
        phi_low = []
        for pair in range(species // 2):
            here = kind == jnp.int16(2 * pair)
            phi[g, 16 * pair : 16 * pair + 16] = jnp.where(here, high, none)
            phi_low.append(jnp.where(here, low, none))
        phi_low = jnp.concatenate(phi_low, axis=0)
        store_sums(kinds_amps, g, sums_of(g, phi[g], phi_low))
        return carry

    lax.fori_loop(0, CHUNKS, first, 0, unroll=16)
    for m in range(9):
        high, low = (v.astype(BF16) for v in split(kinds_amps[m]))
        amps1[m] = mm(high, kind_high) + mm(low, kind_high) + mm(high, kind_low)
    loads[8].wait()

    def update(amps, old, t):
        one = amps[1] * amps[1] + amps[2] * amps[2] + amps[3] * amps[3]
        two = amps[4] * amps[4] + amps[5] * amps[5] + amps[6] * amps[6]
        two += amps[7] * amps[7] + amps[8] * amps[8]
        flat = jnp.concatenate([amps[0], one, two], axis=1).astype(BF16)
        z = mm(flat, uw_ref[t])
        return z, (old + z * jax.nn.sigmoid(z)).astype(BF16)

    def slope(z):
        sig = jax.nn.sigmoid(z)
        return sig * (1.0 + z * (1.0 - sig))

    def back(amps, steep, grad, t):
        grad_z = grad * steep
        grad_inv = nt(grad_z.astype(BF16), uw_ref[t])
        gamps[0] = grad_inv[:, :128]
        for m in range(1, 9):
            part = grad_inv[:, 128:256] if m < 4 else grad_inv[:, 256:]
            gamps[m] = 2.0 * amps[m] * part

    kinds_own = onehot(spc_ref[...], 16).astype(F32).T.astype(BF16)
    h0_own = mm(
        kinds_own, jnp.concatenate([embed, jnp.zeros((16 - species, 128), F32)], axis=0).astype(BF16)
    )
    z1, h1 = update(amps1, h0_own, 0)
    h_sec[1, 0:128] = h1
    h_own[...] = h1

    def h_parts(side):
        dx, dy = side
        if dx == 0:
            return h_own, h_sec.at[1 - dy, pl.ds(0, 128)]
        if dx == 1:
            return h_piece.at[pl.ds(0, 64)], h_sec.at[1 - dy, pl.ds(128, 64)]
        return h_piece.at[pl.ds(64, 64)], h_sec.at[1 - dy, pl.ds(192, 64)]

    copies = exchange(1, h_parts, lambda side: side[0] == 0)
    h_piece[...] = mm(ohxt[...], h1).astype(BF16)
    copies += exchange(1, h_parts, lambda side: side[0] != 0 and side[1] != 0)
    near = exchange(1, h_parts, lambda side: side[1] == 0)
    z1_ref[...] = slope(z1)

    def second_radial(g, carry):
        rad2[:, lanes(g)] = mm(w_t, basis[g])
        return carry

    lax.fori_loop(0, CHUNKS, second_radial, 0, unroll=8)
    own_t = h1.astype(F32).T
    finish(near)

    got_t = h_sec[1, 128:256].astype(F32).T
    near_t = jnp.concatenate([own_t, got_t], axis=1).astype(BF16)

    def first_section(p, carry):
        gat2[:, lanes(p, 2)] = mm(near_t, hot[0:256, lanes(p, 2)]).astype(BF16)
        return carry

    lax.fori_loop(0, PAIRS, first_section, 0, unroll=4)
    finish(copies)
    low_t = mm(ohyt[0], h_sec[0]).T
    high_t = mm(ohyt[1], h_sec[2]).T
    far_t = jnp.concatenate([low_t, high_t], axis=1).astype(BF16)

    def gather(p):
        gat2[:, lanes(p, 2)] += mm(far_t, hot[256:512, lanes(p, 2)]).astype(BF16)

    def second(p, last):
        if not last:
            gather(p + 1)
        for half in range(2):
            g = 2 * p + half
            high, low = (
                v.astype(BF16) for v in split(gat2[:, lanes(g)].astype(F32) * rad2[:, lanes(g)])
            )
            store_sums(amps2, g, sums_of(g, high, low))

    gather(0)
    for p in range(PAIRS):
        second(p, p == PAIRS - 1)
    z2, h2 = update(amps2, h1.astype(F32), 1)
    out_w = ow_ref[...]
    back(amps2, slope(z2), out_w, 1)

    def chunk_rows(ref, g):
        at = pl.ds(pl.multiple_of(g * GROUP, GROUP), GROUP)
        rows = [ref[m, at, :] for m in range(9)]
        return jnp.concatenate(rows + [jnp.zeros_like(rows[0])], axis=0)

    def features(p):
        for g in (2 * p, 2 * p + 1):
            grad = mm(chunk_rows(gamps, g).T.astype(BF16), hmat[g, 0:80])
            gms[:, lanes(g)] = grad.astype(BF16)
            rows_t[:, lanes(g)] = (grad * rad2[:, lanes(g)]).astype(BF16)

    features(0)
    far_rows = jnp.zeros((256, 128), F32)
    for p in range(PAIRS):
        if p + 1 < PAIRS:
            features(p + 1)
        far_rows += nt(hot[256:512, lanes(p, 2)], rows_t[:, lanes(p, 2)])
    far_rows = far_rows.astype(BF16)
    for number in range(2):
        g_sec[2 * number] = mm(ohy[number], far_rows[128 * number : 128 * number + 128]).astype(BF16)

    def g_parts(side):
        dx, dy = side
        if dx == 0:
            return g_sec.at[1 + dy, pl.ds(0, 128)], g_own.at[(1 - dy) // 2]
        if dx == -1:
            return g_sec.at[1 + dy, pl.ds(128, 64)], g_piece.at[1 - dy, pl.ds(0, 64)]
        return g_sec.at[1 + dy, pl.ds(192, 64)], g_piece.at[1 - dy, pl.ds(64, 64)]

    copies = exchange(2, g_parts, lambda side: side[1] != 0)
    near_rows = nt(hot[0:256], rows_t[...])
    g_sec[1, 128:256] = near_rows[128:256].astype(BF16)
    copies += exchange(2, g_parts, lambda side: side[1] == 0)
    gext[...] = near_rows[0:128]

    high, rest = split(out_w)
    mid, low = split(rest)
    readout = jnp.concatenate([high, mid, low, jnp.zeros((5, 128), F32)], axis=0).astype(BF16)
    parts = nt(readout, h2)
    en_ref[...] = parts[0:1] + parts[1:2] + parts[2:3]

    def harmonic_rows(wide):
        which = of_lane[:GROUP]
        result = jnp.zeros((8, EDGES), F32)
        for m in range(8):
            part = wide[(m + 1) * GROUP : (m + 2) * GROUP]
            part = jnp.concatenate(
                [
                    jnp.take_along_axis(part[:, t : t + 128], which[:, t : t + 128], axis=0)
                    for t in range(0, EDGES, 128)
                ],
                axis=1,
            )
            result = jnp.where(iota((8, EDGES), 0) == m, part, result)
        return result

    def distance_row(g, by_basis):
        away, value = radial_basis(g)
        return jnp.sum(by_basis * (-0.25 * away * value), axis=0, keepdims=True)

    def geometry_two(g, carry):
        gathered = gat2[:, lanes(g)].astype(F32)
        message = (gathered * rad2[:, lanes(g)]).astype(BF16)
        gharm[g] = harmonic_rows(mm(chunk_rows(gamps, g).astype(BF16), message))
        two = mm(w_rows, (gms[:, lanes(g)].astype(F32) * gathered).astype(BF16))
        gdist[pl.ds(g, 1), :] = distance_row(g, two[0:NB] + two[NB:])
        return carry

    lax.fori_loop(0, CHUNKS, geometry_two, 0, unroll=8)
    finish(copies)

    grad_h1 = gext[...] + out_w + g_own[0].astype(F32) + g_own[1].astype(F32)
    piece = g_piece[0].astype(F32) + g_piece[1].astype(F32) + g_piece[2].astype(F32)
    grad_h1 += mm(ohx[...], piece.astype(BF16))
    back(amps1, z1_ref[...], grad_h1, 0)

    for m in range(9):
        kinds_amps[m] = nt(gamps[m].astype(BF16), kind_high)

    def geometry_one(g, carry):
        grads = chunk_rows(kinds_amps, g)
        gharm[g] += harmonic_rows(mm(grads.astype(BF16), phi[g]))
        by_kind = mm(grads.T.astype(BF16), hmat[g, 0:80])
        kind = jnp.broadcast_to(spc_d[pl.ds(g, 1), :], (NB, EDGES))
        blocks = [by_kind[k * NB : (k + 1) * NB] for k in range(species)]
        bit = 1
        while len(blocks) > 1:
            odd = (kind & bit) != 0
            blocks = [
                jnp.where(odd, blocks[k + 1], blocks[k]) if k + 1 < len(blocks) else blocks[k]
                for k in range(0, len(blocks), 2)
            ]
            bit *= 2
        by_basis = blocks[0]
        gdist[pl.ds(g, 1), :] += distance_row(g, by_basis)
        return carry

    lax.fori_loop(0, CHUNKS, geometry_one, 0, unroll=16)

    inv, vx, vy, vz = (vec_d[n] for n in range(2, 6))
    g1, g2, g3, g4, g5, g6, g7, g8 = (SCALE * gharm[:, n, :] for n in range(8))
    gx = R3 * g1 + R15 * (vy * g4 + vz * g7 + vx * g8)
    gy = R3 * g2 + R15 * (vx * g4 + vz * g5 - vy * g8)
    gz = R3 * g3 + R15 * (vy * g5 + vx * g7) + 3.0 * R5 * vz * g6
    along = gdist[...] - inv * (gx * vx + gy * vy + gz * vz)
    wide_rows = []
    for grad, unit in ((gx, vx), (gy, vy), (gz, vz)):
        wide_rows += split(grad * inv + unit * along)

    lane_atom = jnp.where(iota((ATOMS, EDGES), 0) % GROUP == of_lane[0:1], 1.0, 0.0).astype(BF16)
    sums = nt(jnp.concatenate(wide_rows, axis=0).astype(BF16), lane_atom)
    here = iota((CHUNKS, 128), 1) // GROUP == iota((CHUNKS, 128), 0)
    own_rows = []
    for number in range(3):
        both = sums[32 * number : 32 * number + 16] + sums[32 * number + 16 : 32 * number + 32]
        own_rows.append(jnp.sum(jnp.where(here, both, 0.0), axis=0, keepdims=True))

    upper = nbr >> 6
    left = []
    for g in range(CHUNKS):
        here = iota((8, EDGES), 0) == upper[g : g + 1]
        left.append(
            jnp.concatenate([jnp.where(here, v[g : g + 1], 0.0) for v in wide_rows], axis=0).astype(BF16)
        )
    both = nt(jnp.concatenate(left, axis=1), low_hot[...])
    coords = []
    for number in range(3):
        value = both[16 * number : 16 * number + 8] + both[16 * number + 8 : 16 * number + 16]
        coords.append(jnp.concatenate([value[k : k + 1] for k in range(8)], axis=1))
    total = jnp.concatenate(coords, axis=0)
    own_rows = jnp.concatenate(own_rows, axis=0)

    def six(value):
        high, low = split(value)
        return jnp.concatenate([high, low, jnp.zeros((2, value.shape[1]), F32)], axis=0).astype(BF16)

    def three(value):
        return value[0:3] + value[3:6]

    pad = jnp.zeros((5, 128), F32)
    for number, start in ((0, 256), (1, 384)):
        spread = three(nt(six(total[:, start : start + 128]), ohy[number]))
        p_out[number] = jnp.concatenate([spread[:, 0:128], pad], axis=0)
        p_piece[2 * number] = jnp.concatenate([spread[:, 128:256], pad], axis=0)
    p_piece[1] = jnp.concatenate([total[:, 128:256], pad], axis=0)

    def p_parts(side):
        dx, dy = side
        if dx == 0:
            return p_out.at[(1 + dy) // 2], p_own.at[(1 - dy) // 2]
        return p_piece.at[1 + dy], p_pin.at[1 - dy, (1 + dx) // 2]

    finish(exchange(3, p_parts))
    up = p_pin[0, 0] + p_pin[1, 0] + p_pin[2, 0]
    down = p_pin[0, 1] + p_pin[1, 1] + p_pin[2, 1]
    piece = jnp.where(iota((8, 128), 1) < 64, up, down)[0:3]
    result = total[:, 0:128] - own_rows + p_own[0][0:3] + p_own[1][0:3]
    result += three(nt(six(piece), ohx[...]))
    fo_ref[...] = -result


def place_outputs(energy_in, forces_in, energy_ref, forces_ref, sems):
    copies = [
        pltpu.make_async_copy(energy_in, energy_ref, sems.at[0]),
        pltpu.make_async_copy(forces_in, forces_ref, sems.at[1]),
    ]
    for copy in copies:
        copy.start()
    for copy in copies:
        copy.wait()


def body(remote, positions, species, neighbours, counts, send_x, send_y, embed, radial_w, update_w, out_w):
    kinds = embed.shape[0] * NB
    whole = (128, CHUNKS * EDGES)
    scratch = [
        pltpu.VMEM((2, 8, 128), F32),
        pltpu.VMEM((8, 128), F32),
        pltpu.VMEM((3, 8, 128), F32),
        pltpu.VMEM((3, 2, 8, 128), F32),
        pltpu.VMEM((3, 256, 128), BF16),
        pltpu.VMEM((128, 128), BF16),
        pltpu.VMEM((128, 128), BF16),
        pltpu.VMEM((3, 256, 128), BF16),
        pltpu.VMEM((2, 128, 128), BF16),
        pltpu.VMEM((3, 128, 128), BF16),
        pltpu.VMEM((2, 8, 128), F32),
        pltpu.VMEM((3, 8, 128), F32),
        pltpu.VMEM((2, 8, 128), F32),
        pltpu.VMEM((3, 2, 8, 128), F32),
        pltpu.VMEM((ATOMS, SLOTS), I32),
        pltpu.VMEM((CHUNKS, EDGES), I32),
        pltpu.VMEM((CHUNKS, EDGES), I32),
        pltpu.VMEM((6, CHUNKS, EDGES), F32),
        pltpu.VMEM((16, CHUNKS, EDGES), F32),
        pltpu.VMEM((EXT, CHUNKS * EDGES), BF16),
        pltpu.VMEM((64, CHUNKS * EDGES), BF16),
        pltpu.VMEM((CHUNKS, 160, EDGES), BF16),
        pltpu.VMEM((CHUNKS, 32, EDGES), BF16),
        pltpu.VMEM((CHUNKS, kinds, EDGES), BF16),
        pltpu.VMEM(whole, F32),
        pltpu.VMEM(whole, BF16),
        pltpu.VMEM(whole, BF16),
        pltpu.VMEM(whole, BF16),
        pltpu.VMEM((9, 128, kinds), F32),
        pltpu.VMEM((9, 128, 128), F32),
        pltpu.VMEM((9, 128, 128), F32),
        pltpu.VMEM((9, 128, 128), F32),
        pltpu.VMEM((128, 128), F32),
        pltpu.VMEM((128, 128), F32),
        pltpu.VMEM((CHUNKS, 8, EDGES), F32),
        pltpu.VMEM((CHUNKS, EDGES), F32),
        pltpu.VMEM((128, 128), BF16),
        pltpu.VMEM((128, 128), BF16),
        pltpu.VMEM((2, 256, 128), BF16),
        pltpu.VMEM((2, 128, 256), BF16),
        pltpu.SemaphoreType.DMA((10,)),
        pltpu.SemaphoreType.DMA((4, 8)),
        pltpu.SemaphoreType.DMA((4, 8)),
    ]
    inputs = (
        positions,
        species.reshape(1, ATOMS),
        neighbours.T,
        counts.reshape(1, ATOMS),
        send_x.reshape(2, 64),
        send_y.reshape(2, 128),
        embed,
        radial_w,
        update_w,
        out_w.reshape(1, WIDTH),
    )
    shapes = (
        jax.ShapeDtypeStruct((1, ATOMS), F32),
        jax.ShapeDtypeStruct((3, ATOMS), F32),
    )
    inputs = tuple(pltpu.with_memory_space_constraint(v, pltpu.HBM) for v in inputs)
    results = pl.pallas_call(
        functools.partial(kernel, remote),
        out_shape=shapes,
        in_specs=[pl.BlockSpec(memory_space=pltpu.HBM)] * len(inputs),
        out_specs=(pl.BlockSpec(memory_space=pltpu.VMEM), pl.BlockSpec(memory_space=pltpu.VMEM)),
        scratch_shapes=[pltpu.VMEM(v.shape, v.dtype) for v in inputs] + scratch,
        compiler_params=pltpu.CompilerParams(
            collective_id=0 if remote else None,
            has_side_effects=remote,
            vmem_limit_bytes=44 * 1024 * 1024,
        ),
    )(*inputs)
    anywhere = pl.BlockSpec(memory_space=pl.ANY)
    vmem = pl.BlockSpec(memory_space=pltpu.VMEM)
    energy, forces = pl.pallas_call(
        place_outputs,
        out_shape=shapes,
        in_specs=[vmem, vmem],
        out_specs=(anywhere, anywhere),
        scratch_shapes=[pltpu.SemaphoreType.DMA((2,))],
        compiler_params=pltpu.CompilerParams(vmem_limit_bytes=1024 * 1024),
    )(*results)
    return energy.reshape(ATOMS), forces


def solution(mesh):
    return jax.shard_map(
        functools.partial(body, True),
        mesh=mesh,
        in_specs=(
            P(None, ("gx", "gy")),
            P(("gx", "gy")),
            P(("gx", "gy"), None),
            P(("gx", "gy")),
            P(("gx", "gy"), None, None),
            P(("gx", "gy"), None, None),
            P(),
            P(),
            P(),
            P(),
        ),
        out_specs=(P(("gx", "gy")), P(None, ("gx", "gy"))),
        check_vma=False,
    )
```

```python
import functools
import math

import jax
import jax.numpy as jnp
from jax import lax
from jax.experimental import pallas as pl
from jax.experimental.pallas import tpu as pltpu
from jax.sharding import PartitionSpec as P

F32 = jnp.float32
BF16 = jnp.bfloat16
I32 = jnp.int32
MESH = pl.DeviceIdType.MESH

ATOMS = 128
SLOTS = 48
GROUP = 8
CHUNKS = ATOMS // GROUP
PAIRS = CHUNKS // 2
EDGES = GROUP * SLOTS
WIDTH = 128
EXT = 512
NB = 8
BOX = 8.0
SCALE = 0.25
SIDES = ((0, 1), (0, -1), (1, 1), (1, -1), (-1, 1), (-1, -1), (1, 0), (-1, 0))
R3, R5, R15 = math.sqrt(3.0), math.sqrt(5.0), math.sqrt(15.0)


def mm(a, b):
    return lax.dot_general(a, b, (((1,), (0,)), ((), ())), preferred_element_type=F32)


def nt(a, b):
    return lax.dot_general(a, b, (((1,), (1,)), ((), ())), preferred_element_type=F32)


def iota(shape, axis):
    return lax.broadcasted_iota(I32, shape, axis)


def split(value):
    high = value.astype(BF16).astype(F32)
    return high, value - high


def onehot(index, total):
    shape = (total, index.shape[1])
    return jnp.where(iota(shape, 0) == index, 1.0, 0.0).astype(BF16)


def lanes_take(row, index):
    return jnp.take_along_axis(jnp.broadcast_to(row, index.shape), index, axis=1)


def kernel(
    remote,
    *refs,
):
    inputs, en_ref, fo_ref, held, refs = refs[:10], refs[10], refs[11], refs[12:22], refs[22:]
    pos_ref, spc_ref, nbr_ref, cnt_ref, sx_ref, sy_ref, emb_ref, rw_ref, uw_ref, ow_ref = held
    (geo_out, geo_x, geo_in, geo_xin,
    h_sec, h_own, h_piece,
    g_sec, g_own, g_piece,
    p_out, p_piece, p_own, p_pin,
    nbr_t, nbr_d, spc_d, vec_d, harm_t, hot, low_hot, hmat, basis, phi, rad2, gat2, gms, rows_t,
    kinds_amps, amps1, amps2, gamps, z1_ref, gext, gharm, gdist, ohx, ohxt, ohy, ohyt,
    in_sem, send_sem, recv_sem) = refs
    loads = [
        pltpu.make_async_copy(src, dst, in_sem.at[number])
        for number, (src, dst) in enumerate(zip(inputs, held))
    ]
    if remote:
        nx, ny = lax.axis_size("gx"), lax.axis_size("gy")
        me_x, me_y = lax.axis_index("gx"), lax.axis_index("gy")

        xs = (me_x, lax.rem(me_x + 1, nx), lax.rem(me_x + nx - 1, nx))
        ys = (me_y, lax.rem(me_y + 1, ny), lax.rem(me_y + ny - 1, ny))

        def place(side):
            return (xs[side[0]], ys[side[1]])

        barrier = pltpu.get_barrier_semaphore()
        for side in SIDES:
            pl.semaphore_signal(barrier, inc=1, device_id=place(side), device_id_type=MESH)

    def exchange(phase, parts, only=None):
        copies = []
        for number, side in enumerate(SIDES):
            if only is not None and not only(side):
                continue
            src, dst = parts(side)
            if remote:
                copy = pltpu.make_async_remote_copy(
                    src_ref=src, dst_ref=dst,
                    send_sem=send_sem.at[phase, number], recv_sem=recv_sem.at[phase, number],
                    device_id=place(side), device_id_type=MESH,
                )
            else:
                copy = pltpu.make_async_copy(src, dst, recv_sem.at[phase, number])
            copy.start()
            copies.append(copy)
        return copies

    def finish(copies):
        for copy in copies:
            copy.wait()

    for number in (0, 1, 4, 5, 2, 3, 6, 7, 9, 8):
        loads[number].start()
    for number in (0, 1, 4, 5):
        loads[number].wait()

    sx = jnp.concatenate([sx_ref[0:1, :], sx_ref[1:2, :]], axis=1)
    sel = jnp.where(iota((ATOMS, 128), 0) == sx, 1.0, 0.0)
    ohx[...] = sel.astype(BF16)
    ohxt[...] = sel.T.astype(BF16)

    spc = spc_ref[...].astype(F32)
    pos = pos_ref[...].astype(F32)
    zero = jnp.zeros((1, 128), F32)
    geo = jnp.concatenate([pos, spc, zero, zero, zero, zero], axis=0)
    sy = sy_ref[...].astype(F32)
    geo_out[0] = jnp.concatenate([pos, spc, sy[1:2], zero, zero, zero], axis=0)
    geo_out[1] = jnp.concatenate([pos, spc, sy[0:1], zero, zero, zero], axis=0)
    geo_x[...] = mm(geo.astype(BF16), ohx[...])

    if remote:
        pl.semaphore_wait(barrier, len(SIDES))

    def geo_parts(side):
        dx, dy = side
        if dx == 0:
            return geo_out.at[(1 + dy) // 2], geo_in.at[1 - dy]
        return geo_x, geo_xin.at[1 - dy, (1 - dx) // 2]

    copies = exchange(0, geo_parts)

    loads[2].wait()
    nbr_t[...] = nbr_ref[...].T
    nbr_d[...] = jnp.concatenate(
        [nbr_t[pl.ds(a, CHUNKS, stride=GROUP), :] for a in range(GROUP)], axis=1
    )

    def lanes(g, count=1):
        return pl.ds(pl.multiple_of(g * (count * EDGES), 128), count * EDGES)

    def build(g, carry):
        index = jnp.broadcast_to(nbr_d[pl.ds(g, 1), :], (16, EDGES)).astype(jnp.int16)
        one, none = jnp.ones((16, EDGES), BF16), jnp.zeros((16, EDGES), BF16)
        first_rows = iota((16, EDGES), 0).astype(jnp.int16)
        for block in range(EXT // 16):
            hot[16 * block : 16 * block + 16, lanes(g)] = jnp.where(
                index - jnp.int16(16 * block) == first_rows, one, none
            )
        lower = index & jnp.int16(63)
        for block in range(4):
            low_hot[16 * block : 16 * block + 16, lanes(g)] = jnp.where(
                lower - jnp.int16(16 * block) == first_rows, one, none
            )
        return carry

    lax.fori_loop(0, CHUNKS, build, 0, unroll=8)

    lane = iota((CHUNKS, EDGES), 1)
    of_lane = jnp.zeros((CHUNKS, EDGES), I32)
    for a in range(1, GROUP):
        of_lane += (lane >= a * SLOTS).astype(I32)
    slot = lane - of_lane * SLOTS
    atom = iota((CHUNKS, EDGES), 0) * GROUP + of_lane
    mask = of_lane[:GROUP] == iota((GROUP, EDGES), 0)

    for number in (3, 6, 7, 9):
        loads[number].wait()
    high, low = split(rw_ref[1])
    w_t = jnp.concatenate([high, high, low, jnp.zeros_like(high)], axis=0).T.astype(BF16)
    w_rows = jnp.concatenate([high, low], axis=0).astype(BF16)
    embed = emb_ref[...].astype(F32)
    species = embed.shape[0]
    kind_w = jnp.concatenate([rw_ref[0] * embed[k : k + 1] for k in range(species)], axis=0)
    kind_high, kind_low = (v.astype(BF16) for v in split(kind_w))

    finish(copies)

    def section(j):
        own = geo if j == 0 else geo_in[1 + j]
        keep = iota((8, 128), 1) < 64
        row = iota((8, 128), 0)
        got = jnp.where(keep, geo_xin[1 + j, 0], geo_xin[1 + j, 1])
        got += jnp.where(row == 0, jnp.where(keep, -BOX, BOX), 0.0)
        return own, got

    row = iota((8, 128), 0)
    blocks = list(section(0))
    for number, j in enumerate((-1, 1)):
        own, got = section(j)
        index = own[4:5].astype(I32)
        chosen = jnp.where(iota((256, 128), 0) == index, 1.0, 0.0)
        ohy[number] = chosen.astype(BF16)
        ohyt[number] = chosen.T.astype(BF16)
        whole = jnp.concatenate([own, got], axis=1)
        whole = jnp.where(iota((8, 256), 0) < 4, whole, 0.0)
        picked = mm(whole.astype(BF16), ohy[number])
        blocks.append(picked + jnp.where(row == 1, BOX * j, 0.0))

    packed = []
    for block in blocks:
        x = ((block[0:1] + BOX) * 16.0).astype(I32)
        y = ((block[1:2] + BOX) * 16.0).astype(I32)
        zc = (block[2:3] * 16.0).astype(I32)
        packed.append(x + y * 512 + zc * 262144 + block[3:4].astype(I32) * 33554432)

    nbr = nbr_d[...]
    near = nbr & 127
    which = nbr >> 7
    far, mine, live = [], [], []
    for t in range(EDGES // 128):
        cut = slice(t * 128, (t + 1) * 128)
        value = lanes_take(packed[0], near[:, cut])
        for b in range(1, 4):
            value = jnp.where(which[:, cut] == b, lanes_take(packed[b], near[:, cut]), value)
        far.append(value)
        mine.append(lanes_take(packed[0], atom[:, cut]))
        live.append(lanes_take(cnt_ref[...], atom[:, cut]))
    far = jnp.concatenate(far, axis=1)
    mine = jnp.concatenate(mine, axis=1)
    live = jnp.where(slot < jnp.concatenate(live, axis=1), 1.0, 0.0)

    def coordinates(value):
        return value & 511, (value >> 9) & 511, (value >> 18) & 127

    rel = [
        (p - q).astype(F32) * (1.0 / 16.0)
        for p, q in zip(coordinates(far), coordinates(mine))
    ]
    square = rel[0] * rel[0] + rel[1] * rel[1] + rel[2] * rel[2] + 1.0
    dist = jnp.sqrt(square)
    inverse = 1.0 / dist
    ux, uy, uz = (r * inverse for r in rel)
    spc_d[...] = far >> 25
    for number, value in enumerate((dist, live, inverse, ux, uy, uz)):
        vec_d[number] = value
    harm = (
        R3 * ux, R3 * uy, R3 * uz, R15 * ux * uy, R15 * uy * uz,
        0.5 * R5 * (3.0 * uz * uz - 1.0), R15 * ux * uz, 0.5 * R15 * (ux * ux - uy * uy),
    )
    for number, value in enumerate(harm):
        harm_t[number], harm_t[8 + number] = split(SCALE * value)

    def radial_basis(g):
        centers = 1.0 + 2.0 * iota((NB, EDGES), 0).astype(F32)
        away = vec_d[0, pl.ds(g, 1), :] - centers
        return away, jnp.exp(-0.125 * away * away) * vec_d[1, pl.ds(g, 1), :]

    def sums_of(g, high, low):
        fill = jnp.zeros((128 - high.shape[0], EDGES), BF16)
        right = [high, low] if high.shape[0] == 128 else [high, fill, low]
        both = nt(hmat[g], jnp.concatenate(right, axis=0))
        n = high.shape[0]
        return both[:72, :n] + both[:72, 128 : 128 + n] + both[72:, :n]

    def store_sums(ref, g, sums):
        at = pl.ds(pl.multiple_of(g * GROUP, GROUP), GROUP)
        for m in range(9):
            ref[m, at, :] = sums[m * GROUP : (m + 1) * GROUP]

    def first(g, carry):
        none = jnp.zeros((GROUP, EDGES), F32)
        rows = [jnp.where(mask, SCALE, 0.0)]
        fine = [none]
        for m in range(8):
            rows.append(jnp.where(mask, harm_t[m, pl.ds(g, 1), :], 0.0))
            fine.append(jnp.where(mask, harm_t[8 + m, pl.ds(g, 1), :], 0.0))
        hmat[g] = jnp.concatenate(rows + fine, axis=0).astype(BF16)
        high, low = split(radial_basis(g)[1])
        basis[g] = jnp.concatenate([high, low, high, none], axis=0).astype(BF16)
        kind = jnp.broadcast_to(spc_d[pl.ds(g, 1), :], (16, EDGES)).astype(jnp.int16)
        kind -= (iota((16, EDGES), 0) >= 8).astype(jnp.int16)
        high, low = (jnp.concatenate([v, v], axis=0).astype(BF16) for v in (high, low))
        none = jnp.zeros((16, EDGES), BF16)
        phi_low = []
        for pair in range(species // 2):
            here = kind == jnp.int16(2 * pair)
            phi[g, 16 * pair : 16 * pair + 16] = jnp.where(here, high, none)
            phi_low.append(jnp.where(here, low, none))
        phi_low = jnp.concatenate(phi_low, axis=0)
        store_sums(kinds_amps, g, sums_of(g, phi[g], phi_low))
        return carry

    lax.fori_loop(0, CHUNKS, first, 0, unroll=16)
    for m in range(9):
        high, low = (v.astype(BF16) for v in split(kinds_amps[m]))
        amps1[m] = mm(high, kind_high) + mm(low, kind_high) + mm(high, kind_low)
    loads[8].wait()

    def update(amps, old, t):
        one = amps[1] * amps[1] + amps[2] * amps[2] + amps[3] * amps[3]
        two = amps[4] * amps[4] + amps[5] * amps[5] + amps[6] * amps[6]
        two += amps[7] * amps[7] + amps[8] * amps[8]
        flat = jnp.concatenate([amps[0], one, two], axis=1).astype(BF16)
        z = mm(flat, uw_ref[t])
        return z, (old + z * jax.nn.sigmoid(z)).astype(BF16)

    def slope(z):
        sig = jax.nn.sigmoid(z)
        return sig * (1.0 + z * (1.0 - sig))

    def back(amps, steep, grad, t):
        grad_z = grad * steep
        grad_inv = nt(grad_z.astype(BF16), uw_ref[t])
        gamps[0] = grad_inv[:, :128]
        for m in range(1, 9):
            part = grad_inv[:, 128:256] if m < 4 else grad_inv[:, 256:]
            gamps[m] = 2.0 * amps[m] * part

    kinds_own = onehot(spc_ref[...], 16).astype(F32).T.astype(BF16)
    h0_own = mm(
        kinds_own, jnp.concatenate([embed, jnp.zeros((16 - species, 128), F32)], axis=0).astype(BF16)
    )
    z1, h1 = update(amps1, h0_own, 0)
    h_sec[1, 0:128] = h1
    h_own[...] = h1

    def h_parts(side):
        dx, dy = side
        if dx == 0:
            return h_own, h_sec.at[1 - dy, pl.ds(0, 128)]
        if dx == 1:
            return h_piece.at[pl.ds(0, 64)], h_sec.at[1 - dy, pl.ds(128, 64)]
        return h_piece.at[pl.ds(64, 64)], h_sec.at[1 - dy, pl.ds(192, 64)]

    copies = exchange(1, h_parts, lambda side: side[0] == 0)
    h_piece[...] = mm(ohxt[...], h1).astype(BF16)
    copies += exchange(1, h_parts, lambda side: side[0] != 0 and side[1] != 0)
    near = exchange(1, h_parts, lambda side: side[1] == 0)
    z1_ref[...] = slope(z1)

    def second_radial(g, carry):
        rad2[:, lanes(g)] = mm(w_t, basis[g])
        return carry

    lax.fori_loop(0, CHUNKS, second_radial, 0, unroll=8)
    own_t = h1.astype(F32).T
    finish(near)

    got_t = h_sec[1, 128:256].astype(F32).T
    near_t = jnp.concatenate([own_t, got_t], axis=1).astype(BF16)

    def first_section(p, carry):
        gat2[:, lanes(p, 2)] = mm(near_t, hot[0:256, lanes(p, 2)]).astype(BF16)
        return carry

    lax.fori_loop(0, PAIRS, first_section, 0, unroll=4)
    finish(copies)
    low_t = mm(ohyt[0], h_sec[0]).T
    high_t = mm(ohyt[1], h_sec[2]).T
    far_t = jnp.concatenate([low_t, high_t], axis=1).astype(BF16)

    def gather(p):
        gat2[:, lanes(p, 2)] += mm(far_t, hot[256:512, lanes(p, 2)]).astype(BF16)

    def second(p, last):
        if not last:
            gather(p + 1)
        for half in range(2):
            g = 2 * p + half
            high, low = (
                v.astype(BF16) for v in split(gat2[:, lanes(g)].astype(F32) * rad2[:, lanes(g)])
            )
            store_sums(amps2, g, sums_of(g, high, low))

    gather(0)
    for p in range(PAIRS):
        second(p, p == PAIRS - 1)
    z2, h2 = update(amps2, h1.astype(F32), 1)
    out_w = ow_ref[...]
    back(amps2, slope(z2), out_w, 1)

    def chunk_rows(ref, g):
        at = pl.ds(pl.multiple_of(g * GROUP, GROUP), GROUP)
        rows = [ref[m, at, :] for m in range(9)]
        return jnp.concatenate(rows + [jnp.zeros_like(rows[0])], axis=0)

    def features(p):
        for g in (2 * p, 2 * p + 1):
            grad = mm(chunk_rows(gamps, g).T.astype(BF16), hmat[g, 0:80])
            gms[:, lanes(g)] = grad.astype(BF16)
            rows_t[:, lanes(g)] = (grad * rad2[:, lanes(g)]).astype(BF16)

    features(0)
    far_rows = jnp.zeros((256, 128), F32)
    for p in range(PAIRS):
        if p + 1 < PAIRS:
            features(p + 1)
        far_rows += nt(hot[256:512, lanes(p, 2)], rows_t[:, lanes(p, 2)])
    far_rows = far_rows.astype(BF16)
    for number in range(2):
        g_sec[2 * number] = mm(ohy[number], far_rows[128 * number : 128 * number + 128]).astype(BF16)

    def g_parts(side):
        dx, dy = side
        if dx == 0:
            return g_sec.at[1 + dy, pl.ds(0, 128)], g_own.at[(1 - dy) // 2]
        if dx == -1:
            return g_sec.at[1 + dy, pl.ds(128, 64)], g_piece.at[1 - dy, pl.ds(0, 64)]
        return g_sec.at[1 + dy, pl.ds(192, 64)], g_piece.at[1 - dy, pl.ds(64, 64)]

    copies = exchange(2, g_parts, lambda side: side[1] != 0)
    near_rows = nt(hot[0:256], rows_t[...])
    g_sec[1, 128:256] = near_rows[128:256].astype(BF16)
    copies += exchange(2, g_parts, lambda side: side[1] == 0)
    gext[...] = near_rows[0:128]

    high, rest = split(out_w)
    mid, low = split(rest)
    readout = jnp.concatenate([high, mid, low, jnp.zeros((5, 128), F32)], axis=0).astype(BF16)
    parts = nt(readout, h2)
    en_ref[...] = parts[0:1] + parts[1:2] + parts[2:3]

    def harmonic_rows(wide):
        which = of_lane[:GROUP]
        result = jnp.zeros((8, EDGES), F32)
        for m in range(8):
            part = wide[(m + 1) * GROUP : (m + 2) * GROUP]
            part = jnp.concatenate(
                [
                    jnp.take_along_axis(part[:, t : t + 128], which[:, t : t + 128], axis=0)
                    for t in range(0, EDGES, 128)
                ],
                axis=1,
            )
            result = jnp.where(iota((8, EDGES), 0) == m, part, result)
        return result

    def distance_row(g, by_basis):
        away, value = radial_basis(g)
        return jnp.sum(by_basis * (-0.25 * away * value), axis=0, keepdims=True)

    def geometry_two(g, carry):
        gathered = gat2[:, lanes(g)].astype(F32)
        message = (gathered * rad2[:, lanes(g)]).astype(BF16)
        gharm[g] = harmonic_rows(mm(chunk_rows(gamps, g).astype(BF16), message))
        two = mm(w_rows, (gms[:, lanes(g)].astype(F32) * gathered).astype(BF16))
        gdist[pl.ds(g, 1), :] = distance_row(g, two[0:NB] + two[NB:])
        return carry

    lax.fori_loop(0, CHUNKS, geometry_two, 0, unroll=8)
    finish(copies)

    grad_h1 = gext[...] + out_w + g_own[0].astype(F32) + g_own[1].astype(F32)
    piece = g_piece[0].astype(F32) + g_piece[1].astype(F32) + g_piece[2].astype(F32)
    grad_h1 += mm(ohx[...], piece.astype(BF16))
    back(amps1, z1_ref[...], grad_h1, 0)

    by_kinds = nt(gamps[...].reshape(9 * ATOMS, WIDTH).astype(BF16), kind_high)
    for m in range(9):
        kinds_amps[m] = by_kinds[m * ATOMS : (m + 1) * ATOMS]

    def geometry_one(g, carry):
        grads = chunk_rows(kinds_amps, g)
        gharm[g] += harmonic_rows(mm(grads.astype(BF16), phi[g]))
        by_kind = mm(grads.T.astype(BF16), hmat[g, 0:80])
        kind = jnp.broadcast_to(spc_d[pl.ds(g, 1), :], (NB, EDGES))
        blocks = [by_kind[k * NB : (k + 1) * NB] for k in range(species)]
        bit = 1
        while len(blocks) > 1:
            odd = (kind & bit) != 0
            blocks = [
                jnp.where(odd, blocks[k + 1], blocks[k]) if k + 1 < len(blocks) else blocks[k]
                for k in range(0, len(blocks), 2)
            ]
            bit *= 2
        by_basis = blocks[0]
        gdist[pl.ds(g, 1), :] += distance_row(g, by_basis)
        return carry

    lax.fori_loop(0, CHUNKS, geometry_one, 0, unroll=16)

    inv, vx, vy, vz = (vec_d[n] for n in range(2, 6))
    g1, g2, g3, g4, g5, g6, g7, g8 = (SCALE * gharm[:, n, :] for n in range(8))
    gx = R3 * g1 + R15 * (vy * g4 + vz * g7 + vx * g8)
    gy = R3 * g2 + R15 * (vx * g4 + vz * g5 - vy * g8)
    gz = R3 * g3 + R15 * (vy * g5 + vx * g7) + 3.0 * R5 * vz * g6
    along = gdist[...] - inv * (gx * vx + gy * vy + gz * vz)
    wide_rows = []
    for grad, unit in ((gx, vx), (gy, vy), (gz, vz)):
        wide_rows += split(grad * inv + unit * along)

    lane_atom = jnp.where(iota((ATOMS, EDGES), 0) % GROUP == of_lane[0:1], 1.0, 0.0).astype(BF16)
    sums = nt(jnp.concatenate(wide_rows, axis=0).astype(BF16), lane_atom)
    here = iota((CHUNKS, 128), 1) // GROUP == iota((CHUNKS, 128), 0)
    own_rows = []
    for number in range(3):
        both = sums[32 * number : 32 * number + 16] + sums[32 * number + 16 : 32 * number + 32]
        own_rows.append(jnp.sum(jnp.where(here, both, 0.0), axis=0, keepdims=True))

    upper = nbr >> 6
    left = []
    for g in range(CHUNKS):
        here = iota((8, EDGES), 0) == upper[g : g + 1]
        left.append(
            jnp.concatenate([jnp.where(here, v[g : g + 1], 0.0) for v in wide_rows], axis=0).astype(BF16)
        )
    both = nt(jnp.concatenate(left, axis=1), low_hot[...])
    coords = []
    for number in range(3):
        value = both[16 * number : 16 * number + 8] + both[16 * number + 8 : 16 * number + 16]
        coords.append(jnp.concatenate([value[k : k + 1] for k in range(8)], axis=1))
    total = jnp.concatenate(coords, axis=0)
    own_rows = jnp.concatenate(own_rows, axis=0)

    def six(value):
        high, low = split(value)
        return jnp.concatenate([high, low, jnp.zeros((2, value.shape[1]), F32)], axis=0).astype(BF16)

    def three(value):
        return value[0:3] + value[3:6]

    pad = jnp.zeros((5, 128), F32)
    for number, start in ((0, 256), (1, 384)):
        spread = three(nt(six(total[:, start : start + 128]), ohy[number]))
        p_out[number] = jnp.concatenate([spread[:, 0:128], pad], axis=0)
        p_piece[2 * number] = jnp.concatenate([spread[:, 128:256], pad], axis=0)
    p_piece[1] = jnp.concatenate([total[:, 128:256], pad], axis=0)

    def p_parts(side):
        dx, dy = side
        if dx == 0:
            return p_out.at[(1 + dy) // 2], p_own.at[(1 - dy) // 2]
        return p_piece.at[1 + dy], p_pin.at[1 - dy, (1 + dx) // 2]

    finish(exchange(3, p_parts))
    up = p_pin[0, 0] + p_pin[1, 0] + p_pin[2, 0]
    down = p_pin[0, 1] + p_pin[1, 1] + p_pin[2, 1]
    piece = jnp.where(iota((8, 128), 1) < 64, up, down)[0:3]
    result = total[:, 0:128] - own_rows + p_own[0][0:3] + p_own[1][0:3]
    result += three(nt(six(piece), ohx[...]))
    fo_ref[...] = -result


def place_outputs(energy_in, forces_in, energy_ref, forces_ref, sems):
    copies = [
        pltpu.make_async_copy(energy_in, energy_ref, sems.at[0]),
        pltpu.make_async_copy(forces_in, forces_ref, sems.at[1]),
    ]
    for copy in copies:
        copy.start()
    for copy in copies:
        copy.wait()


def body(remote, positions, species, neighbours, counts, send_x, send_y, embed, radial_w, update_w, out_w):
    kinds = embed.shape[0] * NB
    whole = (128, CHUNKS * EDGES)
    scratch = [
        pltpu.VMEM((2, 8, 128), F32),
        pltpu.VMEM((8, 128), F32),
        pltpu.VMEM((3, 8, 128), F32),
        pltpu.VMEM((3, 2, 8, 128), F32),
        pltpu.VMEM((3, 256, 128), BF16),
        pltpu.VMEM((128, 128), BF16),
        pltpu.VMEM((128, 128), BF16),
        pltpu.VMEM((3, 256, 128), BF16),
        pltpu.VMEM((2, 128, 128), BF16),
        pltpu.VMEM((3, 128, 128), BF16),
        pltpu.VMEM((2, 8, 128), F32),
        pltpu.VMEM((3, 8, 128), F32),
        pltpu.VMEM((2, 8, 128), F32),
        pltpu.VMEM((3, 2, 8, 128), F32),
        pltpu.VMEM((ATOMS, SLOTS), I32),
        pltpu.VMEM((CHUNKS, EDGES), I32),
        pltpu.VMEM((CHUNKS, EDGES), I32),
        pltpu.VMEM((6, CHUNKS, EDGES), F32),
        pltpu.VMEM((16, CHUNKS, EDGES), F32),
        pltpu.VMEM((EXT, CHUNKS * EDGES), BF16),
        pltpu.VMEM((64, CHUNKS * EDGES), BF16),
        pltpu.VMEM((CHUNKS, 144, EDGES), BF16),
        pltpu.VMEM((CHUNKS, 32, EDGES), BF16),
        pltpu.VMEM((CHUNKS, kinds, EDGES), BF16),
        pltpu.VMEM(whole, F32),
        pltpu.VMEM(whole, BF16),
        pltpu.VMEM(whole, BF16),
        pltpu.VMEM(whole, BF16),
        pltpu.VMEM((9, 128, kinds), F32),
        pltpu.VMEM((9, 128, 128), F32),
        pltpu.VMEM((9, 128, 128), F32),
        pltpu.VMEM((9, 128, 128), F32),
        pltpu.VMEM((128, 128), F32),
        pltpu.VMEM((128, 128), F32),
        pltpu.VMEM((CHUNKS, 8, EDGES), F32),
        pltpu.VMEM((CHUNKS, EDGES), F32),
        pltpu.VMEM((128, 128), BF16),
        pltpu.VMEM((128, 128), BF16),
        pltpu.VMEM((2, 256, 128), BF16),
        pltpu.VMEM((2, 128, 256), BF16),
        pltpu.SemaphoreType.DMA((10,)),
        pltpu.SemaphoreType.DMA((4, 8)),
        pltpu.SemaphoreType.DMA((4, 8)),
    ]
    inputs = (
        positions,
        species.reshape(1, ATOMS),
        neighbours.T,
        counts.reshape(1, ATOMS),
        send_x.reshape(2, 64),
        send_y.reshape(2, 128),
        embed,
        radial_w,
        update_w,
        out_w.reshape(1, WIDTH),
    )
    shapes = (
        jax.ShapeDtypeStruct((1, ATOMS), F32),
        jax.ShapeDtypeStruct((3, ATOMS), F32),
    )
    inputs = tuple(pltpu.with_memory_space_constraint(v, pltpu.HBM) for v in inputs)
    results = pl.pallas_call(
        functools.partial(kernel, remote),
        out_shape=shapes,
        in_specs=[pl.BlockSpec(memory_space=pltpu.HBM)] * len(inputs),
        out_specs=(pl.BlockSpec(memory_space=pltpu.VMEM), pl.BlockSpec(memory_space=pltpu.VMEM)),
        scratch_shapes=[pltpu.VMEM(v.shape, v.dtype) for v in inputs] + scratch,
        compiler_params=pltpu.CompilerParams(
            collective_id=0 if remote else None,
            has_side_effects=remote,
            vmem_limit_bytes=44 * 1024 * 1024,
        ),
    )(*inputs)
    anywhere = pl.BlockSpec(memory_space=pl.ANY)
    vmem = pl.BlockSpec(memory_space=pltpu.VMEM)
    energy, forces = pl.pallas_call(
        place_outputs,
        out_shape=shapes,
        in_specs=[vmem, vmem],
        out_specs=(anywhere, anywhere),
        scratch_shapes=[pltpu.SemaphoreType.DMA((2,))],
        compiler_params=pltpu.CompilerParams(vmem_limit_bytes=1024 * 1024),
    )(*results)
    return energy.reshape(ATOMS), forces


def solution(mesh):
    return jax.shard_map(
        functools.partial(body, True),
        mesh=mesh,
        in_specs=(
            P(None, ("gx", "gy")),
            P(("gx", "gy")),
            P(("gx", "gy"), None),
            P(("gx", "gy")),
            P(("gx", "gy"), None, None),
            P(("gx", "gy"), None, None),
            P(),
            P(),
            P(),
            P(),
        ),
        out_specs=(P(("gx", "gy")), P(None, ("gx", "gy"))),
        check_vma=False,
    )
```
